256 devices in a mesh: rows: 64 (over y, z, core), cols: 4 (over x).
Axes of the slice: x: 4, y: 4, z: 8, core: 2. Of those that a mesh axis runs over, the one named last changes fastest.
Arguments:
- start: float32 [65536, 128], P('rows'), may hold values from -6 to 6
- degrees: int32 [65536], P('rows'), may hold values from 8 to 92
- tiles: bfloat16 [92160, 128, 128], P(('rows', 'cols')), may hold values from -0.0546875 to 0.0546875
- tile_rows: int32 [92160], P(('rows', 'cols')), may hold values from 0 to 511, as said below
- tile_cols: int32 [92160], P(('rows', 'cols')), may hold values from 0 to 511, as said below
- tile_counts: int32 [256], P(('rows', 'cols')), may hold values from 90 to 360
Outputs:
- vectors: float32 [65536, 128], P('rows')
The draws below stay inside these ranges and needn't reach their ends.
Inputs may be any that keep to these rules, and one draw needn't show every extreme that they name: `tile_rows`: each slot's tile row lies in its device's row block: from rows * 8 to rows * 8 + 7. `tile_cols`: A slot's tile column t satisfies (t % 8) // (8 / 4) = the device's cols index.
All inputs are finite; a program needn't handle non-finite values.
Results may differ from the reference program's by a relative error of at most 0.0041.
Values may be sent and summed in bfloat16 or wider, within the bound.
No kernel may reach another device: no remote copies, remote signals or barrier semaphores. Data moves between devices by JAX's collectives and lax.ppermute only.
A program may use at most 64 MiB of HBM per device.

```python
import jax
import jax.numpy as jnp
from jax import lax

VECS = 128
TILE = 128
TPS = 8
TILES_DEV = 360
ITERS = 2
RDEV = 1024
NROWS = 65536
TILES = 92160
N_ROWS = 64
N_COLS = 4
DEVICES = 256


def draw_degrees(key, part):
    key = jax.random.fold_in(key, 11)
    row_ids = jnp.arange(NROWS, dtype=jnp.int32)
    block_ids = row_ids // RDEV
    base = jax.random.randint(key, (NROWS,), 8, 24, dtype=jnp.int32)
    numer = 4 * (N_ROWS - 1) - 3 * block_ids
    result = base * numer // (N_ROWS - 1)
    result = jnp.where(row_ids == 0, 92, result)
    result = jnp.where(row_ids == NROWS - 1, 8, result)
    return result.astype(jnp.int32)


def draw_tile_rows(key, part):
    key = jax.random.fold_in(key, 12)
    slot_ids = jnp.arange(TILES, dtype=jnp.int32)
    device_ids = slot_ids // TILES_DEV
    within = slot_ids % TILES_DEV
    row_block = device_ids // N_COLS
    offset = jax.random.randint(key, (TILES,), 0, TPS, dtype=jnp.int32)
    offset = jnp.where(within == 0, TPS - 1, offset)
    offset = jnp.where(within == 1, 0, offset)
    return (row_block * TPS + offset).astype(jnp.int32)


def draw_tile_cols(key, part):
    key = jax.random.fold_in(key, 13)
    first, second = jax.random.split(key)
    slot_ids = jnp.arange(TILES, dtype=jnp.int32)
    device_ids = slot_ids // TILES_DEV
    within = slot_ids % TILES_DEV
    group = device_ids % N_COLS
    share = TPS // N_COLS
    source = jax.random.randint(first, (TILES,), 0, N_ROWS, dtype=jnp.int32)
    offset = jax.random.randint(second, (TILES,), 0, share, dtype=jnp.int32)
    source = jnp.where(within == 0, N_ROWS - 1, source)
    offset = jnp.where(within == 0, share - 1, offset)
    source = jnp.where(within == 1, 0, source)
    offset = jnp.where(within == 1, 0, offset)
    return (source * TPS + group * share + offset).astype(jnp.int32)


def draw_tile_counts(key, part):
    key = jax.random.fold_in(key, 14)
    first, second, third, fourth = jax.random.split(key, 4)
    base = TILES_DEV // 4 + jax.random.randint(first, (DEVICES,), 0, TILES_DEV // 4 + 1, dtype=jnp.int32)
    heavy = jax.random.randint(second, (DEVICES,), 0, 4, dtype=jnp.int32) == 0
    loaded = TILES_DEV - jax.random.randint(third, (DEVICES,), 0, TILES_DEV // 8 + 1, dtype=jnp.int32)
    result = jnp.where(heavy, loaded, base)
    chosen = jax.random.randint(fourth, (), 0, DEVICES, dtype=jnp.int32)
    device_ids = jnp.arange(DEVICES, dtype=jnp.int32)
    result = jnp.where(device_ids == chosen, TILES_DEV, result)
    result = jnp.where(device_ids == (chosen + DEVICES // 2) % DEVICES, TILES_DEV // 4, result)
    return result.astype(jnp.int32)


def levels(own_key, extent, cuts, least, largest):
    level = 1.0
    for position, shards_of in cuts:
        heights = jax.random.uniform(jax.random.fold_in(jax.random.fold_in(own_key, 6), position), (shards_of,), jnp.float32, least / len(cuts), largest / len(cuts))
        level = level * jnp.repeat(jnp.exp(heights), extent[position] // shards_of).reshape((-1,) + (1,) * (len(extent) - 1 - position))
    return level


def gaussian(key, dims, spread, most, pieces=(), kind=jnp.bfloat16):
    gain = levels(key, dims, pieces, -0.22, 0.18) if pieces else 1.0
    drawn = jax.random.normal(key, dims, jnp.float32) * spread * gain
    return jnp.minimum(jnp.maximum(drawn, -most), most).astype(kind)


def setup_inputs(seed: int = 0) -> dict:
    key_list = jax.random.split(jax.random.key(seed), 7)
    start = gaussian(key_list[0], (NROWS, VECS), 1.0, 6.0, ((0, 64),), jnp.float32)
    degrees = draw_degrees(jax.random.fold_in(key_list[6], 71), 0)
    tiles = gaussian(key_list[2], (TILES, TILE, TILE), (TILE * TILES_DEV * N_COLS // (2 * TPS)) ** -0.5, 0.0546875, ((0, 256),))
    tile_rows = draw_tile_rows(jax.random.fold_in(key_list[6], 71), 0)
    tile_cols = draw_tile_cols(jax.random.fold_in(key_list[6], 71), 0)
    tile_counts = draw_tile_counts(jax.random.fold_in(key_list[6], 71), 0)
    return dict(start=start, degrees=degrees, tiles=tiles, tile_rows=tile_rows, tile_cols=tile_cols, tile_counts=tile_counts)


def orthonormal(image, gram, total_rows):
    factor = jnp.linalg.cholesky(gram / total_rows)
    inverse = lax.linalg.triangular_solve(factor, jnp.eye(factor.shape[0], dtype=jnp.float32), left_side=True, lower=True)
    return jnp.dot(image.astype(jnp.float32), inverse.T.astype(jnp.float32), precision=lax.Precision.HIGHEST, preferred_element_type=jnp.float32)

def reference(start, degrees, tiles, tile_rows, tile_cols, tile_counts):
    scales = lax.rsqrt(degrees.astype(jnp.float32))
    tiles_dev = tiles.reshape(DEVICES, TILES_DEV, TILE, TILE)
    rows_dev = tile_rows.reshape(DEVICES, TILES_DEV)
    cols_dev = tile_cols.reshape(DEVICES, TILES_DEV)
    slot_ids = jnp.arange(TILES_DEV, dtype=jnp.int32)
    current = start
    for rounds in range(ITERS):
        scaled = (current * scales[:, None]).astype(jnp.bfloat16)
        blocks = scaled.reshape(NROWS // TILE, TILE, VECS)

        def gather_tiles(totals, bundle):
            weights, row_ids, col_ids, live_count = bundle
            inputs = blocks[col_ids].astype(jnp.float32)
            terms = jnp.einsum('tij,tjk->tik', weights.astype(jnp.float32), inputs, precision=lax.Precision.HIGHEST)
            terms = jnp.where((slot_ids < live_count)[:, None, None], terms, jnp.float32(0.0))
            return (totals.at[row_ids].add(terms), None)
        totals, unused = lax.scan(gather_tiles, jnp.zeros((NROWS // TILE, TILE, VECS), jnp.float32), (tiles_dev, rows_dev, cols_dev, tile_counts))
        image = totals.reshape(NROWS, VECS) * scales[:, None]
        gram = jnp.dot(image.T.astype(jnp.float32), image.astype(jnp.float32), precision=lax.Precision.HIGHEST, preferred_element_type=jnp.float32)
        current = orthonormal(image, gram, NROWS)
    return current
```

```python
import jax
import jax.numpy as jnp
import numpy as np
from jax import lax
from jax.experimental import pallas as pl
from jax.experimental.pallas import tpu as pltpu
from jax.sharding import PartitionSpec as P

ITERS = 2
NY, NZ, NC = 4, 8, 2
EDGE = 128
STEP = 40
AHEAD = 3
PANEL = 32
HIGHEST = lax.Precision.HIGHEST
F32 = jnp.float32
MIB = 1024 * 1024

VMEM = pl.BlockSpec(memory_space=pltpu.VMEM)
SMEM = pl.BlockSpec(memory_space=pltpu.SMEM)
ANY = pl.BlockSpec(memory_space=pl.ANY)


def row_index(y, z, core):
    return ((y % NY) * NZ + z % NZ) * NC + core


def shift_rows(value, even, odd, flip=0):
    pairs = []
    for y in range(NY):
        for z in range(NZ):
            for core in range(NC):
                dy, dz = (even, odd)[core]
                pairs.append((row_index(y, z, core), row_index(y + dy, z + dz, core ^ flip)))
    return lax.ppermute(value, "rows", pairs)


def shift_cols(value, step):
    size = lax.axis_size("cols")
    return lax.ppermute(value, "cols", [(i, (i + step) % size) for i in range(size)])


class Piece:
    def __init__(self, value, tags):
        self.value, self.tags = value, tags

    def move(self, even, odd, flip=0):
        tags = [None, None]
        for core in range(NC):
            dy, dz = (even, odd)[core]
            tags[core ^ flip] = [((a - dy) % NY, (b - dz) % NZ, k) for a, b, k in self.tags[core]]
        return Piece(shift_rows(self.value, even, odd, flip), tags)

    def first(self, units):
        rows = self.value.shape[0] // len(self.tags[0]) * units
        return Piece(self.value[:rows], [t[:units] for t in self.tags])


def join(*pieces):
    tags = [sum((p.tags[core] for p in pieces), []) for core in range(NC)]
    return Piece(jnp.concatenate([p.value for p in pieces], axis=0), tags)


def gather_rows(part):
    own = Piece(part, [[(0, 0, 0)], [(0, 0, 1)]])
    steps = [own.move(d, d) for d in ((1, 0), (-1, 0), (2, 0))]
    column = join(own, *steps)
    chips = join(column, column.move((0, 0), (0, 0), 1))
    pieces = [chips]
    ring = chips
    for step in range(NZ // 2):
        if step == NZ // 2 - 1:
            ring = ring.first(NY)
        ring = ring.move((0, 1), (0, -1))
        pieces.append(ring)
        pieces.append(ring.move((0, 0), (0, 0), 1))
    return pieces


def places(pieces):
    table = np.full((NC, NY * NZ * NC), -1, np.int32)
    for core in range(NC):
        units = sum((p.tags[core] for p in pieces), [])
        for place, (dy, dz, k) in enumerate(units):
            table[core, (dy * NZ + dz) * NC + k] = place
    assert (table >= 0).all()
    return table


def multiply_tiles(tiles, rows, cols, count, parts, out_parts):
    slots, edge = tiles.shape[0], tiles.shape[1]
    width = parts[0].shape[1]
    row_tiles = out_parts * 2
    depth = AHEAD + 1
    sizes = [p.shape[0] // edge for p in parts]
    offsets = np.cumsum([0] + sizes)
    blocks = int(offsets[-1])

    def kernel(rows_ref, cols_ref, count_ref, tiles_ref, *refs):
        part_refs, refs = refs[: len(parts)], refs[len(parts) :]
        out_refs, refs = refs[:out_parts], refs[out_parts:]
        totals, tile_buffer, block_buffer, tile_sems, part_sems = refs
        copies = [
            pltpu.make_async_copy(
                part_refs[i],
                block_buffer.at[pl.ds(int(offsets[i]) * edge, sizes[i] * edge)],
                part_sems.at[i],
            )
            for i in range(len(parts))
        ]
        for copy in copies:
            copy.start()
        steps = (count_ref[0] + STEP - 1) // STEP

        def tile_copy(step):
            slot = lax.rem(step, depth)
            return pltpu.make_async_copy(
                tiles_ref.at[pl.ds(step * STEP, STEP)], tile_buffer.at[slot], tile_sems.at[slot]
            )

        for step in range(AHEAD):

            @pl.when(step < steps)
            def _():
                tile_copy(step).start()

        totals[...] = jnp.zeros_like(totals)
        block_buffer[pl.ds(blocks * edge, edge)] = jnp.zeros((edge, width), block_buffer.dtype)
        for copy in copies:
            copy.wait()

        def body(step, carry):
            @pl.when(step + AHEAD < steps)
            def _():
                tile_copy(step + AHEAD).start()

            tile_copy(step).wait()
            slot = lax.rem(step, depth)
            terms = []
            for u in range(STEP):
                place = pl.multiple_of(cols_ref[step * STEP + u] * edge, edge)
                terms.append(
                    jnp.dot(
                        tile_buffer[slot, u],
                        block_buffer[pl.ds(place, edge)],
                        preferred_element_type=F32,
                    )
                )
            for u in range(STEP):
                totals[rows_ref[step * STEP + u]] += terms[u]
            return carry

        lax.fori_loop(0, steps, body, 0)
        for i, ref in enumerate(out_refs):
            for half in range(2):
                ref[pl.ds(half * edge, edge)] = totals[2 * i + half]

    return pl.pallas_call(
        kernel,
        name="multiply_tiles",
        out_shape=[jax.ShapeDtypeStruct((2 * edge, width), F32)] * out_parts,
        in_specs=[SMEM, SMEM, SMEM, ANY] + [ANY] * len(parts),
        out_specs=[VMEM] * out_parts,
        scratch_shapes=[
            pltpu.VMEM((row_tiles, edge, width), F32),
            pltpu.VMEM((depth, STEP, edge, edge), tiles.dtype),
            pltpu.VMEM(((blocks + 1) * edge, width), parts[0].dtype),
            pltpu.SemaphoreType.DMA((depth,)),
            pltpu.SemaphoreType.DMA((len(parts),)),
        ],
        compiler_params=pltpu.CompilerParams(vmem_limit_bytes=16 * MIB),
        cost_estimate=pl.CostEstimate(
            flops=2 * slots * edge * edge * width,
            bytes_accessed=slots * edge * edge * 2 + blocks * edge * width * 2,
            transcendentals=0,
        ),
    )(rows, cols, count, tiles, *parts)


def inverse_factor(gram):
    size = gram.shape[0]
    panel = PANEL
    line = lax.broadcasted_iota(jnp.int32, (panel, size), 0)
    lane = lax.broadcasted_iota(jnp.int32, (panel, size), 1)
    identity = jnp.where(line == lane, 1.0, 0.0).astype(F32)
    left = gram
    right = jnp.where(
        lax.broadcasted_iota(jnp.int32, (size, size), 0)
        == lax.broadcasted_iota(jnp.int32, (size, size), 1),
        1.0,
        0.0,
    ).astype(F32)
    done = []
    for start in range(0, size, panel):
        block = jnp.concatenate(
            [left[:panel, start : start + panel], identity[:, : size - panel]], axis=1
        )
        for q in range(0, panel, 2):
            one = jnp.broadcast_to(block[:, q : q + 1], (panel, size))
            two = jnp.broadcast_to(block[:, q + 1 : q + 2], (panel, size))
            cross = two[q : q + 1]
            row_one = block[q : q + 1]
            first = 1.0 / one[q : q + 1]
            ratio = cross * first
            second = 1.0 / (two[q + 1 : q + 2] - cross * ratio)
            factor_one = one * first
            factor_two = (two - factor_one * cross) * second
            row_two = block[q + 1 : q + 2] - ratio * row_one
            block = jnp.where(
                line > q + 1,
                block - factor_one * row_one - factor_two * row_two,
                jnp.where(line == q + 1, row_two, block),
            )
        pivots = jnp.sum(jnp.where(line == lane, block, 0.0), axis=1, keepdims=True)
        small = block[:, panel : 2 * panel] * lax.rsqrt(pivots)
        rows = jnp.dot(
            small,
            jnp.concatenate([left[:panel], right[:panel]], axis=1),
            precision=HIGHEST,
            preferred_element_type=F32,
        )
        done.append(rows[:, size:])
        if start + panel < size:
            update = lax.dot_general(
                rows[:, start + panel : size],
                rows,
                (((0,), (0,)), ((), ())),
                precision=HIGHEST,
                preferred_element_type=F32,
            )
            left = left[panel:] - update[:, :size]
            right = right[panel:] - update[:, size:]
    return jnp.concatenate(done, axis=0)


def apply_inverse(image, inverse):
    return lax.dot_general(
        image, inverse, (((1,), (1,)), ((), ())), precision=HIGHEST, preferred_element_type=F32
    )


def next_scaled(gram, image, spread, total_rows):
    def kernel(gram_ref, image_ref, spread_ref, out_ref):
        inverse = inverse_factor(gram_ref[...] / total_rows)
        current = apply_inverse(image_ref[...], inverse)
        out_ref[...] = (current * spread_ref[...]).astype(out_ref.dtype)

    return pl.pallas_call(
        kernel,
        name="next_scaled",
        out_shape=jax.ShapeDtypeStruct(image.shape, jnp.bfloat16),
        in_specs=[VMEM] * 3,
        out_specs=VMEM,
    )(gram, image, spread)


def last_vectors(gram, images, col_place, total_rows):
    rows, width = images[0].shape
    number = len(images)

    def kernel(place_ref, gram_ref, *refs):
        out_ref = refs[-1]
        inverse = inverse_factor(gram_ref[...] / total_rows)
        for i in range(number):
            target = pl.multiple_of(lax.rem(place_ref[0] + i, number) * rows, rows)
            out_ref[pl.ds(target, rows)] = apply_inverse(refs[i][...], inverse)

    return pl.pallas_call(
        kernel,
        name="last_vectors",
        out_shape=jax.ShapeDtypeStruct((rows * number, width), F32),
        in_specs=[SMEM] + [VMEM] * (1 + number),
        out_specs=VMEM,
    )(col_place.reshape(1), gram, *images)


def sum_gram(gram):
    one, two, three = (shift_cols(gram, d) for d in (1, 2, 3))
    gram = (gram + two) + (one + three)
    gram = gram + shift_rows(gram, (0, 0), (0, 0), 1)
    one, two, three = (shift_rows(gram, (d, 0), (d, 0)) for d in (1, 2, 3))
    gram = (gram + two) + (one + three)
    below = shift_rows(gram, (0, 1), (0, 1))
    above = shift_rows(gram, (0, -1), (0, -1))
    three = (below + above) + gram
    two = gram + above
    upper = shift_rows(three, (0, -3), (0, -3))
    lower = shift_rows(two, (0, 3), (0, 3))
    return three + (upper + lower)


def shards(start, degrees, tiles, tile_rows, tile_cols, tile_counts):
    rows_here, width = start.shape
    edge = tiles.shape[1]
    slots = tiles.shape[0]
    row_tiles = rows_here // edge
    col_parts = lax.axis_size("cols")
    share = row_tiles // col_parts
    quarter = share * edge
    col_place = lax.axis_index("cols").astype(jnp.int32)
    row_place = lax.axis_index("rows").astype(jnp.int32)
    total_rows = rows_here * lax.axis_size("rows")
    core = row_place % NC
    here_z = row_place // NC % NZ
    here_y = row_place // (NC * NZ)

    scales = lax.rsqrt(degrees.astype(F32))
    scales_part = lax.dynamic_slice_in_dim(scales, col_place * quarter, quarter)
    spread = jnp.broadcast_to(scales_part[:, None], (quarter, width))

    out_rows = (tile_rows - row_place * row_tiles - col_place * share) % row_tiles
    source = tile_cols // row_tiles
    away = (
        (source // (NC * NZ) - here_y) % NY * NZ + (source // NC % NZ - here_z) % NZ
    ) * NC + source % NC
    live = jnp.arange(slots, dtype=jnp.int32) < tile_counts[0]

    section = lax.dynamic_slice_in_dim(start, col_place * quarter, quarter)
    scaled = (section * spread).astype(jnp.bfloat16)
    for rounds in range(ITERS):
        pieces = gather_rows(scaled)
        if rounds == 0:
            table = places(pieces)
            units = table.shape[1]
            places_here = jnp.where(core == 0, jnp.asarray(table[0]), jnp.asarray(table[1]))
            hit = away[:, None] == jnp.arange(units, dtype=jnp.int32)[None, :]
            place = jnp.sum(jnp.where(hit, places_here[None, :], 0), axis=1)
            block = jnp.where(live, place * share + tile_cols % share, units * share)
        own, one, two, three = multiply_tiles(
            tiles, out_rows, block.astype(jnp.int32), tile_counts, [p.value for p in pieces], col_parts
        )
        one, two, three = (shift_cols(v, d) for d, v in ((1, one), (2, two), (3, three)))
        image = ((own + two) + (one + three)) * spread
        if rounds == ITERS - 1:
            images = [image] + [shift_cols(image, -d) for d in range(1, col_parts)]
        gram = lax.dot_general(
            image, image, (((0,), (0,)), ((), ())), precision=HIGHEST, preferred_element_type=F32
        )
        gram = sum_gram(gram)
        if rounds < ITERS - 1:
            scaled = next_scaled(gram, image, spread, total_rows)
    return last_vectors(gram, images, col_place, total_rows)


def solution(mesh):
    in_specs = (
        P("rows", None),
        P("rows"),
        P(("rows", "cols"), None, None),
        P(("rows", "cols")),
        P(("rows", "cols")),
        P(("rows", "cols")),
    )
    out_specs = P("rows", None)
    return jax.shard_map(shards, mesh=mesh, in_specs=in_specs, out_specs=out_specs, check_vma=False)
```

```python
import jax
import jax.numpy as jnp
import numpy as np
from jax import lax
from jax.experimental import pallas as pl
from jax.experimental.pallas import tpu as pltpu
from jax.sharding import PartitionSpec as P

ITERS = 2
NY, NZ, NC = 4, 8, 2
EDGE = 128
STEP = 40
PANEL = 64
GROUP = 8
HIGHEST = lax.Precision.HIGHEST
F32 = jnp.float32
MIB = 1024 * 1024

VMEM = pl.BlockSpec(memory_space=pltpu.VMEM)
SMEM = pl.BlockSpec(memory_space=pltpu.SMEM)
ANY = pl.BlockSpec(memory_space=pl.ANY)
HBM = pl.BlockSpec(memory_space=pltpu.HBM)


def row_index(y, z, core):
    return ((y % NY) * NZ + z % NZ) * NC + core


def shift_rows(value, even, odd, flip=0):
    pairs = []
    for y in range(NY):
        for z in range(NZ):
            for core in range(NC):
                dy, dz = (even, odd)[core]
                pairs.append((row_index(y, z, core), row_index(y + dy, z + dz, core ^ flip)))
    return lax.ppermute(value, "rows", pairs)


def shift_cols(value, step):
    size = lax.axis_size("cols")
    return lax.ppermute(value, "cols", [(i, (i + step) % size) for i in range(size)])


class Piece:
    def __init__(self, value, tags):
        self.value, self.tags = value, tags

    def move(self, even, odd, flip=0):
        tags = [None, None]
        for core in range(NC):
            dy, dz = (even, odd)[core]
            tags[core ^ flip] = [((a - dy) % NY, (b - dz) % NZ, k) for a, b, k in self.tags[core]]
        value = None if self.value is None else shift_rows(self.value, even, odd, flip)
        return Piece(value, tags)

    def swap(self):
        return self.move((0, 0), (0, 0), 1)


def join(*pieces):
    tags = [sum((p.tags[core] for p in pieces), []) for core in range(NC)]
    if pieces[0].value is None:
        return Piece(None, tags)
    return Piece(jnp.concatenate([p.value for p in pieces], axis=0), tags)


def gather_rows(part, beside=None):
    own = Piece(part, [[(0, 0, 0)], [(0, 0, 1)]])
    steps = [own.move(d, d) for d in ((1, 0), (-1, 0), (2, 0))]
    column = join(own, *steps)
    rings = [column, column.swap()]
    pieces = list(rings)
    for step in range(NZ // 2 - 1):
        rings = [ring.move((0, 1), (0, -1)) for ring in rings]
        pieces += rings + [ring.swap() for ring in rings]
    if beside is not None:
        rings[0].value, beside = lax.optimization_barrier((rings[0].value, beside))
    last = rings[0].move((0, 1), (0, -1))
    return pieces + [last, last.swap()], beside


def places():
    pieces, _ = gather_rows(None)
    table = np.full((NC, NY * NZ * NC), -1, np.int32)
    for core in range(NC):
        units = sum((p.tags[core] for p in pieces), [])
        for place, (dy, dz, k) in enumerate(units):
            table[core, (dy * NZ + dz) * NC + k] = place
    assert (table >= 0).all()
    return table


def load_tiles(tiles, count):
    def kernel(count_ref, tiles_ref, out_ref, sem):
        steps = (count_ref[0] + STEP - 1) // STEP

        def copy(step):
            place = pl.ds(step * STEP, STEP)
            return pltpu.make_async_copy(tiles_ref.at[place], out_ref.at[place], sem.at[step])

        for step in range(tiles.shape[0] // STEP):

            @pl.when(step < steps)
            def _():
                copy(step).start()

        for step in range(tiles.shape[0] // STEP):

            @pl.when(step < steps)
            def _():
                copy(step).wait()

    return pl.pallas_call(
        kernel,
        name="load_tiles",
        out_shape=jax.ShapeDtypeStruct(tiles.shape, tiles.dtype),
        in_specs=[SMEM, HBM],
        out_specs=VMEM,
        scratch_shapes=[pltpu.SemaphoreType.DMA((tiles.shape[0] // STEP,))],
        compiler_params=pltpu.CompilerParams(vmem_limit_bytes=16 * MIB),
        cost_estimate=pl.CostEstimate(flops=0, bytes_accessed=2 * tiles.size * 2, transcendentals=0),
    )(count, tiles)


def multiply_tiles(tiles, rows, cols, count, parts, out_parts):
    slots, edge = tiles.shape[0], tiles.shape[1]
    width = parts[0].shape[1]
    row_tiles = out_parts * 2
    sizes = [p.shape[0] // edge for p in parts]
    offsets = np.cumsum([0] + sizes)
    blocks = int(offsets[-1])

    def kernel(rows_ref, cols_ref, count_ref, tiles_ref, *refs):
        part_refs, refs = refs[: len(parts)], refs[len(parts) :]
        out_refs, refs = refs[:out_parts], refs[out_parts:]
        totals, block_buffer, part_sems = refs
        copies = [
            pltpu.make_async_copy(
                part_refs[i],
                block_buffer.at[pl.ds(int(offsets[i]) * edge, sizes[i] * edge)],
                part_sems.at[i],
            )
            for i in range(len(parts))
        ]
        for copy in copies:
            copy.start()
        totals[...] = jnp.zeros_like(totals)
        block_buffer[pl.ds(blocks * edge, edge)] = jnp.zeros((edge, width), block_buffer.dtype)
        for copy in copies:
            copy.wait()

        def body(step, carry):
            terms = []
            for u in range(STEP):
                place = pl.multiple_of(cols_ref[step * STEP + u] * edge, edge)
                terms.append(
                    jnp.dot(
                        tiles_ref[step * STEP + u],
                        block_buffer[pl.ds(place, edge)],
                        preferred_element_type=F32,
                    )
                )
            for u in range(STEP):
                totals[rows_ref[step * STEP + u]] += terms[u]
            return carry

        lax.fori_loop(0, (count_ref[0] + STEP - 1) // STEP, body, 0)
        for i, ref in enumerate(out_refs):
            for half in range(2):
                ref[pl.ds(half * edge, edge)] = totals[2 * i + half]

    return pl.pallas_call(
        kernel,
        name="multiply_tiles",
        out_shape=[jax.ShapeDtypeStruct((2 * edge, width), F32)] * out_parts,
        in_specs=[SMEM, SMEM, SMEM, VMEM] + [ANY] * len(parts),
        out_specs=[VMEM] * out_parts,
        scratch_shapes=[
            pltpu.VMEM((row_tiles, edge, width), F32),
            pltpu.VMEM(((blocks + 1) * edge, width), parts[0].dtype),
            pltpu.SemaphoreType.DMA((len(parts),)),
        ],
        compiler_params=pltpu.CompilerParams(vmem_limit_bytes=24 * MIB),
        cost_estimate=pl.CostEstimate(
            flops=2 * slots * edge * edge * width,
            bytes_accessed=slots * edge * edge * 2 + blocks * edge * width * 2,
            transcendentals=0,
        ),
    )(rows, cols, count, tiles, *parts)


def inverse_factor(gram):
    size = gram.shape[0]
    panel = PANEL
    line_all = lax.broadcasted_iota(jnp.int32, (size, size), 0)
    lane_all = lax.broadcasted_iota(jnp.int32, (size, size), 1)
    diagonal = jnp.where(line_all == lane_all, gram, 0.0)
    by_lane = lax.rsqrt(jnp.sum(diagonal, axis=0, keepdims=True))
    by_line = lax.rsqrt(jnp.sum(diagonal, axis=1, keepdims=True))
    left = gram * by_lane * by_line
    right = jnp.where(line_all == lane_all, 1.0, 0.0).astype(F32)
    line = lax.broadcasted_iota(jnp.int32, (panel, size), 0)
    lane = lax.broadcasted_iota(jnp.int32, (panel, size), 1)
    identity = jnp.where(line == lane, 1.0, 0.0).astype(F32)
    done = []
    for start in range(0, size, panel):
        block = jnp.concatenate(
            [left[:panel, start : start + panel], identity[:, : size - panel]], axis=1
        )
        for group in range(0, panel, GROUP):
            spread = [
                jnp.broadcast_to(block[:, group + i : group + i + 1], (panel, size))
                for i in range(GROUP)
            ]
            for p in range(0, GROUP, 2):
                q = group + p
                one, two = spread[p], spread[p + 1]
                a, b, c = one[q : q + 1], two[q : q + 1], two[q + 1 : q + 2]
                scale = 1.0 / (a * c - b * b)
                factor_one = (one * c - two * b) * scale
                factor_two = (two * a - one * b) * scale
                for t in range(p + 2, GROUP):
                    spread[t] = (
                        spread[t]
                        - factor_one * spread[t][q : q + 1]
                        - factor_two * spread[t][q + 1 : q + 2]
                    )
                row_one, row_two = block[q : q + 1], block[q + 1 : q + 2]
                block = jnp.where(
                    line > q + 1,
                    block - factor_one * row_one - factor_two * row_two,
                    jnp.where(line == q + 1, row_two - (b / a) * row_one, block),
                )
        pivots = jnp.sum(jnp.where(line == lane, block, 0.0), axis=1, keepdims=True)
        small = block[:, panel : 2 * panel] * lax.rsqrt(pivots)
        rows = jnp.dot(
            small,
            jnp.concatenate([left[:panel], right[:panel]], axis=1),
            precision=HIGHEST,
            preferred_element_type=F32,
        )
        done.append(rows[:, size:])
        if start + panel < size:
            update = lax.dot_general(
                rows[:, start + panel : size],
                rows,
                (((0,), (0,)), ((), ())),
                precision=HIGHEST,
                preferred_element_type=F32,
            )
            left = left[panel:] - update[:, :size]
            right = right[panel:] - update[:, size:]
    return jnp.concatenate(done, axis=0) * by_lane


def apply_inverse(image, inverse):
    return lax.dot_general(
        image, inverse, (((1,), (1,)), ((), ())), precision=HIGHEST, preferred_element_type=F32
    )


def next_scaled(gram, image, spread, total_rows):
    def kernel(gram_ref, image_ref, spread_ref, out_ref):
        inverse = inverse_factor(gram_ref[...] / total_rows)
        current = apply_inverse(image_ref[...], inverse)
        out_ref[...] = (current * spread_ref[...]).astype(out_ref.dtype)

    return pl.pallas_call(
        kernel,
        name="next_scaled",
        out_shape=jax.ShapeDtypeStruct(image.shape, jnp.bfloat16),
        in_specs=[VMEM] * 3,
        out_specs=VMEM,
    )(gram, image, spread)


def last_vectors(gram, images, col_place, total_rows):
    rows, width = images[0].shape
    number = len(images)

    def kernel(place_ref, gram_ref, *refs):
        out_ref = refs[-1]
        inverse = inverse_factor(gram_ref[...] / total_rows)
        for i in range(number):
            target = pl.multiple_of(lax.rem(place_ref[0] + i, number) * rows, rows)
            out_ref[pl.ds(target, rows)] = apply_inverse(refs[i][...], inverse)

    return pl.pallas_call(
        kernel,
        name="last_vectors",
        out_shape=jax.ShapeDtypeStruct((rows * number, width), F32),
        in_specs=[SMEM] + [VMEM] * (1 + number),
        out_specs=VMEM,
    )(col_place.reshape(1), gram, *images)


def sum_gram(gram, beside=None):
    one, two, three = (shift_cols(gram, d) for d in (1, 2, 3))
    gram = (gram + two) + (one + three)
    gram = gram + shift_rows(gram, (0, 0), (0, 0), 1)
    one, two, three = (shift_rows(gram, (d, 0), (d, 0)) for d in (1, 2, 3))
    gram = (gram + two) + (one + three)
    for sources in (
        (1, 0, 3, 2, 5, 4, 7, 6),
        (2, 3, 0, 1, 6, 7, 4, 5),
        (6, 7, 4, 5, 2, 3, 0, 1),
    ):
        if beside is not None and sources[0] == 6:
            gram, beside = lax.optimization_barrier((gram, beside))
        pairs = [
            (row_index(y, sources[z], core), row_index(y, z, core))
            for y in range(NY)
            for z in range(NZ)
            for core in range(NC)
        ]
        gram = gram + lax.ppermute(gram, "rows", pairs)
    return gram, beside


def shards(start, degrees, tiles, tile_rows, tile_cols, tile_counts):
    rows_here, width = start.shape
    edge = tiles.shape[1]
    slots = tiles.shape[0]
    row_tiles = rows_here // edge
    col_parts = lax.axis_size("cols")
    share = row_tiles // col_parts
    quarter = share * edge
    col_place = lax.axis_index("cols").astype(jnp.int32)
    row_place = lax.axis_index("rows").astype(jnp.int32)
    total_rows = rows_here * lax.axis_size("rows")
    core = row_place % NC
    here_z = row_place // NC % NZ
    here_y = row_place // (NC * NZ)

    scales = lax.rsqrt(degrees.astype(F32))
    scales_part = lax.dynamic_slice_in_dim(scales, col_place * quarter, quarter)
    spread = jnp.broadcast_to(scales_part[:, None], (quarter, width))

    out_rows = (tile_rows - row_place * row_tiles - col_place * share) % row_tiles
    source = tile_cols // row_tiles
    away = (
        (source // (NC * NZ) - here_y) % NY * NZ + (source // NC % NZ - here_z) % NZ
    ) * NC + source % NC
    table = places()
    units = table.shape[1]
    places_here = jnp.where(core == 0, jnp.asarray(table[0]), jnp.asarray(table[1]))
    hit = away[:, None] == jnp.arange(units, dtype=jnp.int32)[None, :]
    place = jnp.sum(jnp.where(hit, places_here[None, :], 0), axis=1)
    live = jnp.arange(slots, dtype=jnp.int32) < tile_counts[0]
    blocks = jnp.where(live, place * share + tile_cols % share, units * share)
    held = (load_tiles(tiles, tile_counts), out_rows, blocks.astype(jnp.int32), spread)

    section = lax.dynamic_slice_in_dim(start, col_place * quarter, quarter)
    scaled = (section * spread).astype(jnp.bfloat16)
    for rounds in range(ITERS):
        if rounds == 0:
            pieces, (held_tiles, out_rows, blocks, spread) = gather_rows(scaled, held)
        else:
            pieces, _ = gather_rows(scaled)
        own, one, two, three = multiply_tiles(
            held_tiles, out_rows, blocks, tile_counts, [p.value for p in pieces], col_parts
        )
        one, two, three = (shift_cols(v, d) for d, v in ((1, one), (2, two), (3, three)))
        image = ((own + two) + (one + three)) * spread
        images = None
        if rounds == ITERS - 1:
            images = [image] + [shift_cols(image, -d) for d in range(1, col_parts)]
        gram = lax.dot_general(
            image, image, (((0,), (0,)), ((), ())), precision=HIGHEST, preferred_element_type=F32
        )
        gram, images = sum_gram(gram, images)
        if rounds < ITERS - 1:
            scaled = next_scaled(gram, image, spread, total_rows)
    return last_vectors(gram, images, col_place, total_rows)


def solution(mesh):
    in_specs = (
        P("rows", None),
        P("rows"),
        P(("rows", "cols"), None, None),
        P(("rows", "cols")),
        P(("rows", "cols")),
        P(("rows", "cols")),
    )
    out_specs = P("rows", None)
    return jax.shard_map(shards, mesh=mesh, in_specs=in_specs, out_specs=out_specs, check_vma=False)
```

```python
import jax
import jax.numpy as jnp
import numpy as np
from jax import lax
from jax.experimental import pallas as pl
from jax.experimental.pallas import tpu as pltpu
from jax.sharding import PartitionSpec as P

ITERS = 2
NY, NZ, NC = 4, 8, 2
EDGE = 128
TILE_ROWS = 8
STEP = 40
CODE = 128
EARLY = 40
PANEL = 64
GROUP = 16
HIGHEST = lax.Precision.HIGHEST
F32 = jnp.float32
MIB = 1024 * 1024

VMEM = pl.BlockSpec(memory_space=pltpu.VMEM)
SMEM = pl.BlockSpec(memory_space=pltpu.SMEM)
ANY = pl.BlockSpec(memory_space=pl.ANY)
HBM = pl.BlockSpec(memory_space=pltpu.HBM)


def row_index(y, z, core):
    return ((y % NY) * NZ + z % NZ) * NC + core


def shift_rows(value, even, odd, flip=0):
    pairs = []
    for y in range(NY):
        for z in range(NZ):
            for core in range(NC):
                dy, dz = (even, odd)[core]
                pairs.append((row_index(y, z, core), row_index(y + dy, z + dz, core ^ flip)))
    return lax.ppermute(value, "rows", pairs)


def shift_cols(value, step):
    size = lax.axis_size("cols")
    return lax.ppermute(value, "cols", [(i, (i + step) % size) for i in range(size)])


class Piece:
    def __init__(self, value, tags):
        self.value, self.tags = value, tags

    def move(self, even, odd, flip=0):
        tags = [None, None]
        for core in range(NC):
            dy, dz = (even, odd)[core]
            tags[core ^ flip] = [((a - dy) % NY, (b - dz) % NZ, k) for a, b, k in self.tags[core]]
        value = None if self.value is None else shift_rows(self.value, even, odd, flip)
        return Piece(value, tags)

    def swap(self):
        return self.move((0, 0), (0, 0), 1)


def join(*pieces):
    tags = [sum((p.tags[core] for p in pieces), []) for core in range(NC)]
    if pieces[0].value is None:
        return Piece(None, tags)
    return Piece(jnp.concatenate([p.value for p in pieces], axis=0), tags)


def gather_rows(part, beside=None):
    own = Piece(part, [[(0, 0, 0)], [(0, 0, 1)]])
    steps = [own.move(d, d) for d in ((1, 0), (-1, 0), (2, 0))]
    column = join(own, *steps)
    rings = [column, column.swap()]
    pieces = list(rings)
    for step in range(NZ // 2 - 1):
        rings = [ring.move((0, 1), (0, -1)) for ring in rings]
        pieces += rings + [ring.swap() for ring in rings]
    if beside is not None:
        rings[0].value, beside = lax.optimization_barrier((rings[0].value, beside))
    last = rings[0].move((0, 1), (0, -1))
    return pieces + [last, last.swap()], beside


def places():
    pieces, _ = gather_rows(None)
    table = np.full((NC, NY * NZ * NC), -1, np.int32)
    for core in range(NC):
        units = sum((p.tags[core] for p in pieces), [])
        for place, (dy, dz, k) in enumerate(units):
            table[core, (dy * NZ + dz) * NC + k] = place
    assert (table >= 0).all()
    return table


def load_tiles(tiles, count):
    def kernel(count_ref, tiles_ref, out_ref, sem):
        steps = (count_ref[0] + STEP - 1) // STEP

        def copy(step):
            place = pl.ds(step * STEP, STEP)
            return pltpu.make_async_copy(tiles_ref.at[place], out_ref.at[place], sem.at[step])

        for step in range(tiles.shape[0] // STEP):

            @pl.when(step < steps)
            def _():
                copy(step).start()

        for step in range(tiles.shape[0] // STEP):

            @pl.when(step < steps)
            def _():
                copy(step).wait()

    return pl.pallas_call(
        kernel,
        name="load_tiles",
        out_shape=jax.ShapeDtypeStruct(tiles.shape, tiles.dtype),
        in_specs=[SMEM, HBM],
        out_specs=VMEM,
        scratch_shapes=[pltpu.SemaphoreType.DMA((tiles.shape[0] // STEP,))],
        compiler_params=pltpu.CompilerParams(vmem_limit_bytes=16 * MIB),
        cost_estimate=pl.CostEstimate(flops=0, bytes_accessed=2 * tiles.size * 2, transcendentals=0),
    )(count, tiles)


def plan_tiles(rows, places, halves, count, early):
    slots = rows.shape[0]
    share = halves[1]
    units = NY * NZ * NC
    index = jnp.arange(slots, dtype=jnp.int32)
    late = (places >= early).astype(jnp.int32)
    lot = jnp.where(index < count, late, 2)
    before = (lot[None, :] == lot[:, None]) & (index[None, :] < index[:, None])
    rank = jnp.sum(before.astype(jnp.int32), axis=1)
    steps_early = (jnp.sum((lot == 0).astype(jnp.int32)) + STEP - 1) // STEP
    steps_late = (jnp.sum((lot == 1).astype(jnp.int32)) + STEP - 1) // STEP
    room = (slots + 2 * STEP - 1) // STEP * STEP
    target = jnp.where(lot == 2, room, rank + late * steps_early * STEP)
    code = (index * TILE_ROWS + rows) * CODE + (places - late * early) * share + halves[0]
    spot = jnp.arange(room, dtype=jnp.int32)
    empty = jnp.where(spot < steps_early * STEP, early * share, (units - early) * share)
    hit = target[None, :] == spot[:, None]
    found = jnp.sum(jnp.where(hit, code[None, :] + 1, 0), axis=1)
    codes = jnp.where(found > 0, found - 1, empty)
    return codes, jnp.stack([jnp.zeros_like(steps_early), steps_early, steps_early + steps_late])


def multiply_tiles(tiles, codes, steps, lot, parts, before=None, out_parts=None):
    slots, edge = tiles.shape[0], tiles.shape[1]
    width = parts[0].shape[1]
    sizes = [p.shape[0] // edge for p in parts]
    offsets = np.cumsum([0] + sizes)
    blocks = int(offsets[-1])
    given = [] if before is None else [before]

    def kernel(codes_ref, steps_ref, tiles_ref, *refs):
        given_refs, refs = refs[: len(given)], refs[len(given) :]
        part_refs, refs = refs[: len(parts)], refs[len(parts) :]
        if out_parts is None:
            totals, block_buffer, part_sems = refs
        else:
            out_refs, (totals, block_buffer, part_sems) = refs[:out_parts], refs[out_parts:]
        copies = [
            pltpu.make_async_copy(
                part_refs[i],
                block_buffer.at[pl.ds(int(offsets[i]) * edge, sizes[i] * edge)],
                part_sems.at[i],
            )
            for i in range(len(parts))
        ]
        for copy in copies:
            copy.start()
        totals[...] = given_refs[0][...] if given else jnp.zeros_like(totals)
        block_buffer[pl.ds(blocks * edge, edge)] = jnp.zeros((edge, width), block_buffer.dtype)
        for copy in copies:
            copy.wait()

        def body(step, carry):
            found = [codes_ref[step * STEP + u] for u in range(STEP)]
            terms = []
            for code in found:
                place = pl.multiple_of(lax.rem(code, CODE) * edge, edge)
                terms.append(
                    jnp.dot(
                        tiles_ref[lax.div(code, CODE * TILE_ROWS)],
                        block_buffer[pl.ds(place, edge)],
                        preferred_element_type=F32,
                    )
                )
            for code, term in zip(found, terms):
                totals[lax.rem(lax.div(code, CODE), TILE_ROWS)] += term
            return carry

        lax.fori_loop(steps_ref[lot], steps_ref[lot + 1], body, 0)
        if out_parts is not None:
            for i, ref in enumerate(out_refs):
                for half in range(2):
                    ref[pl.ds(half * edge, edge)] = totals[2 * i + half]

    whole = (TILE_ROWS, edge, width)
    scratch = [pltpu.VMEM(((blocks + 1) * edge, width), parts[0].dtype), pltpu.SemaphoreType.DMA((len(parts),))]
    if out_parts is None:
        out_shape, out_specs = jax.ShapeDtypeStruct(whole, F32), VMEM
    else:
        out_shape = [jax.ShapeDtypeStruct((2 * edge, width), F32)] * out_parts
        out_specs = [VMEM] * out_parts
        scratch = [pltpu.VMEM(whole, F32)] + scratch
    return pl.pallas_call(
        kernel,
        name="multiply_tiles_early" if out_parts is None else "multiply_tiles_late",
        out_shape=out_shape,
        in_specs=[SMEM, SMEM, VMEM] + [VMEM] * len(given) + [ANY] * len(parts),
        out_specs=out_specs,
        scratch_shapes=scratch,
        compiler_params=pltpu.CompilerParams(vmem_limit_bytes=12 * MIB),
        cost_estimate=pl.CostEstimate(
            flops=2 * slots * edge * edge * width,
            bytes_accessed=slots * edge * edge + blocks * edge * width * 2,
            transcendentals=0,
        ),
    )(codes, steps, tiles, *given, *parts)


def inverse_factor(gram):
    size = gram.shape[0]
    panel = PANEL
    line_all = lax.broadcasted_iota(jnp.int32, (size, size), 0)
    lane_all = lax.broadcasted_iota(jnp.int32, (size, size), 1)
    diagonal = jnp.where(line_all == lane_all, gram, 0.0)
    by_lane = lax.rsqrt(jnp.sum(diagonal, axis=0, keepdims=True))
    by_line = lax.rsqrt(jnp.sum(diagonal, axis=1, keepdims=True))
    left = gram * by_lane * by_line
    right = jnp.where(line_all == lane_all, 1.0, 0.0).astype(F32)
    line = lax.broadcasted_iota(jnp.int32, (panel, size), 0)
    lane = lax.broadcasted_iota(jnp.int32, (panel, size), 1)
    identity = jnp.where(line == lane, 1.0, 0.0).astype(F32)
    done = []
    for start in range(0, size, panel):
        block = jnp.concatenate(
            [left[:panel, start : start + panel], identity[:, : size - panel]], axis=1
        )
        for group in range(0, panel, GROUP):
            spread = [
                jnp.broadcast_to(block[:, group + i : group + i + 1], (panel, size))
                for i in range(GROUP)
            ]
            for p in range(0, GROUP, 2):
                q = group + p
                one, two = spread[p], spread[p + 1]
                a, b, c = one[q : q + 1], two[q : q + 1], two[q + 1 : q + 2]
                scale = 1.0 / (a * c - b * b)
                factor_one = (one * c - two * b) * scale
                factor_two = (two * a - one * b) * scale
                for t in range(p + 2, GROUP):
                    spread[t] = (
                        spread[t]
                        - factor_one * spread[t][q : q + 1]
                        - factor_two * spread[t][q + 1 : q + 2]
                    )
                row_one, row_two = block[q : q + 1], block[q + 1 : q + 2]
                block = jnp.where(
                    line > q + 1,
                    block - factor_one * row_one - factor_two * row_two,
                    jnp.where(line == q + 1, row_two - (b / a) * row_one, block),
                )
        pivots = jnp.sum(jnp.where(line == lane, block, 0.0), axis=1, keepdims=True)
        small = block[:, panel : 2 * panel] * lax.rsqrt(pivots)
        rows = jnp.dot(
            small,
            jnp.concatenate([left[:panel], right[:panel]], axis=1),
            precision=HIGHEST,
            preferred_element_type=F32,
        )
        done.append(rows[:, size:])
        if start + panel < size:
            update = lax.dot_general(
                rows[:, start + panel : size],
                rows,
                (((0,), (0,)), ((), ())),
                precision=HIGHEST,
                preferred_element_type=F32,
            )
            left = left[panel:] - update[:, :size]
            right = right[panel:] - update[:, size:]
    return jnp.concatenate(done, axis=0) * by_lane


def apply_inverse(image, inverse):
    return lax.dot_general(
        image, inverse, (((1,), (1,)), ((), ())), precision=HIGHEST, preferred_element_type=F32
    )


def next_scaled(gram, image, spread, total_rows):
    def kernel(gram_ref, image_ref, spread_ref, out_ref):
        inverse = inverse_factor(gram_ref[...] / total_rows)
        current = apply_inverse(image_ref[...], inverse)
        out_ref[...] = (current * spread_ref[...]).astype(out_ref.dtype)

    return pl.pallas_call(
        kernel,
        name="next_scaled",
        out_shape=jax.ShapeDtypeStruct(image.shape, jnp.bfloat16),
        in_specs=[VMEM] * 3,
        out_specs=VMEM,
        compiler_params=pltpu.CompilerParams(vmem_limit_bytes=8 * MIB),
    )(gram, image, spread)


def last_vectors(gram, images, col_place, total_rows):
    rows, width = images[0].shape
    number = len(images)

    def kernel(place_ref, gram_ref, *refs):
        out_ref = refs[-1]
        inverse = inverse_factor(gram_ref[...] / total_rows)
        for i in range(number):
            target = pl.multiple_of(lax.rem(place_ref[0] + i, number) * rows, rows)
            out_ref[pl.ds(target, rows)] = apply_inverse(refs[i][...], inverse)

    return pl.pallas_call(
        kernel,
        name="last_vectors",
        out_shape=jax.ShapeDtypeStruct((rows * number, width), F32),
        in_specs=[SMEM] + [VMEM] * (1 + number),
        out_specs=VMEM,
        compiler_params=pltpu.CompilerParams(vmem_limit_bytes=8 * MIB),
    )(col_place.reshape(1), gram, *images)


def sum_gram(gram, beside=None):
    one, two, three = (shift_cols(gram, d) for d in (1, 2, 3))
    gram = (gram + two) + (one + three)
    gram = gram + shift_rows(gram, (0, 0), (0, 0), 1)
    one, two, three = (shift_rows(gram, (d, 0), (d, 0)) for d in (1, 2, 3))
    gram = (gram + two) + (one + three)
    for sources in (
        (1, 0, 3, 2, 5, 4, 7, 6),
        (2, 3, 0, 1, 6, 7, 4, 5),
        (6, 7, 4, 5, 2, 3, 0, 1),
    ):
        if beside is not None and sources[0] == 6:
            gram, beside = lax.optimization_barrier((gram, beside))
        pairs = [
            (row_index(y, sources[z], core), row_index(y, z, core))
            for y in range(NY)
            for z in range(NZ)
            for core in range(NC)
        ]
        gram = gram + lax.ppermute(gram, "rows", pairs)
    return gram, beside


def shards(start, degrees, tiles, tile_rows, tile_cols, tile_counts):
    rows_here, width = start.shape
    edge = tiles.shape[1]
    slots = tiles.shape[0]
    row_tiles = rows_here // edge
    col_parts = lax.axis_size("cols")
    share = row_tiles // col_parts
    quarter = share * edge
    col_place = lax.axis_index("cols").astype(jnp.int32)
    row_place = lax.axis_index("rows").astype(jnp.int32)
    total_rows = rows_here * lax.axis_size("rows")
    core = row_place % NC
    here_z = row_place // NC % NZ
    here_y = row_place // (NC * NZ)

    scales = lax.rsqrt(degrees.astype(F32))
    scales_part = lax.dynamic_slice_in_dim(scales, col_place * quarter, quarter)
    spread = jnp.broadcast_to(scales_part[:, None], (quarter, width))

    out_rows = (tile_rows - row_place * row_tiles - col_place * share) % row_tiles
    source = tile_cols // row_tiles
    away = (
        (source // (NC * NZ) - here_y) % NY * NZ + (source // NC % NZ - here_z) % NZ
    ) * NC + source % NC
    table = places()
    units = table.shape[1]
    places_here = jnp.where(core == 0, jnp.asarray(table[0]), jnp.asarray(table[1]))
    hit = away[:, None] == jnp.arange(units, dtype=jnp.int32)[None, :]
    place = jnp.sum(jnp.where(hit, places_here[None, :], 0), axis=1)
    plan = plan_tiles(out_rows, place, (tile_cols % share, share), tile_counts[0], EARLY)
    held = (load_tiles(tiles, tile_counts), plan, spread)

    section = lax.dynamic_slice_in_dim(start, col_place * quarter, quarter)
    scaled = (section * spread).astype(jnp.bfloat16)
    for rounds in range(ITERS):
        if rounds == 0:
            pieces, (held_tiles, (codes, steps), spread) = gather_rows(scaled, held)
        else:
            pieces, _ = gather_rows(scaled)
        sizes = np.cumsum([len(p.tags[0]) for p in pieces])
        early = int(np.searchsorted(sizes, EARLY)) + 1
        values = [p.value for p in pieces]
        totals = multiply_tiles(held_tiles, codes, steps, 0, values[:early])
        own, one, two, three = multiply_tiles(
            held_tiles, codes, steps, 1, values[early:], totals, col_parts
        )
        one, two, three = (shift_cols(v, d) for d, v in ((1, one), (2, two), (3, three)))
        image = ((own + two) + (one + three)) * spread
        images = None
        if rounds == ITERS - 1:
            images = [image] + [shift_cols(image, -d) for d in range(1, col_parts)]
        gram = lax.dot_general(
            image, image, (((0,), (0,)), ((), ())), precision=HIGHEST, preferred_element_type=F32
        )
        gram, images = sum_gram(gram, images)
        if rounds < ITERS - 1:
            scaled = next_scaled(gram, image, spread, total_rows)
    return last_vectors(gram, images, col_place, total_rows)


def solution(mesh):
    in_specs = (
        P("rows", None),
        P("rows"),
        P(("rows", "cols"), None, None),
        P(("rows", "cols")),
        P(("rows", "cols")),
        P(("rows", "cols")),
    )
    out_specs = P("rows", None)
    return jax.shard_map(shards, mesh=mesh, in_specs=in_specs, out_specs=out_specs, check_vma=False)
```

```python
import jax
import jax.numpy as jnp
import numpy as np
from jax import lax
from jax.experimental import pallas as pl
from jax.experimental.pallas import tpu as pltpu
from jax.sharding import PartitionSpec as P

ITERS = 2
NY, NZ, NC = 4, 8, 2
EDGE = 128
TILE_ROWS = 8
STEP = 40
CODE = 128
LOADS = NZ // 2 - 1
PANEL = 64
GROUP = 16
HIGHEST = lax.Precision.HIGHEST
F32 = jnp.float32
MIB = 1024 * 1024

VMEM = pl.BlockSpec(memory_space=pltpu.VMEM)
SMEM = pl.BlockSpec(memory_space=pltpu.SMEM)
ANY = pl.BlockSpec(memory_space=pl.ANY)
HBM = pl.BlockSpec(memory_space=pltpu.HBM)


def row_index(y, z, core):
    return ((y % NY) * NZ + z % NZ) * NC + core


def shift_rows(value, even, odd, flip=0):
    pairs = []
    for y in range(NY):
        for z in range(NZ):
            for core in range(NC):
                dy, dz = (even, odd)[core]
                pairs.append((row_index(y, z, core), row_index(y + dy, z + dz, core ^ flip)))
    return lax.ppermute(value, "rows", pairs)


def shift_cols(value, step):
    size = lax.axis_size("cols")
    return lax.ppermute(value, "cols", [(i, (i + step) % size) for i in range(size)])


class Piece:
    def __init__(self, value, tags):
        self.value, self.tags = value, tags

    def move(self, even, odd, flip=0):
        tags = [None, None]
        for core in range(NC):
            dy, dz = (even, odd)[core]
            tags[core ^ flip] = [((a - dy) % NY, (b - dz) % NZ, k) for a, b, k in self.tags[core]]
        value = None if self.value is None else shift_rows(self.value, even, odd, flip)
        return Piece(value, tags)

    def swap(self):
        return self.move((0, 0), (0, 0), 1)


def join(*pieces):
    tags = [sum((p.tags[core] for p in pieces), []) for core in range(NC)]
    if pieces[0].value is None:
        return Piece(None, tags)
    return Piece(jnp.concatenate([p.value for p in pieces], axis=0), tags)


def column_steps(own):
    return [own] + [own.move(d, d) for d in ((1, 0), (-1, 0), (2, 0))]


def gather_column(column, beside, early):
    rings = [column, column.swap()]
    pieces = list(rings)
    held = None
    for step in range(NZ // 2 - 1):
        if step == NZ // 2 - 2:
            first, pieces = pieces, []
        rings = [ring.move((0, 1), (0, -1)) for ring in rings]
        if beside:
            held = beside[step](held)
            rings[0].value, held = lax.optimization_barrier((rings[0].value, held))
        pieces += rings + [ring.swap() for ring in rings]
    last = rings[0].move((0, 1), (0, -1))
    result = early(first, held)
    if column.value is not None:
        last.value, result = lax.optimization_barrier((last.value, result))
    return result, pieces + [last, last.swap()], held


def places():
    column = join(*column_steps(Piece(None, [[(0, 0, 0)], [(0, 0, 1)]])))
    first, late, _ = gather_column(column, None, lambda pieces, held: pieces)
    table = np.full((NC, NY * NZ * NC), -1, np.int32)
    for core in range(NC):
        units = sum((p.tags[core] for p in first + late), [])
        for place, (dy, dz, k) in enumerate(units):
            table[core, (dy * NZ + dz) * NC + k] = place
    assert (table >= 0).all()
    return table, sum(len(p.tags[0]) for p in first)


def load_tiles(tiles, count, load, held=None):
    given = [] if held is None else [held]
    all_steps = range(tiles.shape[0] // STEP)
    mine = all_steps[load * len(all_steps) // LOADS : (load + 1) * len(all_steps) // LOADS]

    def kernel(count_ref, tiles_ref, *refs):
        out_ref, sem = refs[-2:]
        steps = (count_ref[0] + STEP - 1) // STEP

        def copy(step):
            place = pl.ds(step * STEP, STEP)
            return pltpu.make_async_copy(tiles_ref.at[place], out_ref.at[place], sem.at[step])

        for step in mine:

            @pl.when(step < steps)
            def _():
                copy(step).start()

        for step in mine:

            @pl.when(step < steps)
            def _():
                copy(step).wait()

    return pl.pallas_call(
        kernel,
        name="load_tiles",
        out_shape=jax.ShapeDtypeStruct(tiles.shape, tiles.dtype),
        in_specs=[SMEM, HBM] + [VMEM] * len(given),
        out_specs=VMEM,
        scratch_shapes=[pltpu.SemaphoreType.DMA((len(all_steps),))],
        input_output_aliases={2: 0} if given else {},
        compiler_params=pltpu.CompilerParams(vmem_limit_bytes=40 * MIB),
        cost_estimate=pl.CostEstimate(
            flops=0, bytes_accessed=2 * tiles.size * 2 // LOADS, transcendentals=0
        ),
    )(count, tiles, *given)


def plan_tiles(rows, places, halves, count, early):
    slots = rows.shape[0]
    share = halves[1]
    units = NY * NZ * NC
    index = jnp.arange(slots, dtype=jnp.int32)
    late = (places >= early).astype(jnp.int32)
    lot = jnp.where(index < count, late, 2)
    before = (lot[None, :] == lot[:, None]) & (index[None, :] < index[:, None])
    rank = jnp.sum(before.astype(jnp.int32), axis=1)
    steps_early = (jnp.sum((lot == 0).astype(jnp.int32)) + STEP - 1) // STEP
    steps_late = (jnp.sum((lot == 1).astype(jnp.int32)) + STEP - 1) // STEP
    room = (slots + 2 * STEP - 1) // STEP * STEP
    target = jnp.where(lot == 2, room, rank + late * steps_early * STEP)
    code = (index * TILE_ROWS + rows) * CODE + (places - late * early) * share + halves[0]
    spot = jnp.arange(room, dtype=jnp.int32)
    empty = jnp.where(spot < steps_early * STEP, early * share, (units - early) * share)
    hit = target[None, :] == spot[:, None]
    found = jnp.sum(jnp.where(hit, code[None, :] + 1, 0), axis=1)
    codes = jnp.where(found > 0, found - 1, empty)
    return codes, jnp.stack([jnp.zeros_like(steps_early), steps_early, steps_early + steps_late])


def multiply_tiles(tiles, codes, steps, lot, parts, before=None, out_parts=None):
    slots, edge = tiles.shape[0], tiles.shape[1]
    width = parts[0].shape[1]
    sizes = [p.shape[0] // edge for p in parts]
    offsets = np.cumsum([0] + sizes)
    blocks = int(offsets[-1])
    given = [] if before is None else [before]

    def kernel(codes_ref, steps_ref, tiles_ref, *refs):
        given_refs, refs = refs[: len(given)], refs[len(given) :]
        part_refs, refs = refs[: len(parts)], refs[len(parts) :]
        if out_parts is None:
            totals, block_buffer, part_sems = refs
        else:
            out_refs, (totals, block_buffer, part_sems) = refs[:out_parts], refs[out_parts:]
        copies = [
            pltpu.make_async_copy(
                part_refs[i],
                block_buffer.at[pl.ds(int(offsets[i]) * edge, sizes[i] * edge)],
                part_sems.at[i],
            )
            for i in range(len(parts))
        ]
        for copy in copies:
            copy.start()
        totals[...] = given_refs[0][...] if given else jnp.zeros_like(totals)
        block_buffer[pl.ds(blocks * edge, edge)] = jnp.zeros((edge, width), block_buffer.dtype)
        for copy in copies:
            copy.wait()

        def body(step, carry):
            found = [codes_ref[step * STEP + u] for u in range(STEP)]
            terms = []
            for code in found:
                place = pl.multiple_of(lax.rem(code, CODE) * edge, edge)
                terms.append(
                    jnp.dot(
                        tiles_ref[lax.div(code, CODE * TILE_ROWS)],
                        block_buffer[pl.ds(place, edge)],
                        preferred_element_type=F32,
                    )
                )
            for code, term in zip(found, terms):
                totals[lax.rem(lax.div(code, CODE), TILE_ROWS)] += term
            return carry

        lax.fori_loop(steps_ref[lot], steps_ref[lot + 1], body, 0)
        if out_parts is not None:
            for i, ref in enumerate(out_refs):
                for half in range(2):
                    ref[pl.ds(half * edge, edge)] = totals[2 * i + half]

    whole = (TILE_ROWS, edge, width)
    scratch = [pltpu.VMEM(((blocks + 1) * edge, width), parts[0].dtype), pltpu.SemaphoreType.DMA((len(parts),))]
    if out_parts is None:
        out_shape, out_specs = jax.ShapeDtypeStruct(whole, F32), VMEM
    else:
        out_shape = [jax.ShapeDtypeStruct((2 * edge, width), F32)] * out_parts
        out_specs = [VMEM] * out_parts
        scratch = [pltpu.VMEM(whole, F32)] + scratch
    return pl.pallas_call(
        kernel,
        name="multiply_tiles_early" if out_parts is None else "multiply_tiles_late",
        out_shape=out_shape,
        in_specs=[SMEM, SMEM, VMEM] + [VMEM] * len(given) + [ANY] * len(parts),
        out_specs=out_specs,
        scratch_shapes=scratch,
        compiler_params=pltpu.CompilerParams(vmem_limit_bytes=12 * MIB),
        cost_estimate=pl.CostEstimate(
            flops=2 * slots * edge * edge * width,
            bytes_accessed=slots * edge * edge + blocks * edge * width * 2,
            transcendentals=0,
        ),
    )(codes, steps, tiles, *given, *parts)


def inverse_factor(gram):
    size = gram.shape[0]
    panel = PANEL
    line_all = lax.broadcasted_iota(jnp.int32, (size, size), 0)
    lane_all = lax.broadcasted_iota(jnp.int32, (size, size), 1)
    diagonal = jnp.where(line_all == lane_all, gram, 0.0)
    by_lane = lax.rsqrt(jnp.sum(diagonal, axis=0, keepdims=True))
    by_line = lax.rsqrt(jnp.sum(diagonal, axis=1, keepdims=True))
    left = gram * by_lane * by_line
    right = jnp.where(line_all == lane_all, 1.0, 0.0).astype(F32)
    line = lax.broadcasted_iota(jnp.int32, (panel, size), 0)
    lane = lax.broadcasted_iota(jnp.int32, (panel, size), 1)
    identity = jnp.where(line == lane, 1.0, 0.0).astype(F32)
    done = []
    for start in range(0, size, panel):
        block = jnp.concatenate(
            [left[:panel, start : start + panel], identity[:, : size - panel]], axis=1
        )
        for group in range(0, panel, GROUP):
            spread = [
                jnp.broadcast_to(block[:, group + i : group + i + 1], (panel, size))
                for i in range(GROUP)
            ]
            for p in range(0, GROUP, 2):
                q = group + p
                one, two = spread[p], spread[p + 1]
                a, b, c = one[q : q + 1], two[q : q + 1], two[q + 1 : q + 2]
                scale = 1.0 / (a * c - b * b)
                factor_one = (one * c - two * b) * scale
                factor_two = (two * a - one * b) * scale
                for t in range(p + 2, GROUP):
                    spread[t] = (
                        spread[t]
                        - factor_one * spread[t][q : q + 1]
                        - factor_two * spread[t][q + 1 : q + 2]
                    )
                row_one, row_two = block[q : q + 1], block[q + 1 : q + 2]
                block = jnp.where(
                    line > q + 1,
                    block - factor_one * row_one - factor_two * row_two,
                    jnp.where(line == q + 1, row_two - (b / a) * row_one, block),
                )
        pivots = jnp.sum(jnp.where(line == lane, block, 0.0), axis=1, keepdims=True)
        small = block[:, panel : 2 * panel] * lax.rsqrt(pivots)
        rows = jnp.dot(
            small,
            jnp.concatenate([left[:panel], right[:panel]], axis=1),
            precision=HIGHEST,
            preferred_element_type=F32,
        )
        done.append(rows[:, size:])
        if start + panel < size:
            update = lax.dot_general(
                rows[:, start + panel : size],
                rows,
                (((0,), (0,)), ((), ())),
                precision=HIGHEST,
                preferred_element_type=F32,
            )
            left = left[panel:] - update[:, :size]
            right = right[panel:] - update[:, size:]
    return jnp.concatenate(done, axis=0) * by_lane


def apply_inverse(image, inverse):
    return lax.dot_general(
        image, inverse, (((1,), (1,)), ((), ())), precision=HIGHEST, preferred_element_type=F32
    )


def next_scaled(gram, spreads, total_rows):
    rows, width = spreads[0].shape

    def kernel(gram_ref, *refs):
        out_ref = refs[-1]
        inverse = inverse_factor(gram_ref[...] / total_rows)
        for i, ref in enumerate(refs[:-1]):
            current = apply_inverse(ref[...], inverse)
            out_ref[pl.ds(i * rows, rows)] = current.astype(out_ref.dtype)

    return pl.pallas_call(
        kernel,
        name="next_scaled",
        out_shape=jax.ShapeDtypeStruct((rows * len(spreads), width), jnp.bfloat16),
        in_specs=[VMEM] * (1 + len(spreads)),
        out_specs=VMEM,
        compiler_params=pltpu.CompilerParams(vmem_limit_bytes=8 * MIB),
    )(gram, *spreads)


def last_vectors(gram, images, col_place, total_rows):
    rows, width = images[0].shape
    number = len(images)

    def kernel(place_ref, gram_ref, *refs):
        out_ref = refs[-1]
        inverse = inverse_factor(gram_ref[...] / total_rows)
        for i in range(number):
            target = pl.multiple_of(lax.rem(place_ref[0] + i, number) * rows, rows)
            out_ref[pl.ds(target, rows)] = apply_inverse(refs[i][...], inverse)

    return pl.pallas_call(
        kernel,
        name="last_vectors",
        out_shape=jax.ShapeDtypeStruct((rows * number, width), F32),
        in_specs=[SMEM] + [VMEM] * (1 + number),
        out_specs=VMEM,
        compiler_params=pltpu.CompilerParams(vmem_limit_bytes=8 * MIB),
    )(col_place.reshape(1), gram, *images)


def sum_gram(gram, beside):
    one, two, three = (shift_cols(gram, d) for d in (1, 2, 3))
    gram = (gram + two) + (one + three)
    gram = gram + shift_rows(gram, (0, 0), (0, 0), 1)
    one, two, three = (shift_rows(gram, (d, 0), (d, 0)) for d in (1, 2, 3))
    gram = (gram + two) + (one + three)
    for sources in (
        (1, 0, 3, 2, 5, 4, 7, 6),
        (2, 3, 0, 1, 6, 7, 4, 5),
        (6, 7, 4, 5, 2, 3, 0, 1),
    ):
        if sources[0] == 6:
            gram, beside = lax.optimization_barrier((gram, beside))
        pairs = [
            (row_index(y, sources[z], core), row_index(y, z, core))
            for y in range(NY)
            for z in range(NZ)
            for core in range(NC)
        ]
        gram = gram + lax.ppermute(gram, "rows", pairs)
    return gram, beside


def shards(start, degrees, tiles, tile_rows, tile_cols, tile_counts):
    rows_here, width = start.shape
    edge = tiles.shape[1]
    slots = tiles.shape[0]
    row_tiles = rows_here // edge
    col_parts = lax.axis_size("cols")
    share = row_tiles // col_parts
    quarter = share * edge
    col_place = lax.axis_index("cols").astype(jnp.int32)
    row_place = lax.axis_index("rows").astype(jnp.int32)
    total_rows = rows_here * lax.axis_size("rows")
    core = row_place % NC
    here_z = row_place // NC % NZ
    here_y = row_place // (NC * NZ)

    scales = lax.rsqrt(degrees.astype(F32))
    scales_part = lax.dynamic_slice_in_dim(scales, col_place * quarter, quarter)
    spread = jnp.broadcast_to(scales_part[:, None], (quarter, width))

    out_rows = (tile_rows - row_place * row_tiles - col_place * share) % row_tiles
    source = tile_cols // row_tiles
    away = (
        (source // (NC * NZ) - here_y) % NY * NZ + (source // NC % NZ - here_z) % NZ
    ) * NC + source % NC
    table, early_units = places()
    units = table.shape[1]
    places_here = jnp.where(core == 0, jnp.asarray(table[0]), jnp.asarray(table[1]))
    hit = away[:, None] == jnp.arange(units, dtype=jnp.int32)[None, :]
    place = jnp.sum(jnp.where(hit, places_here[None, :], 0), axis=1)
    plan = plan_tiles(out_rows, place, (tile_cols % share, share), tile_counts[0], early_units)

    def load(number):
        def run(held):
            tiles_held = load_tiles(tiles, tile_counts, number, held if number == 0 else held[0])
            return (tiles_held, plan, spread) if number == LOADS - 1 else (tiles_held,)

        return run

    own_tags = [[(0, 0, 0)], [(0, 0, 1)]]
    section = lax.dynamic_slice_in_dim(start, col_place * quarter, quarter)
    column = join(*column_steps(Piece((section * spread).astype(jnp.bfloat16), own_tags)))
    held = None
    for rounds in range(ITERS):
        known = held

        def early(pieces, fresh):
            tiles_held, (codes, steps), _ = known or fresh
            return multiply_tiles(tiles_held, codes, steps, 0, [p.value for p in pieces])

        beside = [load(i) for i in range(LOADS)] if rounds == 0 else None
        totals, late, fresh = gather_column(column, beside, early)
        held = known or fresh
        tiles_held, (codes, steps), spread = held
        own, one, two, three = multiply_tiles(
            tiles_held, codes, steps, 1, [p.value for p in late], totals, col_parts
        )
        one, two, three = (shift_cols(v, d) for d, v in ((1, one), (2, two), (3, three)))
        image = ((own + two) + (one + three)) * spread
        gram = lax.dot_general(
            image, image, (((0,), (0,)), ((), ())), precision=HIGHEST, preferred_element_type=F32
        )
        if rounds < ITERS - 1:
            steps_y = column_steps(Piece(image * spread, own_tags))
            gram, spreads = sum_gram(gram, [p.value for p in steps_y])
            tags = join(*(Piece(None, p.tags) for p in steps_y)).tags
            column = Piece(next_scaled(gram, spreads, total_rows), tags)
        else:
            images = [image] + [shift_cols(image, -d) for d in range(1, col_parts)]
            gram, images = sum_gram(gram, images)
    return last_vectors(gram, images, col_place, total_rows)


def solution(mesh):
    in_specs = (
        P("rows", None),
        P("rows"),
        P(("rows", "cols"), None, None),
        P(("rows", "cols")),
        P(("rows", "cols")),
        P(("rows", "cols")),
    )
    out_specs = P("rows", None)
    return jax.shard_map(shards, mesh=mesh, in_specs=in_specs, out_specs=out_specs, check_vma=False)
```

```python
import jax
import jax.numpy as jnp
import numpy as np
from jax import lax
from jax.experimental import pallas as pl
from jax.experimental.pallas import tpu as pltpu
from jax.sharding import PartitionSpec as P

ITERS = 2
NY, NZ, NC = 4, 8, 2
EDGE = 128
TILE_ROWS = 8
STEP = 40
CODE = 128
LOAD_STEP = 1
PANEL = 64
GROUP = 16
HIGHEST = lax.Precision.HIGHEST
F32 = jnp.float32
MIB = 1024 * 1024

VMEM = pl.BlockSpec(memory_space=pltpu.VMEM)
SMEM = pl.BlockSpec(memory_space=pltpu.SMEM)
ANY = pl.BlockSpec(memory_space=pl.ANY)
HBM = pl.BlockSpec(memory_space=pltpu.HBM)


def row_index(y, z, core):
    return ((y % NY) * NZ + z % NZ) * NC + core


def shift_rows(value, even, odd, flip=0):
    pairs = []
    for y in range(NY):
        for z in range(NZ):
            for core in range(NC):
                dy, dz = (even, odd)[core]
                pairs.append((row_index(y, z, core), row_index(y + dy, z + dz, core ^ flip)))
    return lax.ppermute(value, "rows", pairs)


def shift_cols(value, step):
    size = lax.axis_size("cols")
    return lax.ppermute(value, "cols", [(i, (i + step) % size) for i in range(size)])


class Piece:
    def __init__(self, value, tags):
        self.value, self.tags = value, tags

    def move(self, even, odd, flip=0):
        tags = [None, None]
        for core in range(NC):
            dy, dz = (even, odd)[core]
            tags[core ^ flip] = [((a - dy) % NY, (b - dz) % NZ, k) for a, b, k in self.tags[core]]
        value = None if self.value is None else shift_rows(self.value, even, odd, flip)
        return Piece(value, tags)

    def swap(self):
        return self.move((0, 0), (0, 0), 1)


def join(*pieces):
    tags = [sum((p.tags[core] for p in pieces), []) for core in range(NC)]
    if pieces[0].value is None:
        return Piece(None, tags)
    return Piece(jnp.concatenate([p.value for p in pieces], axis=0), tags)


def column_steps(own):
    return [own] + [own.move(d, d) for d in ((1, 0), (-1, 0), (2, 0))]


def gather_column(column, beside, early):
    rings = [column, column.swap()]
    pieces = list(rings)
    held = None
    for step in range(NZ // 2 - 1):
        if step == NZ // 2 - 2:
            first, pieces = pieces, []
        rings = [ring.move((0, 1), (0, -1)) for ring in rings]
        if beside and step == LOAD_STEP:
            held = beside()
            rings[0].value, held = lax.optimization_barrier((rings[0].value, held))
        if step < NZ // 2 - 2:
            pieces += rings + [ring.swap() for ring in rings]
    last = rings[0].move((0, 1), (0, -1))
    result = early(first, held)
    if column.value is not None:
        rings[1].value, result = lax.optimization_barrier((rings[1].value, result))
        other = rings[1].swap()
        last.value, other.value = lax.optimization_barrier((last.value, other.value))
    if column.value is None:
        other = rings[1].swap()
    late = [rings[0], rings[1], rings[0].swap(), other, last, last.swap()]
    return result, late, held


def place_of(dy, dz, k, core, where):
    mine = k == core
    line = where(dy == 0, 0, where(dy == NY - 1, 1, dy + 1))
    direct = (dz < NZ // 2) == (core == 1)
    hops = where(dz < NZ // 2, dz, NZ - dz)
    piece = 4 * hops - 2 + where(direct, where(mine, 0, 1), where(mine, 3, 2))
    ends = where(mine, 0, 1)
    piece = where(dz == 0, ends, where(dz == NZ // 2, ends + 2 * NZ - 2, piece))
    return piece * NY + line


def early_units():
    column = join(*column_steps(Piece(None, [[(0, 0, 0)], [(0, 0, 1)]])))
    first, late, _ = gather_column(column, None, lambda pieces, held: pieces)
    for core in range(NC):
        units = np.array(sum((p.tags[core] for p in first + late), []))
        found = place_of(units[:, 0], units[:, 1], units[:, 2], core, np.where)
        assert (found == np.arange(NY * NZ * NC)).all()
    return sum(len(p.tags[0]) for p in first)


def load_tiles(tiles, count):
    all_steps = range(tiles.shape[0] // STEP)

    def kernel(count_ref, tiles_ref, out_ref, sem):
        steps = (count_ref[0] + STEP - 1) // STEP

        def copy(step):
            place = pl.ds(step * STEP, STEP)
            return pltpu.make_async_copy(tiles_ref.at[place], out_ref.at[place], sem.at[step])

        for step in all_steps:

            @pl.when(step < steps)
            def _():
                copy(step).start()

        for step in all_steps:

            @pl.when(step < steps)
            def _():
                copy(step).wait()

    return pl.pallas_call(
        kernel,
        name="load_tiles",
        out_shape=jax.ShapeDtypeStruct(tiles.shape, tiles.dtype),
        in_specs=[SMEM, HBM],
        out_specs=VMEM,
        scratch_shapes=[pltpu.SemaphoreType.DMA((len(all_steps),))],
        compiler_params=pltpu.CompilerParams(vmem_limit_bytes=40 * MIB),
        cost_estimate=pl.CostEstimate(flops=0, bytes_accessed=2 * tiles.size, transcendentals=0),
    )(count, tiles)


def plan_tiles(rows, places, halves, count, early):
    slots = rows.shape[0]
    share = halves[1]
    units = NY * NZ * NC
    index = jnp.arange(slots, dtype=jnp.int32)
    late = (places >= early).astype(jnp.int32)
    lot = jnp.where(index < count, late, 2)
    before = (lot[None, :] == lot[:, None]) & (index[None, :] < index[:, None])
    rank = jnp.sum(before.astype(jnp.int32), axis=1)
    steps_early = (jnp.sum((lot == 0).astype(jnp.int32)) + STEP - 1) // STEP
    steps_late = (jnp.sum((lot == 1).astype(jnp.int32)) + STEP - 1) // STEP
    room = (slots + 2 * STEP - 1) // STEP * STEP
    target = jnp.where(lot == 2, room, rank + late * steps_early * STEP)
    code = (index * TILE_ROWS + rows) * CODE + (places - late * early) * share + halves[0]
    spot = jnp.arange(room, dtype=jnp.int32)
    empty = jnp.where(spot < steps_early * STEP, early * share, (units - early) * share)
    hit = target[None, :] == spot[:, None]
    found = jnp.sum(jnp.where(hit, code[None, :] + 1, 0), axis=1)
    codes = jnp.where(found > 0, found - 1, empty)
    return codes, jnp.stack([jnp.zeros_like(steps_early), steps_early, steps_early + steps_late])


def multiply_tiles(tiles, codes, steps, lot, parts, before=None, out_parts=None):
    slots, edge = tiles.shape[0], tiles.shape[1]
    width = parts[0].shape[1]
    sizes = [p.shape[0] // edge for p in parts]
    offsets = np.cumsum([0] + sizes)
    blocks = int(offsets[-1])
    given = [] if before is None else [before]

    def kernel(codes_ref, steps_ref, tiles_ref, *refs):
        given_refs, refs = refs[: len(given)], refs[len(given) :]
        part_refs, refs = refs[: len(parts)], refs[len(parts) :]
        if out_parts is None:
            totals, block_buffer, part_sems = refs
        else:
            out_refs, (totals, block_buffer, part_sems) = refs[:out_parts], refs[out_parts:]
        copies = [
            pltpu.make_async_copy(
                part_refs[i],
                block_buffer.at[pl.ds(int(offsets[i]) * edge, sizes[i] * edge)],
                part_sems.at[i],
            )
            for i in range(len(parts))
        ]
        for copy in copies:
            copy.start()
        totals[...] = given_refs[0][...] if given else jnp.zeros_like(totals)
        block_buffer[pl.ds(blocks * edge, edge)] = jnp.zeros((edge, width), block_buffer.dtype)
        for copy in copies:
            copy.wait()

        def body(step, carry):
            found = [codes_ref[step * STEP + u] for u in range(STEP)]
            terms = []
            for code in found:
                place = pl.multiple_of(lax.rem(code, CODE) * edge, edge)
                terms.append(
                    jnp.dot(
                        tiles_ref[lax.div(code, CODE * TILE_ROWS)],
                        block_buffer[pl.ds(place, edge)],
                        preferred_element_type=F32,
                    )
                )
            for code, term in zip(found, terms):
                totals[lax.rem(lax.div(code, CODE), TILE_ROWS)] += term
            return carry

        lax.fori_loop(steps_ref[lot], steps_ref[lot + 1], body, 0)
        if out_parts is not None:
            for i, ref in enumerate(out_refs):
                for half in range(2):
                    ref[pl.ds(half * edge, edge)] = totals[2 * i + half]

    whole = (TILE_ROWS, edge, width)
    scratch = [pltpu.VMEM(((blocks + 1) * edge, width), parts[0].dtype), pltpu.SemaphoreType.DMA((len(parts),))]
    if out_parts is None:
        out_shape, out_specs = jax.ShapeDtypeStruct(whole, F32), VMEM
    else:
        out_shape = [jax.ShapeDtypeStruct((2 * edge, width), F32)] * out_parts
        out_specs = [VMEM] * out_parts
        scratch = [pltpu.VMEM(whole, F32)] + scratch
    return pl.pallas_call(
        kernel,
        name="multiply_tiles_early" if out_parts is None else "multiply_tiles_late",
        out_shape=out_shape,
        in_specs=[SMEM, SMEM, VMEM] + [VMEM] * len(given) + [ANY] * len(parts),
        out_specs=out_specs,
        scratch_shapes=scratch,
        compiler_params=pltpu.CompilerParams(vmem_limit_bytes=12 * MIB),
        cost_estimate=pl.CostEstimate(
            flops=2 * slots * edge * edge * width,
            bytes_accessed=slots * edge * edge + blocks * edge * width * 2,
            transcendentals=0,
        ),
    )(codes, steps, tiles, *given, *parts)


def inverse_factor(gram):
    size = gram.shape[0]
    panel = PANEL
    line_all = lax.broadcasted_iota(jnp.int32, (size, size), 0)
    lane_all = lax.broadcasted_iota(jnp.int32, (size, size), 1)
    diagonal = jnp.where(line_all == lane_all, gram, 0.0)
    by_lane = lax.rsqrt(jnp.sum(diagonal, axis=0, keepdims=True))
    by_line = lax.rsqrt(jnp.sum(diagonal, axis=1, keepdims=True))
    left = gram * by_lane * by_line
    right = jnp.where(line_all == lane_all, 1.0, 0.0).astype(F32)
    line = lax.broadcasted_iota(jnp.int32, (panel, size), 0)
    lane = lax.broadcasted_iota(jnp.int32, (panel, size), 1)
    identity = jnp.where(line == lane, 1.0, 0.0).astype(F32)
    done = []
    for start in range(0, size, panel):
        block = jnp.concatenate(
            [left[:panel, start : start + panel], identity[:, : size - panel]], axis=1
        )
        for group in range(0, panel, GROUP):
            spread = [
                jnp.broadcast_to(block[:, group + i : group + i + 1], (panel, size))
                for i in range(GROUP)
            ]
            for p in range(0, GROUP, 2):
                q = group + p
                one, two = spread[p], spread[p + 1]
                a, b, c = one[q : q + 1], two[q : q + 1], two[q + 1 : q + 2]
                scale = 1.0 / (a * c - b * b)
                factor_one = (one * c - two * b) * scale
                factor_two = (two * a - one * b) * scale
                for t in range(p + 2, GROUP):
                    spread[t] = (
                        spread[t]
                        - factor_one * spread[t][q : q + 1]
                        - factor_two * spread[t][q + 1 : q + 2]
                    )
                row_one, row_two = block[q : q + 1], block[q + 1 : q + 2]
                block = jnp.where(
                    line > q + 1,
                    block - factor_one * row_one - factor_two * row_two,
                    jnp.where(line == q + 1, row_two - (b / a) * row_one, block),
                )
        pivots = jnp.sum(jnp.where(line == lane, block, 0.0), axis=1, keepdims=True)
        small = block[:, panel : 2 * panel] * lax.rsqrt(pivots)
        rows = jnp.dot(
            small,
            jnp.concatenate([left[:panel], right[:panel]], axis=1),
            precision=HIGHEST,
            preferred_element_type=F32,
        )
        done.append(rows[:, size:])
        if start + panel < size:
            update = lax.dot_general(
                rows[:, start + panel : size],
                rows,
                (((0,), (0,)), ((), ())),
                precision=HIGHEST,
                preferred_element_type=F32,
            )
            left = left[panel:] - update[:, :size]
            right = right[panel:] - update[:, size:]
    return jnp.concatenate(done, axis=0) * by_lane


def apply_inverse(image, inverse):
    return lax.dot_general(
        image, inverse, (((1,), (1,)), ((), ())), precision=HIGHEST, preferred_element_type=F32
    )


def next_scaled(gram, spreads, total_rows):
    rows, width = spreads[0].shape

    def kernel(gram_ref, *refs):
        out_ref = refs[-1]
        inverse = inverse_factor(gram_ref[...] / total_rows)
        for i, ref in enumerate(refs[:-1]):
            current = apply_inverse(ref[...], inverse)
            out_ref[pl.ds(i * rows, rows)] = current.astype(out_ref.dtype)

    return pl.pallas_call(
        kernel,
        name="next_scaled",
        out_shape=jax.ShapeDtypeStruct((rows * len(spreads), width), jnp.bfloat16),
        in_specs=[VMEM] * (1 + len(spreads)),
        out_specs=VMEM,
        compiler_params=pltpu.CompilerParams(vmem_limit_bytes=8 * MIB),
    )(gram, *spreads)


def last_vectors(gram, images, col_place, total_rows):
    rows, width = images[0].shape
    number = len(images)

    def kernel(place_ref, gram_ref, *refs):
        out_ref = refs[-1]
        inverse = inverse_factor(gram_ref[...] / total_rows)
        for i in range(number):
            target = pl.multiple_of(lax.rem(place_ref[0] + i, number) * rows, rows)
            out_ref[pl.ds(target, rows)] = apply_inverse(refs[i][...], inverse)

    return pl.pallas_call(
        kernel,
        name="last_vectors",
        out_shape=jax.ShapeDtypeStruct((rows * number, width), F32),
        in_specs=[SMEM] + [VMEM] * (1 + number),
        out_specs=VMEM,
        compiler_params=pltpu.CompilerParams(vmem_limit_bytes=8 * MIB),
    )(col_place.reshape(1), gram, *images)


def sum_gram(gram, beside):
    one, two, three = (shift_cols(gram, d) for d in (1, 2, 3))
    gram = (gram + two) + (one + three)
    gram = gram + shift_rows(gram, (0, 0), (0, 0), 1)
    one, two, three = (shift_rows(gram, (d, 0), (d, 0)) for d in (1, 2, 3))
    gram = (gram + two) + (one + three)
    for sources in (
        (1, 0, 3, 2, 5, 4, 7, 6),
        (2, 3, 0, 1, 6, 7, 4, 5),
        (6, 7, 4, 5, 2, 3, 0, 1),
    ):
        if sources[0] == 6:
            gram, beside = lax.optimization_barrier((gram, beside))
        pairs = [
            (row_index(y, sources[z], core), row_index(y, z, core))
            for y in range(NY)
            for z in range(NZ)
            for core in range(NC)
        ]
        gram = gram + lax.ppermute(gram, "rows", pairs)
    return gram, beside


def shards(start, degrees, tiles, tile_rows, tile_cols, tile_counts):
    rows_here, width = start.shape
    edge = tiles.shape[1]
    slots = tiles.shape[0]
    row_tiles = rows_here // edge
    col_parts = lax.axis_size("cols")
    share = row_tiles // col_parts
    quarter = share * edge
    col_place = lax.axis_index("cols").astype(jnp.int32)
    row_place = lax.axis_index("rows").astype(jnp.int32)
    total_rows = rows_here * lax.axis_size("rows")
    core = row_place % NC
    here_z = row_place // NC % NZ
    here_y = row_place // (NC * NZ)

    degrees_part = lax.dynamic_slice_in_dim(degrees, col_place * quarter, quarter)
    spread = jnp.broadcast_to(lax.rsqrt(degrees_part.astype(F32))[:, None], (quarter, width))

    out_rows = (tile_rows - row_place * row_tiles - col_place * share) % row_tiles
    source = tile_cols // row_tiles
    place = place_of(
        (source // (NC * NZ) - here_y) % NY,
        (source // NC % NZ - here_z) % NZ,
        source % NC,
        core,
        jnp.where,
    )
    plan = plan_tiles(out_rows, place, (tile_cols % share, share), tile_counts[0], early_units())

    def load():
        return load_tiles(tiles, tile_counts), plan, spread

    own_tags = [[(0, 0, 0)], [(0, 0, 1)]]
    section = lax.dynamic_slice_in_dim(start, col_place * quarter, quarter)
    column = join(*column_steps(Piece((section * spread).astype(jnp.bfloat16), own_tags)))
    held = None
    for rounds in range(ITERS):
        known = held

        def early(pieces, fresh):
            tiles_held, (codes, steps), _ = known or fresh
            return multiply_tiles(tiles_held, codes, steps, 0, [p.value for p in pieces])

        beside = load if rounds == 0 else None
        totals, late, fresh = gather_column(column, beside, early)
        held = known or fresh
        tiles_held, (codes, steps), spread = held
        own, one, two, three = multiply_tiles(
            tiles_held, codes, steps, 1, [p.value for p in late], totals, col_parts
        )
        one, two, three = (shift_cols(v, d) for d, v in ((1, one), (2, two), (3, three)))
        image = ((own + two) + (one + three)) * spread
        gram = lax.dot_general(
            image, image, (((0,), (0,)), ((), ())), precision=HIGHEST, preferred_element_type=F32
        )
        if rounds < ITERS - 1:
            steps_y = column_steps(Piece(image * spread, own_tags))
            gram, spreads = sum_gram(gram, [p.value for p in steps_y])
            tags = join(*(Piece(None, p.tags) for p in steps_y)).tags
            column = Piece(next_scaled(gram, spreads, total_rows), tags)
        else:
            images = [image] + [shift_cols(image, -d) for d in range(1, col_parts)]
            gram, images = sum_gram(gram, images)
    return last_vectors(gram, images, col_place, total_rows)


def solution(mesh):
    in_specs = (
        P("rows", None),
        P("rows"),
        P(("rows", "cols"), None, None),
        P(("rows", "cols")),
        P(("rows", "cols")),
        P(("rows", "cols")),
    )
    out_specs = P("rows", None)
    return jax.shard_map(shards, mesh=mesh, in_specs=in_specs, out_specs=out_specs, check_vma=False)
```

```python
import jax
import jax.numpy as jnp
import numpy as np
from jax import lax
from jax.experimental import pallas as pl
from jax.experimental.pallas import tpu as pltpu
from jax.sharding import PartitionSpec as P

ITERS = 2
NY, NZ, NC = 4, 8, 2
EDGE = 128
TILE_ROWS = 8
STEP = 40
CODE = 128
PLAN_STEP = 1
PANEL = 64
GROUP = 16
HIGHEST = lax.Precision.HIGHEST
F32 = jnp.float32
MIB = 1024 * 1024

VMEM = pl.BlockSpec(memory_space=pltpu.VMEM)
SMEM = pl.BlockSpec(memory_space=pltpu.SMEM)
ANY = pl.BlockSpec(memory_space=pl.ANY)
HBM = pl.BlockSpec(memory_space=pltpu.HBM)


def row_index(y, z, core):
    return ((y % NY) * NZ + z % NZ) * NC + core


def shift_rows(value, even, odd, flip=0):
    pairs = []
    for y in range(NY):
        for z in range(NZ):
            for core in range(NC):
                dy, dz = (even, odd)[core]
                pairs.append((row_index(y, z, core), row_index(y + dy, z + dz, core ^ flip)))
    return lax.ppermute(value, "rows", pairs)


def shift_cols(value, step):
    size = lax.axis_size("cols")
    return lax.ppermute(value, "cols", [(i, (i + step) % size) for i in range(size)])


def shift_cols_apart(value):
    size = lax.axis_size("cols")
    pairs = [
        (row * size + i, row * size + (i + (1, -1)[row % NC]) % size)
        for row in range(NY * NZ * NC)
        for i in range(size)
    ]
    return lax.ppermute(value, ("rows", "cols"), pairs)


class Piece:
    def __init__(self, value, tags):
        self.value, self.tags = value, tags

    def move(self, even, odd, flip=0):
        tags = [None, None]
        for core in range(NC):
            dy, dz = (even, odd)[core]
            tags[core ^ flip] = [((a - dy) % NY, (b - dz) % NZ, k) for a, b, k in self.tags[core]]
        value = None if self.value is None else shift_rows(self.value, even, odd, flip)
        return Piece(value, tags)

    def swap(self):
        return self.move((0, 0), (0, 0), 1)


def join(*pieces):
    tags = [sum((p.tags[core] for p in pieces), []) for core in range(NC)]
    if pieces[0].value is None:
        return Piece(None, tags)
    return Piece(jnp.concatenate([p.value for p in pieces], axis=0), tags)


def column_steps(own):
    return [own] + [own.move(d, d) for d in ((1, 0), (-1, 0), (2, 0))]


def gather_column(column, beside, early):
    rings = [column, column.swap()]
    pieces = list(rings)
    held = None
    for step in range(NZ // 2 - 1):
        if step == NZ // 2 - 2:
            first, pieces = pieces, []
        rings = [ring.move((0, 1), (0, -1)) for ring in rings]
        if beside and step == PLAN_STEP:
            rings[0].value, held = lax.optimization_barrier((rings[0].value, beside))
        if step < NZ // 2 - 2:
            pieces += rings + [ring.swap() for ring in rings]
    last = rings[0].move((0, 1), (0, -1))
    result = early(first, held)
    if column.value is not None:
        rings[1].value, result = lax.optimization_barrier((rings[1].value, result))
        other = rings[1].swap()
        last.value, other.value = lax.optimization_barrier((last.value, other.value))
    if column.value is None:
        other = rings[1].swap()
    late = [rings[0], rings[1], rings[0].swap(), other, last, last.swap()]
    return result, late, held


def place_of(dy, dz, k, core, where):
    mine = k == core
    line = where(dy == 0, 0, where(dy == NY - 1, 1, dy + 1))
    direct = (dz < NZ // 2) == (core == 1)
    hops = where(dz < NZ // 2, dz, NZ - dz)
    piece = 4 * hops - 2 + where(direct, where(mine, 0, 1), where(mine, 3, 2))
    ends = where(mine, 0, 1)
    piece = where(dz == 0, ends, where(dz == NZ // 2, ends + 2 * NZ - 2, piece))
    return piece * NY + line


def early_units():
    column = join(*column_steps(Piece(None, [[(0, 0, 0)], [(0, 0, 1)]])))
    first, late, _ = gather_column(column, None, lambda pieces, held: pieces)
    for core in range(NC):
        units = np.array(sum((p.tags[core] for p in first + late), []))
        found = place_of(units[:, 0], units[:, 1], units[:, 2], core, np.where)
        assert (found == np.arange(NY * NZ * NC)).all()
    return sum(len(p.tags[0]) for p in first)


def load_tiles(tiles, count):
    all_steps = range(tiles.shape[0] // STEP)

    def kernel(count_ref, tiles_ref, out_ref, sem):
        steps = (count_ref[0] + STEP - 1) // STEP

        def copy(step):
            place = pl.ds(step * STEP, STEP)
            return pltpu.make_async_copy(tiles_ref.at[place], out_ref.at[place], sem.at[step])

        for step in all_steps:

            @pl.when(step < steps)
            def _():
                copy(step).start()

        for step in all_steps:

            @pl.when(step < steps)
            def _():
                copy(step).wait()

    return pl.pallas_call(
        kernel,
        name="load_tiles",
        out_shape=jax.ShapeDtypeStruct(tiles.shape, tiles.dtype),
        in_specs=[SMEM, HBM],
        out_specs=VMEM,
        scratch_shapes=[pltpu.SemaphoreType.DMA((len(all_steps),))],
        compiler_params=pltpu.CompilerParams(vmem_limit_bytes=40 * MIB),
        cost_estimate=pl.CostEstimate(flops=0, bytes_accessed=2 * tiles.size, transcendentals=0),
    )(count, tiles)


def plan_tiles(rows, places, halves, count, early):
    slots = rows.shape[0]
    share = halves[1]
    units = NY * NZ * NC
    index = jnp.arange(slots, dtype=jnp.int32)
    late = (places >= early).astype(jnp.int32)
    lot = jnp.where(index < count, late, 2)
    before = (lot[None, :] == lot[:, None]) & (index[None, :] < index[:, None])
    rank = jnp.sum(before.astype(jnp.int32), axis=1)
    steps_early = (jnp.sum((lot == 0).astype(jnp.int32)) + STEP - 1) // STEP
    steps_late = (jnp.sum((lot == 1).astype(jnp.int32)) + STEP - 1) // STEP
    room = (slots + 2 * STEP - 1) // STEP * STEP
    target = jnp.where(lot == 2, room, rank + late * steps_early * STEP)
    code = (index * TILE_ROWS + rows) * CODE + (places - late * early) * share + halves[0]
    spot = jnp.arange(room, dtype=jnp.int32)
    empty = jnp.where(spot < steps_early * STEP, early * share, (units - early) * share)
    hit = target[None, :] == spot[:, None]
    found = jnp.sum(jnp.where(hit, code[None, :] + 1, 0), axis=1)
    codes = jnp.where(found > 0, found - 1, empty)
    return codes, jnp.stack([jnp.zeros_like(steps_early), steps_early, steps_early + steps_late])


def multiply_tiles(tiles, codes, steps, lot, parts, before=None, out_parts=None):
    slots, edge = tiles.shape[0], tiles.shape[1]
    width = parts[0].shape[1]
    sizes = [p.shape[0] // edge for p in parts]
    offsets = np.cumsum([0] + sizes)
    blocks = int(offsets[-1])
    given = [] if before is None else [before]

    def kernel(codes_ref, steps_ref, tiles_ref, *refs):
        given_refs, refs = refs[: len(given)], refs[len(given) :]
        part_refs, refs = refs[: len(parts)], refs[len(parts) :]
        if out_parts is None:
            totals, block_buffer, part_sems = refs
        else:
            out_refs, (totals, block_buffer, part_sems) = refs[:out_parts], refs[out_parts:]
        copies = [
            pltpu.make_async_copy(
                part_refs[i],
                block_buffer.at[pl.ds(int(offsets[i]) * edge, sizes[i] * edge)],
                part_sems.at[i],
            )
            for i in range(len(parts))
        ]
        for copy in copies:
            copy.start()
        totals[...] = given_refs[0][...] if given else jnp.zeros_like(totals)
        block_buffer[pl.ds(blocks * edge, edge)] = jnp.zeros((edge, width), block_buffer.dtype)
        for copy in copies:
            copy.wait()

        def body(step, carry):
            found = [codes_ref[step * STEP + u] for u in range(STEP)]
            terms = []
            for code in found:
                place = pl.multiple_of(lax.rem(code, CODE) * edge, edge)
                terms.append(
                    jnp.dot(
                        tiles_ref[lax.div(code, CODE * TILE_ROWS)],
                        block_buffer[pl.ds(place, edge)],
                        preferred_element_type=F32,
                    )
                )
            for code, term in zip(found, terms):
                totals[lax.rem(lax.div(code, CODE), TILE_ROWS)] += term
            return carry

        lax.fori_loop(steps_ref[lot], steps_ref[lot + 1], body, 0)
        if out_parts is not None:
            for i, ref in enumerate(out_refs):
                for half in range(2):
                    ref[pl.ds(half * edge, edge)] = totals[2 * i + half]

    whole = (TILE_ROWS, edge, width)
    scratch = [pltpu.VMEM(((blocks + 1) * edge, width), parts[0].dtype), pltpu.SemaphoreType.DMA((len(parts),))]
    if out_parts is None:
        out_shape, out_specs = jax.ShapeDtypeStruct(whole, F32), VMEM
    else:
        out_shape = [jax.ShapeDtypeStruct((2 * edge, width), F32)] * out_parts
        out_specs = [VMEM] * out_parts
        scratch = [pltpu.VMEM(whole, F32)] + scratch
    return pl.pallas_call(
        kernel,
        name="multiply_tiles_early" if out_parts is None else "multiply_tiles_late",
        out_shape=out_shape,
        in_specs=[SMEM, SMEM, VMEM] + [VMEM] * len(given) + [ANY] * len(parts),
        out_specs=out_specs,
        scratch_shapes=scratch,
        compiler_params=pltpu.CompilerParams(vmem_limit_bytes=12 * MIB),
        cost_estimate=pl.CostEstimate(
            flops=2 * slots * edge * edge * width,
            bytes_accessed=slots * edge * edge + blocks * edge * width * 2,
            transcendentals=0,
        ),
    )(codes, steps, tiles, *given, *parts)


def inverse_factor(gram):
    size = gram.shape[0]
    panel = PANEL
    line_all = lax.broadcasted_iota(jnp.int32, (size, size), 0)
    lane_all = lax.broadcasted_iota(jnp.int32, (size, size), 1)
    diagonal = jnp.where(line_all == lane_all, gram, 0.0)
    by_lane = lax.rsqrt(jnp.sum(diagonal, axis=0, keepdims=True))
    by_line = lax.rsqrt(jnp.sum(diagonal, axis=1, keepdims=True))
    left = gram * by_lane * by_line
    right = jnp.where(line_all == lane_all, 1.0, 0.0).astype(F32)
    line = lax.broadcasted_iota(jnp.int32, (panel, size), 0)
    lane = lax.broadcasted_iota(jnp.int32, (panel, size), 1)
    identity = jnp.where(line == lane, 1.0, 0.0).astype(F32)
    done = []
    for start in range(0, size, panel):
        block = jnp.concatenate(
            [left[:panel, start : start + panel], identity[:, : size - panel]], axis=1
        )
        for group in range(0, panel, GROUP):
            spread = [
                jnp.broadcast_to(block[:, group + i : group + i + 1], (panel, size))
                for i in range(GROUP)
            ]
            for p in range(0, GROUP, 2):
                q = group + p
                one, two = spread[p], spread[p + 1]
                a, b, c = one[q : q + 1], two[q : q + 1], two[q + 1 : q + 2]
                scale = 1.0 / (a * c - b * b)
                factor_one = (one * c - two * b) * scale
                factor_two = (two * a - one * b) * scale
                for t in range(p + 2, GROUP):
                    spread[t] = (
                        spread[t]
                        - factor_one * spread[t][q : q + 1]
                        - factor_two * spread[t][q + 1 : q + 2]
                    )
                row_one, row_two = block[q : q + 1], block[q + 1 : q + 2]
                block = jnp.where(
                    line > q + 1,
                    block - factor_one * row_one - factor_two * row_two,
                    jnp.where(line == q + 1, row_two - (b / a) * row_one, block),
                )
        pivots = jnp.sum(jnp.where(line == lane, block, 0.0), axis=1, keepdims=True)
        small = block[:, panel : 2 * panel] * lax.rsqrt(pivots)
        rows = jnp.dot(
            small,
            jnp.concatenate([left[:panel], right[:panel]], axis=1),
            precision=HIGHEST,
            preferred_element_type=F32,
        )
        done.append(rows[:, size:])
        if start + panel < size:
            update = lax.dot_general(
                rows[:, start + panel : size],
                rows,
                (((0,), (0,)), ((), ())),
                precision=HIGHEST,
                preferred_element_type=F32,
            )
            left = left[panel:] - update[:, :size]
            right = right[panel:] - update[:, size:]
    return jnp.concatenate(done, axis=0) * by_lane


def apply_inverse(image, inverse):
    return lax.dot_general(
        image, inverse, (((1,), (1,)), ((), ())), precision=HIGHEST, preferred_element_type=F32
    )


def next_scaled(gram, spreads, total_rows):
    rows, width = spreads[0].shape

    def kernel(gram_ref, *refs):
        out_ref = refs[-1]
        inverse = inverse_factor(gram_ref[...] / total_rows)
        for i, ref in enumerate(refs[:-1]):
            current = apply_inverse(ref[...], inverse)
            out_ref[pl.ds(i * rows, rows)] = current.astype(out_ref.dtype)

    return pl.pallas_call(
        kernel,
        name="next_scaled",
        out_shape=jax.ShapeDtypeStruct((rows * len(spreads), width), jnp.bfloat16),
        in_specs=[VMEM] * (1 + len(spreads)),
        out_specs=VMEM,
        compiler_params=pltpu.CompilerParams(vmem_limit_bytes=8 * MIB),
    )(gram, *spreads)


def last_vectors(gram, images, col_place, total_rows):
    rows, width = images[0].shape
    number = len(images)

    def kernel(place_ref, gram_ref, *refs):
        out_ref = refs[-1]
        inverse = inverse_factor(gram_ref[...] / total_rows)
        for i in range(number):
            target = pl.multiple_of(lax.rem(place_ref[0] + i, number) * rows, rows)
            out_ref[pl.ds(target, rows)] = apply_inverse(refs[i][...], inverse)

    return pl.pallas_call(
        kernel,
        name="last_vectors",
        out_shape=jax.ShapeDtypeStruct((rows * number, width), F32),
        in_specs=[SMEM] + [VMEM] * (1 + number),
        out_specs=VMEM,
        compiler_params=pltpu.CompilerParams(vmem_limit_bytes=8 * MIB),
    )(col_place.reshape(1), gram, *images)


def sum_along(gram, one, two):
    next_one, opposite = one(gram), two(gram)
    return (gram + opposite) + (next_one + shift_rows(next_one, (0, 0), (0, 0), 1))


def sum_gram(gram, beside, axis):
    gram = gram + shift_rows(gram, (0, 0), (0, 0), 1)
    for place, (one, two) in enumerate(
        (
            (shift_cols_apart, lambda g: shift_cols(g, 2)),
            (lambda g: shift_rows(g, (1, 0), (-1, 0)), lambda g: shift_rows(g, (2, 0), (2, 0))),
        )
    ):
        gram = sum_along(gram, one, two)
        if place == axis:
            gram, beside = lax.optimization_barrier((gram, beside))
    for sources in (
        (1, 0, 3, 2, 5, 4, 7, 6),
        (2, 3, 0, 1, 6, 7, 4, 5),
        (6, 7, 4, 5, 2, 3, 0, 1),
    ):
        pairs = [
            (row_index(y, sources[z], core), row_index(y, z, core))
            for y in range(NY)
            for z in range(NZ)
            for core in range(NC)
        ]
        gram = gram + lax.ppermute(gram, "rows", pairs)
    return gram, beside


def shards(start, degrees, tiles, tile_rows, tile_cols, tile_counts):
    rows_here, width = start.shape
    edge = tiles.shape[1]
    slots = tiles.shape[0]
    row_tiles = rows_here // edge
    col_parts = lax.axis_size("cols")
    share = row_tiles // col_parts
    quarter = share * edge
    col_place = lax.axis_index("cols").astype(jnp.int32)
    row_place = lax.axis_index("rows").astype(jnp.int32)
    total_rows = rows_here * lax.axis_size("rows")
    core = row_place % NC
    here_z = row_place // NC % NZ
    here_y = row_place // (NC * NZ)

    degrees_part = lax.dynamic_slice_in_dim(degrees, col_place * quarter, quarter)
    spread = jnp.broadcast_to(lax.rsqrt(degrees_part.astype(F32))[:, None], (quarter, width))

    out_rows = (tile_rows - row_place * row_tiles - col_place * share) % row_tiles
    source = tile_cols // row_tiles
    place = place_of(
        (source // (NC * NZ) - here_y) % NY,
        (source // NC % NZ - here_z) % NZ,
        source % NC,
        core,
        jnp.where,
    )
    plan = plan_tiles(out_rows, place, (tile_cols % share, share), tile_counts[0], early_units())

    own_tags = [[(0, 0, 0)], [(0, 0, 1)]]
    section = lax.dynamic_slice_in_dim(start, col_place * quarter, quarter)
    steps_y = column_steps(Piece((section * spread).astype(jnp.bfloat16), own_tags))
    steps_y[-1].value, tiles_held = lax.optimization_barrier(
        (steps_y[-1].value, load_tiles(tiles, tile_counts))
    )
    column = join(*steps_y)
    beside = (tiles_held, plan, spread)
    held = None
    for rounds in range(ITERS):
        known = held

        def early(pieces, fresh):
            tiles_held, (codes, steps), _ = known or fresh
            return multiply_tiles(tiles_held, codes, steps, 0, [p.value for p in pieces])

        totals, late, fresh = gather_column(column, None if known else beside, early)
        held = known or fresh
        tiles_held, (codes, steps), spread = held
        own, one, two, three = multiply_tiles(
            tiles_held, codes, steps, 1, [p.value for p in late], totals, col_parts
        )
        one, two, three = (shift_cols(v, d) for d, v in ((1, one), (2, two), (3, three)))
        image = ((own + two) + (one + three)) * spread
        gram = lax.dot_general(
            image, image, (((0,), (0,)), ((), ())), precision=HIGHEST, preferred_element_type=F32
        )
        if rounds < ITERS - 1:
            steps_y = column_steps(Piece(image * spread, own_tags))
            gram, spreads = sum_gram(gram, [p.value for p in steps_y], 1)
            tags = join(*(Piece(None, p.tags) for p in steps_y)).tags
            column = Piece(next_scaled(gram, spreads, total_rows), tags)
        else:
            images = [image] + [shift_cols(image, -d) for d in range(1, col_parts)]
            gram, images = sum_gram(gram, images, 0)
    return last_vectors(gram, images, col_place, total_rows)


def solution(mesh):
    in_specs = (
        P("rows", None),
        P("rows"),
        P(("rows", "cols"), None, None),
        P(("rows", "cols")),
        P(("rows", "cols")),
        P(("rows", "cols")),
    )
    out_specs = P("rows", None)
    return jax.shard_map(shards, mesh=mesh, in_specs=in_specs, out_specs=out_specs, check_vma=False)
```

```python
import jax
import jax.numpy as jnp
import numpy as np
from jax import lax
from jax.experimental import pallas as pl
from jax.experimental.pallas import tpu as pltpu
from jax.sharding import PartitionSpec as P

ITERS = 2
NY, NZ, NC = 4, 8, 2
EDGE = 128
TILE_ROWS = 8
STEP = 40
CODE = 128
PLAN_STEP = 1
PANEL = 64
GROUP = 16
HIGHEST = lax.Precision.HIGHEST
F32 = jnp.float32
MIB = 1024 * 1024

VMEM = pl.BlockSpec(memory_space=pltpu.VMEM)
SMEM = pl.BlockSpec(memory_space=pltpu.SMEM)
ANY = pl.BlockSpec(memory_space=pl.ANY)
HBM = pl.BlockSpec(memory_space=pltpu.HBM)


def row_index(y, z, core):
    return ((y % NY) * NZ + z % NZ) * NC + core


def shift_rows(value, even, odd, flip=0):
    pairs = []
    for y in range(NY):
        for z in range(NZ):
            for core in range(NC):
                dy, dz = (even, odd)[core]
                pairs.append((row_index(y, z, core), row_index(y + dy, z + dz, core ^ flip)))
    return lax.ppermute(value, "rows", pairs)


def shift_cols(value, step):
    size = lax.axis_size("cols")
    return lax.ppermute(value, "cols", [(i, (i + step) % size) for i in range(size)])


class Piece:
    def __init__(self, value, tags):
        self.value, self.tags = value, tags

    def move(self, even, odd, flip=0):
        tags = [None, None]
        for core in range(NC):
            dy, dz = (even, odd)[core]
            tags[core ^ flip] = [((a - dy) % NY, (b - dz) % NZ, k) for a, b, k in self.tags[core]]
        value = None if self.value is None else shift_rows(self.value, even, odd, flip)
        return Piece(value, tags)

    def swap(self):
        return self.move((0, 0), (0, 0), 1)


def join(*pieces):
    tags = [sum((p.tags[core] for p in pieces), []) for core in range(NC)]
    if pieces[0].value is None:
        return Piece(None, tags)
    return Piece(jnp.concatenate([p.value for p in pieces], axis=0), tags)


def column_steps(own):
    return [own] + [own.move(d, d) for d in ((1, 0), (-1, 0), (2, 0))]


def gather_column(column, beside, early):
    rings = [column, column.swap()]
    pieces = list(rings)
    held = None
    for step in range(NZ // 2 - 1):
        if step == NZ // 2 - 2:
            first, pieces = pieces, []
        rings = [ring.move((0, 1), (0, -1)) for ring in rings]
        if beside and step == PLAN_STEP:
            rings[0].value, held = lax.optimization_barrier((rings[0].value, beside))
        if step < NZ // 2 - 2:
            pieces += rings + [ring.swap() for ring in rings]
    last = rings[0].move((0, 1), (0, -1))
    result = early(first, held)
    if column.value is not None:
        rings[1].value, result = lax.optimization_barrier((rings[1].value, result))
        other = rings[1].swap()
        last.value, other.value = lax.optimization_barrier((last.value, other.value))
    if column.value is None:
        other = rings[1].swap()
    late = [rings[0], rings[1], rings[0].swap(), other, last, last.swap()]
    return result, late, held


def place_of(dy, dz, k, core, where):
    mine = k == core
    line = where(dy == 0, 0, where(dy == NY - 1, 1, dy + 1))
    direct = (dz < NZ // 2) == (core == 1)
    hops = where(dz < NZ // 2, dz, NZ - dz)
    piece = 4 * hops - 2 + where(direct, where(mine, 0, 1), where(mine, 3, 2))
    ends = where(mine, 0, 1)
    piece = where(dz == 0, ends, where(dz == NZ // 2, ends + 2 * NZ - 2, piece))
    return piece * NY + line


def early_units():
    column = join(*column_steps(Piece(None, [[(0, 0, 0)], [(0, 0, 1)]])))
    first, late, _ = gather_column(column, None, lambda pieces, held: pieces)
    for core in range(NC):
        units = np.array(sum((p.tags[core] for p in first + late), []))
        found = place_of(units[:, 0], units[:, 1], units[:, 2], core, np.where)
        assert (found == np.arange(NY * NZ * NC)).all()
    return sum(len(p.tags[0]) for p in first)


def plan_tiles(rows, places, halves, count, early):
    slots = rows.shape[0]
    share = halves[1]
    units = NY * NZ * NC
    index = jnp.arange(slots, dtype=jnp.int32)
    late = (places >= early).astype(jnp.int32)
    lot = jnp.where(index < count, late, 2)
    before = (lot[None, :] == lot[:, None]) & (index[None, :] < index[:, None])
    rank = jnp.sum(before.astype(jnp.int32), axis=1)
    steps_early = (jnp.sum((lot == 0).astype(jnp.int32)) + STEP - 1) // STEP
    steps_late = (jnp.sum((lot == 1).astype(jnp.int32)) + STEP - 1) // STEP
    room = (slots + 2 * STEP - 1) // STEP * STEP
    target = jnp.where(lot == 2, room, rank + late * steps_early * STEP)
    code = (index * TILE_ROWS + rows) * CODE + (places - late * early) * share + halves[0]
    spot = jnp.arange(room, dtype=jnp.int32)
    empty = jnp.where(spot < steps_early * STEP, early * share, (units - early) * share)
    hit = target[None, :] == spot[:, None]
    found = jnp.sum(jnp.where(hit, code[None, :] + 1, 0), axis=1)
    codes = jnp.where(found > 0, found - 1, empty)
    return codes, jnp.stack([jnp.zeros_like(steps_early), steps_early, steps_early + steps_late])


def multiply_tiles(tiles, codes, steps, count, lot, parts, before=None, out_parts=None):
    slots, edge = tiles.shape[0], tiles.shape[1]
    width = parts[0].shape[1]
    sizes = [p.shape[0] // edge for p in parts]
    offsets = np.cumsum([0] + sizes)
    blocks = int(offsets[-1])
    given = [] if before is None else [before]
    whole = (TILE_ROWS, edge, width)
    number = 1 if out_parts is None else out_parts

    def kernel(*refs):
        refs = list(refs)

        def take(amount):
            taken = refs[:amount]
            del refs[:amount]
            return taken

        codes_ref, steps_ref = take(2)
        count_refs = take(0 if count is None else 1)
        (tiles_ref,) = take(1)
        given_refs, part_refs, out_refs = take(len(given)), take(len(parts)), take(number)
        held_refs = take(0 if count is None else 1)
        (totals,) = out_refs if out_parts is None else take(1)
        block_buffer, part_sems = take(2)
        copies = [
            pltpu.make_async_copy(
                part_refs[i],
                block_buffer.at[pl.ds(int(offsets[i]) * edge, sizes[i] * edge)],
                part_sems.at[i],
            )
            for i in range(len(parts))
        ]
        for copy in copies:
            copy.start()
        if count is None:
            held_ref = tiles_ref
        else:
            (held_ref,), (tile_sems,) = held_refs, refs
            chunks = (count_refs[0][0] + STEP - 1) // STEP

            def chunk_copy(chunk):
                place = pl.ds(chunk * STEP, STEP)
                return pltpu.make_async_copy(
                    tiles_ref.at[place], held_ref.at[place], tile_sems.at[chunk]
                )

            def wait_chunk(chunk, carry):
                chunk_copy(chunk).wait()
                return carry

            for chunk in range(slots // STEP):

                @pl.when(chunk < chunks)
                def _():
                    chunk_copy(chunk).start()

        totals[...] = given_refs[0][...] if given else jnp.zeros_like(totals)
        block_buffer[pl.ds(blocks * edge, edge)] = jnp.zeros((edge, width), block_buffer.dtype)
        for copy in copies:
            copy.wait()
        last = steps_ref[lot + 1]

        def body(step, waited):
            if count is not None:
                top = lax.div(codes_ref[step * STEP + STEP - 1], CODE * TILE_ROWS * STEP) + 1
                need = jnp.where(step + 1 == last, chunks, top)
                lax.fori_loop(waited, need, wait_chunk, 0)
                waited = jnp.maximum(waited, need)
            found = [codes_ref[step * STEP + u] for u in range(STEP)]
            terms = []
            for code in found:
                place = pl.multiple_of(lax.rem(code, CODE) * edge, edge)
                terms.append(
                    jnp.dot(
                        held_ref[lax.div(code, CODE * TILE_ROWS)],
                        block_buffer[pl.ds(place, edge)],
                        preferred_element_type=F32,
                    )
                )
            for code, term in zip(found, terms):
                totals[lax.rem(lax.div(code, CODE), TILE_ROWS)] += term
            return waited

        waited = lax.fori_loop(steps_ref[lot], last, body, jnp.int32(0))
        if count is not None:
            lax.fori_loop(waited, chunks, wait_chunk, 0)
        if out_parts is not None:
            for i, ref in enumerate(out_refs):
                for half in range(2):
                    ref[pl.ds(half * edge, edge)] = totals[2 * i + half]

    if out_parts is None:
        out_shape = [jax.ShapeDtypeStruct(whole, F32)]
    else:
        out_shape = [jax.ShapeDtypeStruct((2 * edge, width), F32)] * out_parts
    scratch = [] if out_parts is None else [pltpu.VMEM(whole, F32)]
    scratch += [
        pltpu.VMEM(((blocks + 1) * edge, width), parts[0].dtype),
        pltpu.SemaphoreType.DMA((len(parts),)),
    ]
    counts, limit, tile_spec = [], 12 * MIB, VMEM
    if count is not None:
        out_shape.append(jax.ShapeDtypeStruct(tiles.shape, tiles.dtype))
        scratch.append(pltpu.SemaphoreType.DMA((slots // STEP,)))
        counts, limit, tile_spec = [count], 36 * MIB, HBM
    return pl.pallas_call(
        kernel,
        name="multiply_tiles_early" if out_parts is None else "multiply_tiles_late",
        out_shape=out_shape,
        in_specs=[SMEM] * (2 + len(counts)) + [tile_spec] + [VMEM] * len(given) + [ANY] * len(parts),
        out_specs=[VMEM] * len(out_shape),
        scratch_shapes=scratch,
        compiler_params=pltpu.CompilerParams(vmem_limit_bytes=limit),
        cost_estimate=pl.CostEstimate(
            flops=2 * slots * edge * edge * width,
            bytes_accessed=slots * edge * edge + blocks * edge * width * 2,
            transcendentals=0,
        ),
    )(codes, steps, *counts, tiles, *given, *parts)


def inverse_factor(gram):
    size = gram.shape[0]
    panel = PANEL
    line_all = lax.broadcasted_iota(jnp.int32, (size, size), 0)
    lane_all = lax.broadcasted_iota(jnp.int32, (size, size), 1)
    diagonal = jnp.where(line_all == lane_all, gram, 0.0)
    by_lane = lax.rsqrt(jnp.sum(diagonal, axis=0, keepdims=True))
    by_line = lax.rsqrt(jnp.sum(diagonal, axis=1, keepdims=True))
    left = gram * by_lane * by_line
    right = jnp.where(line_all == lane_all, 1.0, 0.0).astype(F32)
    line = lax.broadcasted_iota(jnp.int32, (panel, size), 0)
    lane = lax.broadcasted_iota(jnp.int32, (panel, size), 1)
    identity = jnp.where(line == lane, 1.0, 0.0).astype(F32)
    done = []
    for start in range(0, size, panel):
        block = jnp.concatenate(
            [left[:panel, start : start + panel], identity[:, : size - panel]], axis=1
        )
        for group in range(0, panel, GROUP):
            spread = [
                jnp.broadcast_to(block[:, group + i : group + i + 1], (panel, size))
                for i in range(GROUP)
            ]
            for p in range(0, GROUP, 2):
                q = group + p
                one, two = spread[p], spread[p + 1]
                a, b, c = one[q : q + 1], two[q : q + 1], two[q + 1 : q + 2]
                scale = 1.0 / (a * c - b * b)
                factor_one = (one * c - two * b) * scale
                factor_two = (two * a - one * b) * scale
                for t in range(p + 2, GROUP):
                    spread[t] = (
                        spread[t]
                        - factor_one * spread[t][q : q + 1]
                        - factor_two * spread[t][q + 1 : q + 2]
                    )
                row_one, row_two = block[q : q + 1], block[q + 1 : q + 2]
                block = jnp.where(
                    line > q + 1,
                    block - factor_one * row_one - factor_two * row_two,
                    jnp.where(line == q + 1, row_two - (b / a) * row_one, block),
                )
        pivots = jnp.sum(jnp.where(line == lane, block, 0.0), axis=1, keepdims=True)
        small = block[:, panel : 2 * panel] * lax.rsqrt(pivots)
        rows = jnp.dot(
            small,
            jnp.concatenate([left[:panel], right[:panel]], axis=1),
            precision=HIGHEST,
            preferred_element_type=F32,
        )
        done.append(rows[:, size:])
        if start + panel < size:
            update = lax.dot_general(
                rows[:, start + panel : size],
                rows,
                (((0,), (0,)), ((), ())),
                precision=HIGHEST,
                preferred_element_type=F32,
            )
            left = left[panel:] - update[:, :size]
            right = right[panel:] - update[:, size:]
    return jnp.concatenate(done, axis=0) * by_lane


def apply_inverse(image, inverse):
    return lax.dot_general(
        image, inverse, (((1,), (1,)), ((), ())), precision=HIGHEST, preferred_element_type=F32
    )


def next_scaled(gram, spreads, total_rows):
    rows, width = spreads[0].shape

    def kernel(gram_ref, *refs):
        out_ref = refs[-1]
        inverse = inverse_factor(gram_ref[...] / total_rows)
        for i, ref in enumerate(refs[:-1]):
            current = apply_inverse(ref[...], inverse)
            out_ref[pl.ds(i * rows, rows)] = current.astype(out_ref.dtype)

    return pl.pallas_call(
        kernel,
        name="next_scaled",
        out_shape=jax.ShapeDtypeStruct((rows * len(spreads), width), jnp.bfloat16),
        in_specs=[VMEM] * (1 + len(spreads)),
        out_specs=VMEM,
        compiler_params=pltpu.CompilerParams(vmem_limit_bytes=8 * MIB),
    )(gram, *spreads)


def last_vectors(gram, images, col_place, total_rows):
    rows, width = images[0].shape
    number = len(images)

    def kernel(place_ref, gram_ref, *refs):
        out_ref = refs[-1]
        inverse = inverse_factor(gram_ref[...] / total_rows)
        for i in range(number):
            target = pl.multiple_of(lax.rem(place_ref[0] + i, number) * rows, rows)
            out_ref[pl.ds(target, rows)] = apply_inverse(refs[i][...], inverse)

    return pl.pallas_call(
        kernel,
        name="last_vectors",
        out_shape=jax.ShapeDtypeStruct((rows * number, width), F32),
        in_specs=[SMEM] + [VMEM] * (1 + number),
        out_specs=VMEM,
        compiler_params=pltpu.CompilerParams(vmem_limit_bytes=8 * MIB),
    )(col_place.reshape(1), gram, *images)


def sum_gram(gram, beside):
    one, two, three = (shift_cols(gram, d) for d in (1, 2, 3))
    gram = (gram + two) + (one + three)
    gram = gram + shift_rows(gram, (0, 0), (0, 0), 1)
    one, two, three = (shift_rows(gram, (d, 0), (d, 0)) for d in (1, 2, 3))
    gram = (gram + two) + (one + three)
    for sources in (
        (1, 0, 3, 2, 5, 4, 7, 6),
        (2, 3, 0, 1, 6, 7, 4, 5),
        (6, 7, 4, 5, 2, 3, 0, 1),
    ):
        if sources[0] == 6:
            gram, beside = lax.optimization_barrier((gram, beside))
        pairs = [
            (row_index(y, sources[z], core), row_index(y, z, core))
            for y in range(NY)
            for z in range(NZ)
            for core in range(NC)
        ]
        gram = gram + lax.ppermute(gram, "rows", pairs)
    return gram, beside


def shards(start, degrees, tiles, tile_rows, tile_cols, tile_counts):
    rows_here, width = start.shape
    edge = tiles.shape[1]
    slots = tiles.shape[0]
    row_tiles = rows_here // edge
    col_parts = lax.axis_size("cols")
    share = row_tiles // col_parts
    quarter = share * edge
    col_place = lax.axis_index("cols").astype(jnp.int32)
    row_place = lax.axis_index("rows").astype(jnp.int32)
    total_rows = rows_here * lax.axis_size("rows")
    core = row_place % NC
    here_z = row_place // NC % NZ
    here_y = row_place // (NC * NZ)

    degrees_part = lax.dynamic_slice_in_dim(degrees, col_place * quarter, quarter)
    spread = jnp.broadcast_to(lax.rsqrt(degrees_part.astype(F32))[:, None], (quarter, width))

    out_rows = (tile_rows - row_place * row_tiles - col_place * share) % row_tiles
    source = tile_cols // row_tiles
    place = place_of(
        (source // (NC * NZ) - here_y) % NY,
        (source // NC % NZ - here_z) % NZ,
        source % NC,
        core,
        jnp.where,
    )
    plan = plan_tiles(out_rows, place, (tile_cols % share, share), tile_counts[0], early_units())

    own_tags = [[(0, 0, 0)], [(0, 0, 1)]]
    section = lax.dynamic_slice_in_dim(start, col_place * quarter, quarter)
    column = join(*column_steps(Piece((section * spread).astype(jnp.bfloat16), own_tags)))
    tiles_held = None
    for rounds in range(ITERS):

        def early(pieces, fresh):
            codes, steps = plan if fresh is None else fresh[0]
            values = [p.value for p in pieces]
            if tiles_held is None:
                return multiply_tiles(tiles, codes, steps, tile_counts, 0, values)
            return *multiply_tiles(tiles_held, codes, steps, None, 0, values), tiles_held

        beside = (plan, spread) if rounds == 0 else None
        (totals, tiles_held), late, fresh = gather_column(column, beside, early)
        if rounds == 0:
            plan, spread = fresh
        own, one, two, three = multiply_tiles(
            tiles_held, *plan, None, 1, [p.value for p in late], totals, col_parts
        )
        one, two, three = (shift_cols(v, d) for d, v in ((1, one), (2, two), (3, three)))
        image = ((own + two) + (one + three)) * spread
        gram = lax.dot_general(
            image, image, (((0,), (0,)), ((), ())), precision=HIGHEST, preferred_element_type=F32
        )
        if rounds < ITERS - 1:
            steps_y = column_steps(Piece(image * spread, own_tags))
            gram, spreads = sum_gram(gram, [p.value for p in steps_y])
            tags = join(*(Piece(None, p.tags) for p in steps_y)).tags
            column = Piece(next_scaled(gram, spreads, total_rows), tags)
        else:
            images = [image] + [shift_cols(image, -d) for d in range(1, col_parts)]
            gram, images = sum_gram(gram, images)
    return last_vectors(gram, images, col_place, total_rows)


def solution(mesh):
    in_specs = (
        P("rows", None),
        P("rows"),
        P(("rows", "cols"), None, None),
        P(("rows", "cols")),
        P(("rows", "cols")),
        P(("rows", "cols")),
    )
    out_specs = P("rows", None)
    return jax.shard_map(shards, mesh=mesh, in_specs=in_specs, out_specs=out_specs, check_vma=False)
```

```python
import jax
import jax.numpy as jnp
import numpy as np
from jax import lax
from jax.experimental import pallas as pl
from jax.experimental.pallas import tpu as pltpu
from jax.sharding import PartitionSpec as P

ITERS = 2
NY, NZ, NC = 4, 8, 2
EDGE = 128
TILE_ROWS = 8
STEP = 40
ROW_BITS, SLOT_BITS = 7, 10
CODE = 1 << ROW_BITS
LOAD_STEP = 0
PANEL = 64
GROUP = 16
HIGHEST = lax.Precision.HIGHEST
F32 = jnp.float32
MIB = 1024 * 1024

VMEM = pl.BlockSpec(memory_space=pltpu.VMEM)
SMEM = pl.BlockSpec(memory_space=pltpu.SMEM)
ANY = pl.BlockSpec(memory_space=pl.ANY)


def row_index(y, z, core):
    return ((y % NY) * NZ + z % NZ) * NC + core


def shift_rows(value, even, odd, flip=0):
    pairs = []
    for y in range(NY):
        for z in range(NZ):
            for core in range(NC):
                dy, dz = (even, odd)[core]
                pairs.append((row_index(y, z, core), row_index(y + dy, z + dz, core ^ flip)))
    return lax.ppermute(value, "rows", pairs)


def shift_cols(value, step):
    size = lax.axis_size("cols")
    return lax.ppermute(value, "cols", [(i, (i + step) % size) for i in range(size)])


class Piece:
    def __init__(self, value, tags):
        self.value, self.tags = value, tags

    def move(self, even, odd, flip=0):
        tags = [None, None]
        for core in range(NC):
            dy, dz = (even, odd)[core]
            tags[core ^ flip] = [((a - dy) % NY, (b - dz) % NZ, k) for a, b, k in self.tags[core]]
        value = None if self.value is None else shift_rows(self.value, even, odd, flip)
        return Piece(value, tags)

    def swap(self):
        return self.move((0, 0), (0, 0), 1)


def join(*pieces):
    tags = [sum((p.tags[core] for p in pieces), []) for core in range(NC)]
    if pieces[0].value is None:
        return Piece(None, tags)
    return Piece(jnp.concatenate([p.value for p in pieces], axis=0), tags)


def column_steps(own):
    return [own] + [own.move(d, d) for d in ((1, 0), (-1, 0), (2, 0))]


def gather_column(column, beside, early):
    rings = [column, column.swap()]
    pieces = list(rings)
    held = None
    for step in range(NZ // 2 - 1):
        if step == NZ // 2 - 2:
            first, pieces = pieces, []
        rings = [ring.move((0, 1), (0, -1)) for ring in rings]
        if beside and step == LOAD_STEP:
            rings[0].value, held = lax.optimization_barrier((rings[0].value, beside))
            held = (load_tiles(held[0]), *held[1:])
        if step < NZ // 2 - 2:
            pieces += rings + [ring.swap() for ring in rings]
    last = rings[0].move((0, 1), (0, -1))
    result = early(first, held)
    if column.value is not None:
        rings[1].value, result = lax.optimization_barrier((rings[1].value, result))
        other = rings[1].swap()
        last.value, other.value = lax.optimization_barrier((last.value, other.value))
    if column.value is None:
        other = rings[1].swap()
    late = [rings[0], rings[1], rings[0].swap(), other, last, last.swap()]
    return result, late, held


def place_of(dy, dz, k, core, where):
    mine = k == core
    line = where(dy == 0, 0, where(dy == NY - 1, 1, dy + 1))
    direct = (dz < NZ // 2) == (core == 1)
    hops = where(dz < NZ // 2, dz, NZ - dz)
    piece = 4 * hops - 2 + where(direct, where(mine, 0, 1), where(mine, 3, 2))
    ends = where(mine, 0, 1)
    piece = where(dz == 0, ends, where(dz == NZ // 2, ends + 2 * NZ - 2, piece))
    return piece * NY + line


def early_units():
    column = join(*column_steps(Piece(None, [[(0, 0, 0)], [(0, 0, 1)]])))
    first, late, _ = gather_column(column, None, lambda pieces, held: pieces)
    for core in range(NC):
        units = np.array(sum((p.tags[core] for p in first + late), []))
        found = place_of(units[:, 0], units[:, 1], units[:, 2], core, np.where)
        assert (found == np.arange(NY * NZ * NC)).all()
    return sum(len(p.tags[0]) for p in first)


def load_tiles(tiles):
    devices = lax.axis_size("rows") * lax.axis_size("cols")
    return lax.ppermute(tiles, ("rows", "cols"), [(i, i) for i in range(devices)])


def plan_tiles(rows, places, halves, count, early):
    slots = rows.shape[0]
    share = halves[1]
    units = NY * NZ * NC
    index = jnp.arange(slots, dtype=jnp.int32)
    late = (places >= early).astype(jnp.int32)
    lot = jnp.where(index < count, late, 2)
    before = (lot[None, :] == lot[:, None]) & (index[None, :] < index[:, None])
    rank = jnp.sum(before.astype(jnp.int32), axis=1)
    steps_early = (jnp.sum((lot == 0).astype(jnp.int32)) + STEP - 1) // STEP
    steps_late = (jnp.sum((lot == 1).astype(jnp.int32)) + STEP - 1) // STEP
    room = (slots + 2 * STEP - 1) // STEP * STEP
    target = jnp.where(lot == 2, room, rank + late * steps_early * STEP)
    code = (index * TILE_ROWS + rows) * CODE + (places - late * early) * share + halves[0]
    spot = jnp.arange(room, dtype=jnp.int32)
    empty = jnp.where(spot < steps_early * STEP, early * share, (units - early) * share)
    hit = target[None, :] == spot[:, None]
    found = jnp.sum(jnp.where(hit, code[None, :] + 1, 0), axis=1)
    codes = jnp.where(found > 0, found - 1, empty)
    return codes, jnp.stack([jnp.zeros_like(steps_early), steps_early, steps_early + steps_late])


def multiply_tiles(tiles, codes, steps, lot, parts, before=None, out_parts=None):
    slots, edge = tiles.shape[0], tiles.shape[1]
    width = parts[0].shape[1]
    sizes = [p.shape[0] // edge for p in parts]
    offsets = np.cumsum([0] + sizes)
    blocks = int(offsets[-1])
    given = [] if before is None else [before]

    def kernel(codes_ref, steps_ref, tiles_ref, *refs):
        given_refs, refs = refs[: len(given)], refs[len(given) :]
        part_refs, refs = refs[: len(parts)], refs[len(parts) :]
        if out_parts is None:
            totals, block_buffer, part_sems = refs
        else:
            out_refs, (totals, block_buffer, part_sems) = refs[:out_parts], refs[out_parts:]
        copies = [
            pltpu.make_async_copy(
                part_refs[i],
                block_buffer.at[pl.ds(int(offsets[i]) * edge, sizes[i] * edge)],
                part_sems.at[i],
            )
            for i in range(len(parts))
        ]
        for copy in copies:
            copy.start()
        totals[...] = given_refs[0][...] if given else jnp.zeros_like(totals)
        block_buffer[pl.ds(blocks * edge, edge)] = jnp.zeros((edge, width), block_buffer.dtype)
        for copy in copies:
            copy.wait()

        def body(step, carry):
            found = [codes_ref[step * STEP + u] for u in range(STEP)]
            terms = []
            for code in found:
                place = pl.multiple_of((code & (CODE - 1)) * edge, edge)
                terms.append(
                    jnp.dot(
                        tiles_ref[code >> SLOT_BITS],
                        block_buffer[pl.ds(place, edge)],
                        preferred_element_type=F32,
                    )
                )
            for code, term in zip(found, terms):
                totals[(code >> ROW_BITS) & (TILE_ROWS - 1)] += term
            return carry

        lax.fori_loop(steps_ref[lot], steps_ref[lot + 1], body, 0)
        if out_parts is not None:
            for i, ref in enumerate(out_refs):
                for half in range(2):
                    ref[pl.ds(half * edge, edge)] = totals[2 * i + half]

    whole = (TILE_ROWS, edge, width)
    scratch = [pltpu.VMEM(((blocks + 1) * edge, width), parts[0].dtype), pltpu.SemaphoreType.DMA((len(parts),))]
    if out_parts is None:
        out_shape, out_specs = jax.ShapeDtypeStruct(whole, F32), VMEM
    else:
        out_shape = [jax.ShapeDtypeStruct((2 * edge, width), F32)] * out_parts
        out_specs = [VMEM] * out_parts
        scratch = [pltpu.VMEM(whole, F32)] + scratch
    return pl.pallas_call(
        kernel,
        name="multiply_tiles_early" if out_parts is None else "multiply_tiles_late",
        out_shape=out_shape,
        in_specs=[SMEM, SMEM, VMEM] + [VMEM] * len(given) + [ANY] * len(parts),
        out_specs=out_specs,
        scratch_shapes=scratch,
        compiler_params=pltpu.CompilerParams(vmem_limit_bytes=12 * MIB),
        cost_estimate=pl.CostEstimate(
            flops=2 * slots * edge * edge * width,
            bytes_accessed=slots * edge * edge + blocks * edge * width * 2,
            transcendentals=0,
        ),
    )(codes, steps, tiles, *given, *parts)


def inverse_factor(gram):
    size = gram.shape[0]
    panel = PANEL
    line_all = lax.broadcasted_iota(jnp.int32, (size, size), 0)
    lane_all = lax.broadcasted_iota(jnp.int32, (size, size), 1)
    diagonal = jnp.where(line_all == lane_all, gram, 0.0)
    by_lane = lax.rsqrt(jnp.sum(diagonal, axis=0, keepdims=True))
    by_line = lax.rsqrt(jnp.sum(diagonal, axis=1, keepdims=True))
    left = gram * by_lane * by_line
    right = jnp.where(line_all == lane_all, 1.0, 0.0).astype(F32)
    line = lax.broadcasted_iota(jnp.int32, (panel, size), 0)
    lane = lax.broadcasted_iota(jnp.int32, (panel, size), 1)
    identity = jnp.where(line == lane, 1.0, 0.0).astype(F32)
    done = []
    for start in range(0, size, panel):
        block = jnp.concatenate(
            [left[:panel, start : start + panel], identity[:, : size - panel]], axis=1
        )
        for group in range(0, panel, GROUP):
            spread = [
                jnp.broadcast_to(block[:, group + i : group + i + 1], (panel, size))
                for i in range(GROUP)
            ]
            for p in range(0, GROUP, 2):
                q = group + p
                one, two = spread[p], spread[p + 1]
                a, b, c = one[q : q + 1], two[q : q + 1], two[q + 1 : q + 2]
                scale = 1.0 / (a * c - b * b)
                factor_one = (one * c - two * b) * scale
                factor_two = (two * a - one * b) * scale
                for t in range(p + 2, GROUP):
                    spread[t] = (
                        spread[t]
                        - factor_one * spread[t][q : q + 1]
                        - factor_two * spread[t][q + 1 : q + 2]
                    )
                row_one, row_two = block[q : q + 1], block[q + 1 : q + 2]
                block = jnp.where(
                    line > q + 1,
                    block - factor_one * row_one - factor_two * row_two,
                    jnp.where(line == q + 1, row_two - (b / a) * row_one, block),
                )
        pivots = jnp.sum(jnp.where(line == lane, block, 0.0), axis=1, keepdims=True)
        small = block[:, panel : 2 * panel] * lax.rsqrt(pivots)
        rows = jnp.dot(
            small,
            jnp.concatenate([left[:panel], right[:panel]], axis=1),
            precision=HIGHEST,
            preferred_element_type=F32,
        )
        done.append(rows[:, size:])
        if start + panel < size:
            update = lax.dot_general(
                rows[:, start + panel : size],
                rows,
                (((0,), (0,)), ((), ())),
                precision=HIGHEST,
                preferred_element_type=F32,
            )
            left = left[panel:] - update[:, :size]
            right = right[panel:] - update[:, size:]
    return jnp.concatenate(done, axis=0) * by_lane


def apply_inverse(image, inverse):
    return lax.dot_general(
        image, inverse, (((1,), (1,)), ((), ())), precision=HIGHEST, preferred_element_type=F32
    )


def next_scaled(gram, spreads, total_rows):
    rows, width = spreads[0].shape

    def kernel(gram_ref, *refs):
        out_ref = refs[-1]
        inverse = inverse_factor(gram_ref[...] / total_rows)
        for i, ref in enumerate(refs[:-1]):
            current = apply_inverse(ref[...], inverse)
            out_ref[pl.ds(i * rows, rows)] = current.astype(out_ref.dtype)

    return pl.pallas_call(
        kernel,
        name="next_scaled",
        out_shape=jax.ShapeDtypeStruct((rows * len(spreads), width), jnp.bfloat16),
        in_specs=[VMEM] * (1 + len(spreads)),
        out_specs=VMEM,
        compiler_params=pltpu.CompilerParams(vmem_limit_bytes=8 * MIB),
    )(gram, *spreads)


def last_vectors(gram, images, col_place, total_rows):
    rows, width = images[0].shape
    number = len(images)

    def kernel(place_ref, gram_ref, *refs):
        out_ref = refs[-1]
        inverse = inverse_factor(gram_ref[...] / total_rows)
        for i in range(number):
            target = pl.multiple_of(lax.rem(place_ref[0] + i, number) * rows, rows)
            out_ref[pl.ds(target, rows)] = apply_inverse(refs[i][...], inverse)

    return pl.pallas_call(
        kernel,
        name="last_vectors",
        out_shape=jax.ShapeDtypeStruct((rows * number, width), F32),
        in_specs=[SMEM] + [VMEM] * (1 + number),
        out_specs=VMEM,
        compiler_params=pltpu.CompilerParams(vmem_limit_bytes=8 * MIB),
    )(col_place.reshape(1), gram, *images)


def sum_gram(gram, beside):
    one, two, three = (shift_cols(gram, d) for d in (1, 2, 3))
    gram = (gram + two) + (one + three)
    gram = gram + shift_rows(gram, (0, 0), (0, 0), 1)
    one, two, three = (shift_rows(gram, (d, 0), (d, 0)) for d in (1, 2, 3))
    gram = (gram + two) + (one + three)
    for sources in (
        (1, 0, 3, 2, 5, 4, 7, 6),
        (2, 3, 0, 1, 6, 7, 4, 5),
        (6, 7, 4, 5, 2, 3, 0, 1),
    ):
        if sources[0] == 6:
            gram, beside = lax.optimization_barrier((gram, beside))
        pairs = [
            (row_index(y, sources[z], core), row_index(y, z, core))
            for y in range(NY)
            for z in range(NZ)
            for core in range(NC)
        ]
        gram = gram + lax.ppermute(gram, "rows", pairs)
    return gram, beside


def shards(start, degrees, tiles, tile_rows, tile_cols, tile_counts):
    rows_here, width = start.shape
    edge = tiles.shape[1]
    slots = tiles.shape[0]
    row_tiles = rows_here // edge
    col_parts = lax.axis_size("cols")
    share = row_tiles // col_parts
    quarter = share * edge
    col_place = lax.axis_index("cols").astype(jnp.int32)
    row_place = lax.axis_index("rows").astype(jnp.int32)
    total_rows = rows_here * lax.axis_size("rows")
    core = row_place % NC
    here_z = row_place // NC % NZ
    here_y = row_place // (NC * NZ)

    degrees_part = lax.dynamic_slice_in_dim(degrees, col_place * quarter, quarter)
    spread = jnp.broadcast_to(lax.rsqrt(degrees_part.astype(F32))[:, None], (quarter, width))

    out_rows = (tile_rows - row_place * row_tiles - col_place * share) % row_tiles
    source = tile_cols // row_tiles
    place = place_of(
        (source // (NC * NZ) - here_y) % NY,
        (source // NC % NZ - here_z) % NZ,
        source % NC,
        core,
        jnp.where,
    )
    plan = plan_tiles(out_rows, place, (tile_cols % share, share), tile_counts[0], early_units())

    own_tags = [[(0, 0, 0)], [(0, 0, 1)]]
    section = lax.dynamic_slice_in_dim(start, col_place * quarter, quarter)
    column = join(*column_steps(Piece((section * spread).astype(jnp.bfloat16), own_tags)))
    held = None
    for rounds in range(ITERS):
        known = held

        def early(pieces, fresh):
            tiles_held, (codes, steps), _ = known or fresh
            return multiply_tiles(tiles_held, codes, steps, 0, [p.value for p in pieces])

        beside = (tiles, plan, spread) if rounds == 0 else None
        totals, late, fresh = gather_column(column, beside, early)
        held = known or fresh
        tiles_held, (codes, steps), spread = held
        own, one, two, three = multiply_tiles(
            tiles_held, codes, steps, 1, [p.value for p in late], totals, col_parts
        )
        one, two, three = (shift_cols(v, d) for d, v in ((1, one), (2, two), (3, three)))
        image = ((own + two) + (one + three)) * spread
        gram = lax.dot_general(
            image, image, (((0,), (0,)), ((), ())), precision=HIGHEST, preferred_element_type=F32
        )
        if rounds < ITERS - 1:
            steps_y = column_steps(Piece(image * spread, own_tags))
            gram, spreads = sum_gram(gram, [p.value for p in steps_y])
            tags = join(*(Piece(None, p.tags) for p in steps_y)).tags
            column = Piece(next_scaled(gram, spreads, total_rows), tags)
        else:
            images = [image] + [shift_cols(image, -d) for d in range(1, col_parts)]
            gram, images = sum_gram(gram, images)
    return last_vectors(gram, images, col_place, total_rows)


def solution(mesh):
    in_specs = (
        P("rows", None),
        P("rows"),
        P(("rows", "cols"), None, None),
        P(("rows", "cols")),
        P(("rows", "cols")),
        P(("rows", "cols")),
    )
    out_specs = P("rows", None)
    return jax.shard_map(shards, mesh=mesh, in_specs=in_specs, out_specs=out_specs, check_vma=False)
```

```python
import jax
import jax.numpy as jnp
import numpy as np
from jax import lax
from jax.experimental import pallas as pl
from jax.experimental.pallas import tpu as pltpu
from jax.sharding import PartitionSpec as P

ITERS = 2
NY, NZ, NC = 4, 8, 2
EDGE = 128
TILE_ROWS = 8
STEP = 40
ROW_BITS, SLOT_BITS = 7, 10
CODE = 1 << ROW_BITS
LOAD_STEP = 1
PANEL = 64
GROUP = 16
HIGHEST = lax.Precision.HIGHEST
F32 = jnp.float32
MIB = 1024 * 1024

VMEM = pl.BlockSpec(memory_space=pltpu.VMEM)
SMEM = pl.BlockSpec(memory_space=pltpu.SMEM)
ANY = pl.BlockSpec(memory_space=pl.ANY)
HBM = pl.BlockSpec(memory_space=pltpu.HBM)


def row_index(y, z, core):
    return ((y % NY) * NZ + z % NZ) * NC + core


def shift_rows(value, even, odd, flip=0):
    pairs = []
    for y in range(NY):
        for z in range(NZ):
            for core in range(NC):
                dy, dz = (even, odd)[core]
                pairs.append((row_index(y, z, core), row_index(y + dy, z + dz, core ^ flip)))
    return lax.ppermute(value, "rows", pairs)


def shift_cols(value, step):
    size = lax.axis_size("cols")
    return lax.ppermute(value, "cols", [(i, (i + step) % size) for i in range(size)])


class Piece:
    def __init__(self, value, tags):
        self.value, self.tags = value, tags

    def move(self, even, odd, flip=0):
        tags = [None, None]
        for core in range(NC):
            dy, dz = (even, odd)[core]
            tags[core ^ flip] = [((a - dy) % NY, (b - dz) % NZ, k) for a, b, k in self.tags[core]]
        value = None if self.value is None else shift_rows(self.value, even, odd, flip)
        return Piece(value, tags)

    def swap(self):
        return self.move((0, 0), (0, 0), 1)


def join(*pieces):
    tags = [sum((p.tags[core] for p in pieces), []) for core in range(NC)]
    if pieces[0].value is None:
        return Piece(None, tags)
    return Piece(jnp.concatenate([p.value for p in pieces], axis=0), tags)


def column_steps(own):
    return [own] + [own.move(d, d) for d in ((1, 0), (-1, 0), (2, 0))]


def gather_column(column, beside, early, far=None):
    rings = [column, column.swap()]
    pieces = list(rings)
    held = None
    for step in range(NZ // 2 - 1):
        if step == NZ // 2 - 2:
            first, pieces = pieces, []
        rings = [ring.move((0, 1), (0, -1)) for ring in rings]
        if beside and step == LOAD_STEP:
            held = beside()
            rings[0].value, held = lax.optimization_barrier((rings[0].value, held))
        if step < NZ // 2 - 2:
            pieces += rings + [ring.swap() for ring in rings]
    last = far or rings[0].move((0, 1), (0, -1))
    result = early(first, held)
    if column.value is None:
        other = rings[1].swap()
    else:
        rings[1].value, result = lax.optimization_barrier((rings[1].value, result))
        other = rings[1].swap()
        if far is None:
            last.value, other.value = lax.optimization_barrier((last.value, other.value))
    late = [rings[0], rings[1], rings[0].swap(), other, last, last.swap()]
    return result, late, held


def place_of(dy, dz, k, core, where):
    mine = k == core
    line = where(dy == 0, 0, where(dy == NY - 1, 1, dy + 1))
    direct = (dz < NZ // 2) == (core == 1)
    hops = where(dz < NZ // 2, dz, NZ - dz)
    piece = 4 * hops - 2 + where(direct, where(mine, 0, 1), where(mine, 3, 2))
    ends = where(mine, 0, 1)
    piece = where(dz == 0, ends, where(dz == NZ // 2, ends + 2 * NZ - 2, piece))
    return piece * NY + line


def early_units():
    column = join(*column_steps(Piece(None, [[(0, 0, 0)], [(0, 0, 1)]])))
    first, late, _ = gather_column(column, None, lambda pieces, held: pieces)
    for core in range(NC):
        units = np.array(sum((p.tags[core] for p in first + late), []))
        found = place_of(units[:, 0], units[:, 1], units[:, 2], core, np.where)
        assert (found == np.arange(NY * NZ * NC)).all()
    return sum(len(p.tags[0]) for p in first)


def load_tiles(tiles, count):
    all_steps = range(tiles.shape[0] // STEP)

    def kernel(count_ref, tiles_ref, out_ref, sem):
        steps = (count_ref[0] + STEP - 1) // STEP

        def copy(step):
            place = pl.ds(step * STEP, STEP)
            return pltpu.make_async_copy(tiles_ref.at[place], out_ref.at[place], sem.at[step])

        for step in all_steps:

            @pl.when(step < steps)
            def _():
                copy(step).start()

        for step in all_steps:

            @pl.when(step < steps)
            def _():
                copy(step).wait()

    return pl.pallas_call(
        kernel,
        name="load_tiles",
        out_shape=jax.ShapeDtypeStruct(tiles.shape, tiles.dtype),
        in_specs=[SMEM, HBM],
        out_specs=VMEM,
        scratch_shapes=[pltpu.SemaphoreType.DMA((len(all_steps),))],
        compiler_params=pltpu.CompilerParams(vmem_limit_bytes=40 * MIB),
        cost_estimate=pl.CostEstimate(flops=0, bytes_accessed=2 * tiles.size, transcendentals=0),
    )(count, tiles)


def plan_tiles(rows, places, halves, count, early):
    slots = rows.shape[0]
    share = halves[1]
    units = NY * NZ * NC
    index = jnp.arange(slots, dtype=jnp.int32)
    late = (places >= early).astype(jnp.int32)
    lot = jnp.where(index < count, late, 2)
    before = (lot[None, :] == lot[:, None]) & (index[None, :] < index[:, None])
    rank = jnp.sum(before.astype(jnp.int32), axis=1)
    steps_early = (jnp.sum((lot == 0).astype(jnp.int32)) + STEP - 1) // STEP
    steps_late = (jnp.sum((lot == 1).astype(jnp.int32)) + STEP - 1) // STEP
    room = (slots + 2 * STEP - 1) // STEP * STEP
    target = jnp.where(lot == 2, room, rank + late * steps_early * STEP)
    code = (index * TILE_ROWS + rows) * CODE + (places - late * early) * share + halves[0]
    spot = jnp.arange(room, dtype=jnp.int32)
    empty = jnp.where(spot < steps_early * STEP, early * share, (units - early) * share)
    hit = target[None, :] == spot[:, None]
    found = jnp.sum(jnp.where(hit, code[None, :] + 1, 0), axis=1)
    codes = jnp.where(found > 0, found - 1, empty)
    return codes, jnp.stack([jnp.zeros_like(steps_early), steps_early, steps_early + steps_late])


def multiply_tiles(tiles, codes, steps, lot, parts, before=None, out_parts=None):
    slots, edge = tiles.shape[0], tiles.shape[1]
    width = parts[0].shape[1]
    sizes = [p.shape[0] // edge for p in parts]
    offsets = np.cumsum([0] + sizes)
    blocks = int(offsets[-1])
    given = [] if before is None else [before]

    def kernel(codes_ref, steps_ref, tiles_ref, *refs):
        given_refs, refs = refs[: len(given)], refs[len(given) :]
        part_refs, refs = refs[: len(parts)], refs[len(parts) :]
        if out_parts is None:
            totals, block_buffer, part_sems = refs
        else:
            out_refs, (totals, block_buffer, part_sems) = refs[:out_parts], refs[out_parts:]
        copies = [
            pltpu.make_async_copy(
                part_refs[i],
                block_buffer.at[pl.ds(int(offsets[i]) * edge, sizes[i] * edge)],
                part_sems.at[i],
            )
            for i in range(len(parts))
        ]
        for copy in copies:
            copy.start()
        totals[...] = given_refs[0][...] if given else jnp.zeros_like(totals)
        block_buffer[pl.ds(blocks * edge, edge)] = jnp.zeros((edge, width), block_buffer.dtype)
        for copy in copies:
            copy.wait()

        def body(step, carry):
            found = [codes_ref[step * STEP + u] for u in range(STEP)]
            terms = []
            for code in found:
                place = pl.multiple_of((code & (CODE - 1)) * edge, edge)
                terms.append(
                    jnp.dot(
                        tiles_ref[code >> SLOT_BITS],
                        block_buffer[pl.ds(place, edge)],
                        preferred_element_type=F32,
                    )
                )
            for code, term in zip(found, terms):
                totals[(code >> ROW_BITS) & (TILE_ROWS - 1)] += term
            return carry

        lax.fori_loop(steps_ref[lot], steps_ref[lot + 1], body, 0)
        if out_parts is not None:
            for i, ref in enumerate(out_refs):
                for half in range(2):
                    ref[pl.ds(half * edge, edge)] = totals[2 * i + half]

    whole = (TILE_ROWS, edge, width)
    scratch = [pltpu.VMEM(((blocks + 1) * edge, width), parts[0].dtype), pltpu.SemaphoreType.DMA((len(parts),))]
    if out_parts is None:
        out_shape, out_specs = jax.ShapeDtypeStruct(whole, F32), VMEM
    else:
        out_shape = [jax.ShapeDtypeStruct((2 * edge, width), F32)] * out_parts
        out_specs = [VMEM] * out_parts
        scratch = [pltpu.VMEM(whole, F32)] + scratch
    return pl.pallas_call(
        kernel,
        name="multiply_tiles_early" if out_parts is None else "multiply_tiles_late",
        out_shape=out_shape,
        in_specs=[SMEM, SMEM, VMEM] + [VMEM] * len(given) + [ANY] * len(parts),
        out_specs=out_specs,
        scratch_shapes=scratch,
        compiler_params=pltpu.CompilerParams(vmem_limit_bytes=12 * MIB),
        cost_estimate=pl.CostEstimate(
            flops=2 * slots * edge * edge * width,
            bytes_accessed=slots * edge * edge + blocks * edge * width * 2,
            transcendentals=0,
        ),
    )(codes, steps, tiles, *given, *parts)


def inverse_factor(gram):
    size = gram.shape[0]
    panel = PANEL
    line_all = lax.broadcasted_iota(jnp.int32, (size, size), 0)
    lane_all = lax.broadcasted_iota(jnp.int32, (size, size), 1)
    diagonal = jnp.where(line_all == lane_all, gram, 0.0)
    by_lane = lax.rsqrt(jnp.sum(diagonal, axis=0, keepdims=True))
    by_line = lax.rsqrt(jnp.sum(diagonal, axis=1, keepdims=True))
    left = gram * by_lane * by_line
    right = jnp.where(line_all == lane_all, 1.0, 0.0).astype(F32)
    line = lax.broadcasted_iota(jnp.int32, (panel, size), 0)
    lane = lax.broadcasted_iota(jnp.int32, (panel, size), 1)
    identity = jnp.where(line == lane, 1.0, 0.0).astype(F32)
    done = []
    for start in range(0, size, panel):
        block = jnp.concatenate(
            [left[:panel, start : start + panel], identity[:, : size - panel]], axis=1
        )
        for group in range(0, panel, GROUP):
            spread = [
                jnp.broadcast_to(block[:, group + i : group + i + 1], (panel, size))
                for i in range(GROUP)
            ]
            for p in range(0, GROUP, 2):
                q = group + p
                one, two = spread[p], spread[p + 1]
                a, b, c = one[q : q + 1], two[q : q + 1], two[q + 1 : q + 2]
                scale = 1.0 / (a * c - b * b)
                factor_one = (one * c - two * b) * scale
                factor_two = (two * a - one * b) * scale
                for t in range(p + 2, GROUP):
                    spread[t] = (
                        spread[t]
                        - factor_one * spread[t][q : q + 1]
                        - factor_two * spread[t][q + 1 : q + 2]
                    )
                row_one, row_two = block[q : q + 1], block[q + 1 : q + 2]
                block = jnp.where(
                    line > q + 1,
                    block - factor_one * row_one - factor_two * row_two,
                    jnp.where(line == q + 1, row_two - (b / a) * row_one, block),
                )
        pivots = jnp.sum(jnp.where(line == lane, block, 0.0), axis=1, keepdims=True)
        small = block[:, panel : 2 * panel] * lax.rsqrt(pivots)
        rows = jnp.dot(
            small,
            jnp.concatenate([left[:panel], right[:panel]], axis=1),
            precision=HIGHEST,
            preferred_element_type=F32,
        )
        done.append(rows[:, size:])
        if start + panel < size:
            update = lax.dot_general(
                rows[:, start + panel : size],
                rows,
                (((0,), (0,)), ((), ())),
                precision=HIGHEST,
                preferred_element_type=F32,
            )
            left = left[panel:] - update[:, :size]
            right = right[panel:] - update[:, size:]
    return jnp.concatenate(done, axis=0) * by_lane


def apply_inverse(image, inverse):
    return lax.dot_general(
        image, inverse, (((1,), (1,)), ((), ())), precision=HIGHEST, preferred_element_type=F32
    )


def next_scaled(gram, spreads, columns, total_rows):
    width = spreads[0].shape[1]
    rows = spreads[0].shape[0] // columns

    def kernel(gram_ref, *refs):
        part_refs, out_refs = refs[: len(spreads)], refs[len(spreads) :]
        inverse = inverse_factor(gram_ref[...] / total_rows)
        for i, ref in enumerate(part_refs):
            current = apply_inverse(ref[...], inverse).astype(jnp.bfloat16)
            for j, out_ref in enumerate(out_refs):
                out_ref[pl.ds(i * rows, rows)] = current[j * rows : (j + 1) * rows]

    return pl.pallas_call(
        kernel,
        name="next_scaled",
        out_shape=[jax.ShapeDtypeStruct((rows * len(spreads), width), jnp.bfloat16)] * columns,
        in_specs=[VMEM] * (1 + len(spreads)),
        out_specs=[VMEM] * columns,
        compiler_params=pltpu.CompilerParams(vmem_limit_bytes=8 * MIB),
    )(gram, *spreads)


def last_vectors(gram, images, col_place, total_rows):
    rows, width = images[0].shape
    number = len(images)

    def kernel(place_ref, gram_ref, *refs):
        out_ref = refs[-1]
        inverse = inverse_factor(gram_ref[...] / total_rows)
        for i in range(number):
            target = pl.multiple_of(lax.rem(place_ref[0] + i, number) * rows, rows)
            out_ref[pl.ds(target, rows)] = apply_inverse(refs[i][...], inverse)

    return pl.pallas_call(
        kernel,
        name="last_vectors",
        out_shape=jax.ShapeDtypeStruct((rows * number, width), F32),
        in_specs=[SMEM] + [VMEM] * (1 + number),
        out_specs=VMEM,
        compiler_params=pltpu.CompilerParams(vmem_limit_bytes=8 * MIB),
    )(col_place.reshape(1), gram, *images)


def sum_gram(gram, beside):
    one, two, three = (shift_cols(gram, d) for d in (1, 2, 3))
    gram = (gram + two) + (one + three)
    gram = gram + shift_rows(gram, (0, 0), (0, 0), 1)
    one, two, three = (shift_rows(gram, (d, 0), (d, 0)) for d in (1, 2, 3))
    gram = (gram + two) + (one + three)
    for sources in (
        (1, 0, 3, 2, 5, 4, 7, 6),
        (2, 3, 0, 1, 6, 7, 4, 5),
        (6, 7, 4, 5, 2, 3, 0, 1),
    ):
        if sources[0] == 6:
            gram, beside = lax.optimization_barrier((gram, beside))
        pairs = [
            (row_index(y, sources[z], core), row_index(y, z, core))
            for y in range(NY)
            for z in range(NZ)
            for core in range(NC)
        ]
        gram = gram + lax.ppermute(gram, "rows", pairs)
    return gram, beside


def shards(start, degrees, tiles, tile_rows, tile_cols, tile_counts):
    rows_here, width = start.shape
    edge = tiles.shape[1]
    slots = tiles.shape[0]
    row_tiles = rows_here // edge
    col_parts = lax.axis_size("cols")
    share = row_tiles // col_parts
    quarter = share * edge
    col_place = lax.axis_index("cols").astype(jnp.int32)
    row_place = lax.axis_index("rows").astype(jnp.int32)
    total_rows = rows_here * lax.axis_size("rows")
    core = row_place % NC
    here_z = row_place // NC % NZ
    here_y = row_place // (NC * NZ)

    degrees_part = lax.dynamic_slice_in_dim(degrees, col_place * quarter, quarter)
    spread = jnp.broadcast_to(lax.rsqrt(degrees_part.astype(F32))[:, None], (quarter, width))

    out_rows = (tile_rows - row_place * row_tiles - col_place * share) % row_tiles
    source = tile_cols // row_tiles
    place = place_of(
        (source // (NC * NZ) - here_y) % NY,
        (source // NC % NZ - here_z) % NZ,
        source % NC,
        core,
        jnp.where,
    )
    plan = plan_tiles(out_rows, place, (tile_cols % share, share), tile_counts[0], early_units())

    def load():
        return load_tiles(tiles, tile_counts), plan, spread

    own_tags = [[(0, 0, 0)], [(0, 0, 1)]]
    section = lax.dynamic_slice_in_dim(start, col_place * quarter, quarter)
    column = join(*column_steps(Piece((section * spread).astype(jnp.bfloat16), own_tags)))
    held = far = None
    for rounds in range(ITERS):
        known = held

        def early(pieces, fresh):
            tiles_held, (codes, steps), _ = known or fresh
            return multiply_tiles(tiles_held, codes, steps, 0, [p.value for p in pieces])

        beside = load if rounds == 0 else None
        totals, late, fresh = gather_column(column, beside, early, far)
        held = known or fresh
        tiles_held, (codes, steps), spread = held
        own, one, two, three = multiply_tiles(
            tiles_held, codes, steps, 1, [p.value for p in late], totals, col_parts
        )
        one, two, three = (shift_cols(v, d) for d, v in ((1, one), (2, two), (3, three)))
        image = ((own + two) + (one + three)) * spread
        gram = lax.dot_general(
            image, image, (((0,), (0,)), ((), ())), precision=HIGHEST, preferred_element_type=F32
        )
        if rounds < ITERS - 1:
            own = Piece(image * spread, own_tags)
            steps_y = column_steps(join(own, own.move((0, NZ // 2), (0, NZ // 2))))
            gram, spreads = sum_gram(gram, [p.value for p in steps_y])
            column, far = (
                Piece(value, [[p.tags[core][i] for p in steps_y] for core in range(NC)])
                for i, value in enumerate(next_scaled(gram, spreads, 2, total_rows))
            )
        else:
            images = [image] + [shift_cols(image, -d) for d in range(1, col_parts)]
            gram, images = sum_gram(gram, images)
    return last_vectors(gram, images, col_place, total_rows)


def solution(mesh):
    in_specs = (
        P("rows", None),
        P("rows"),
        P(("rows", "cols"), None, None),
        P(("rows", "cols")),
        P(("rows", "cols")),
        P(("rows", "cols")),
    )
    out_specs = P("rows", None)
    return jax.shard_map(shards, mesh=mesh, in_specs=in_specs, out_specs=out_specs, check_vma=False)
```

```python
import jax
import jax.numpy as jnp
import numpy as np
from jax import lax
from jax.experimental import pallas as pl
from jax.experimental.pallas import tpu as pltpu
from jax.sharding import PartitionSpec as P

ITERS = 2
NY, NZ, NC = 4, 8, 2
EDGE = 128
TILE_ROWS = 8
STEP = 40
ROW_BITS, SLOT_BITS = 7, 10
CODE = 1 << ROW_BITS
FLIGHT = 4
PLAN_STEP = 1
PANEL = 64
GROUP = 16
HIGHEST = lax.Precision.HIGHEST
F32 = jnp.float32
MIB = 1024 * 1024

VMEM = pl.BlockSpec(memory_space=pltpu.VMEM)
SMEM = pl.BlockSpec(memory_space=pltpu.SMEM)
ANY = pl.BlockSpec(memory_space=pl.ANY)
HBM = pl.BlockSpec(memory_space=pltpu.HBM)


def row_index(y, z, core):
    return ((y % NY) * NZ + z % NZ) * NC + core


def shift_rows(value, even, odd, flip=0):
    pairs = []
    for y in range(NY):
        for z in range(NZ):
            for core in range(NC):
                dy, dz = (even, odd)[core]
                pairs.append((row_index(y, z, core), row_index(y + dy, z + dz, core ^ flip)))
    return lax.ppermute(value, "rows", pairs)


def shift_cols(value, step):
    size = lax.axis_size("cols")
    return lax.ppermute(value, "cols", [(i, (i + step) % size) for i in range(size)])


class Piece:
    def __init__(self, value, tags):
        self.value, self.tags = value, tags

    def move(self, even, odd, flip=0):
        tags = [None, None]
        for core in range(NC):
            dy, dz = (even, odd)[core]
            tags[core ^ flip] = [((a - dy) % NY, (b - dz) % NZ, k) for a, b, k in self.tags[core]]
        value = None if self.value is None else shift_rows(self.value, even, odd, flip)
        return Piece(value, tags)

    def swap(self):
        return self.move((0, 0), (0, 0), 1)


def join(*pieces):
    tags = [sum((p.tags[core] for p in pieces), []) for core in range(NC)]
    if pieces[0].value is None:
        return Piece(None, tags)
    return Piece(jnp.concatenate([p.value for p in pieces], axis=0), tags)


def column_steps(own):
    return [own] + [own.move(d, d) for d in ((1, 0), (-1, 0), (2, 0))]


def gather_column(column, beside, early):
    rings = [column, column.swap()]
    pieces = list(rings)
    held = None
    for step in range(NZ // 2 - 1):
        if step == NZ // 2 - 2:
            first, pieces = pieces, []
        rings = [ring.move((0, 1), (0, -1)) for ring in rings]
        if beside and step == PLAN_STEP:
            rings[0].value, held = lax.optimization_barrier((rings[0].value, beside))
        if step < NZ // 2 - 2:
            pieces += rings + [ring.swap() for ring in rings]
    last = rings[0].move((0, 1), (0, -1))
    result = early(first, held)
    if column.value is not None:
        rings[1].value, result = lax.optimization_barrier((rings[1].value, result))
        other = rings[1].swap()
        last.value, other.value = lax.optimization_barrier((last.value, other.value))
    if column.value is None:
        other = rings[1].swap()
    late = [rings[0], rings[1], rings[0].swap(), other, last, last.swap()]
    return result, late, held


def place_of(dy, dz, k, core, where):
    mine = k == core
    line = where(dy == 0, 0, where(dy == NY - 1, 1, dy + 1))
    direct = (dz < NZ // 2) == (core == 1)
    hops = where(dz < NZ // 2, dz, NZ - dz)
    piece = 4 * hops - 2 + where(direct, where(mine, 0, 1), where(mine, 3, 2))
    ends = where(mine, 0, 1)
    piece = where(dz == 0, ends, where(dz == NZ // 2, ends + 2 * NZ - 2, piece))
    return piece * NY + line


def early_units():
    column = join(*column_steps(Piece(None, [[(0, 0, 0)], [(0, 0, 1)]])))
    first, late, _ = gather_column(column, None, lambda pieces, held: pieces)
    for core in range(NC):
        units = np.array(sum((p.tags[core] for p in first + late), []))
        found = place_of(units[:, 0], units[:, 1], units[:, 2], core, np.where)
        assert (found == np.arange(NY * NZ * NC)).all()
    return sum(len(p.tags[0]) for p in first)


def plan_tiles(rows, places, halves, count, early):
    slots = rows.shape[0]
    share = halves[1]
    units = NY * NZ * NC
    index = jnp.arange(slots, dtype=jnp.int32)
    late = (places >= early).astype(jnp.int32)
    lot = jnp.where(index < count, late, 2)
    before = (lot[None, :] == lot[:, None]) & (index[None, :] < index[:, None])
    rank = jnp.sum(before.astype(jnp.int32), axis=1)
    steps_early = (jnp.sum((lot == 0).astype(jnp.int32)) + STEP - 1) // STEP
    steps_late = (jnp.sum((lot == 1).astype(jnp.int32)) + STEP - 1) // STEP
    room = (slots + 2 * STEP - 1) // STEP * STEP
    target = jnp.where(lot == 2, room, rank + late * steps_early * STEP)
    code = (index * TILE_ROWS + rows) * CODE + (places - late * early) * share + halves[0]
    spot = jnp.arange(room, dtype=jnp.int32)
    empty = jnp.where(spot < steps_early * STEP, early * share, (units - early) * share)
    hit = target[None, :] == spot[:, None]
    found = jnp.sum(jnp.where(hit, code[None, :] + 1, 0), axis=1)
    codes = jnp.where(found > 0, found - 1, empty)
    return codes, jnp.stack([jnp.zeros_like(steps_early), steps_early, steps_early + steps_late])


def multiply_tiles(tiles, codes, steps, count, lot, parts, before=None, out_parts=None):
    slots, edge = tiles.shape[0], tiles.shape[1]
    width = parts[0].shape[1]
    sizes = [p.shape[0] // edge for p in parts]
    offsets = np.cumsum([0] + sizes)
    blocks = int(offsets[-1])
    given = [] if before is None else [before]
    whole = (TILE_ROWS, edge, width)
    number = 1 if out_parts is None else out_parts

    def kernel(*refs):
        refs = list(refs)

        def take(amount):
            taken = refs[:amount]
            del refs[:amount]
            return taken

        codes_ref, steps_ref = take(2)
        count_refs = take(0 if count is None else 1)
        (tiles_ref,) = take(1)
        given_refs, part_refs, out_refs = take(len(given)), take(len(parts)), take(number)
        held_refs = take(0 if count is None else 1)
        (totals,) = out_refs if out_parts is None else take(1)
        block_buffer, part_sems = take(2)
        copies = [
            pltpu.make_async_copy(
                part_refs[i],
                block_buffer.at[pl.ds(int(offsets[i]) * edge, sizes[i] * edge)],
                part_sems.at[i],
            )
            for i in range(len(parts))
        ]
        for copy in copies:
            copy.start()
        if count is None:
            held_ref = tiles_ref
        else:
            (held_ref,), (tile_sems,) = held_refs, refs
            chunks = (count_refs[0][0] + STEP - 1) // STEP

            def chunk_copy(chunk):
                place = pl.ds(chunk * STEP, STEP)
                return pltpu.make_async_copy(
                    tiles_ref.at[place], held_ref.at[place], tile_sems.at[chunk]
                )

            def wait_chunk(chunk, carry):
                chunk_copy(chunk).wait()

                @pl.when(chunk + FLIGHT < chunks)
                def _():
                    chunk_copy(chunk + FLIGHT).start()

                return carry

            for chunk in range(FLIGHT):

                @pl.when(chunk < chunks)
                def _():
                    chunk_copy(chunk).start()

        totals[...] = given_refs[0][...] if given else jnp.zeros_like(totals)
        block_buffer[pl.ds(blocks * edge, edge)] = jnp.zeros((edge, width), block_buffer.dtype)
        for copy in copies:
            copy.wait()
        last = steps_ref[lot + 1]

        def body(step, waited):
            if count is not None:
                top = lax.div(codes_ref[step * STEP + STEP - 1] >> SLOT_BITS, STEP) + 1
                need = jnp.where(step + 1 == last, chunks, top)
                lax.fori_loop(waited, need, wait_chunk, 0)
                waited = jnp.maximum(waited, need)
            found = [codes_ref[step * STEP + u] for u in range(STEP)]
            terms = []
            for code in found:
                place = pl.multiple_of((code & (CODE - 1)) * edge, edge)
                terms.append(
                    jnp.dot(
                        held_ref[code >> SLOT_BITS],
                        block_buffer[pl.ds(place, edge)],
                        preferred_element_type=F32,
                    )
                )
            for code, term in zip(found, terms):
                totals[(code >> ROW_BITS) & (TILE_ROWS - 1)] += term
            return waited

        waited = lax.fori_loop(steps_ref[lot], last, body, jnp.int32(0))
        if count is not None:
            lax.fori_loop(waited, chunks, wait_chunk, 0)
        if out_parts is not None:
            for i, ref in enumerate(out_refs):
                for half in range(2):
                    ref[pl.ds(half * edge, edge)] = totals[2 * i + half]

    if out_parts is None:
        out_shape = [jax.ShapeDtypeStruct(whole, F32)]
    else:
        out_shape = [jax.ShapeDtypeStruct((2 * edge, width), F32)] * out_parts
    scratch = [] if out_parts is None else [pltpu.VMEM(whole, F32)]
    scratch += [
        pltpu.VMEM(((blocks + 1) * edge, width), parts[0].dtype),
        pltpu.SemaphoreType.DMA((len(parts),)),
    ]
    counts, limit, tile_spec = [], 12 * MIB, VMEM
    if count is not None:
        out_shape.append(jax.ShapeDtypeStruct(tiles.shape, tiles.dtype))
        scratch.append(pltpu.SemaphoreType.DMA((slots // STEP,)))
        counts, limit, tile_spec = [count], 36 * MIB, HBM
    return pl.pallas_call(
        kernel,
        name="multiply_tiles_early" if out_parts is None else "multiply_tiles_late",
        out_shape=out_shape,
        in_specs=[SMEM] * (2 + len(counts)) + [tile_spec] + [VMEM] * len(given) + [ANY] * len(parts),
        out_specs=[VMEM] * len(out_shape),
        scratch_shapes=scratch,
        compiler_params=pltpu.CompilerParams(vmem_limit_bytes=limit),
        cost_estimate=pl.CostEstimate(
            flops=2 * slots * edge * edge * width,
            bytes_accessed=slots * edge * edge + blocks * edge * width * 2,
            transcendentals=0,
        ),
    )(codes, steps, *counts, tiles, *given, *parts)


def inverse_factor(gram):
    size = gram.shape[0]
    panel = PANEL
    line_all = lax.broadcasted_iota(jnp.int32, (size, size), 0)
    lane_all = lax.broadcasted_iota(jnp.int32, (size, size), 1)
    diagonal = jnp.where(line_all == lane_all, gram, 0.0)
    by_lane = lax.rsqrt(jnp.sum(diagonal, axis=0, keepdims=True))
    by_line = lax.rsqrt(jnp.sum(diagonal, axis=1, keepdims=True))
    left = gram * by_lane * by_line
    right = jnp.where(line_all == lane_all, 1.0, 0.0).astype(F32)
    line = lax.broadcasted_iota(jnp.int32, (panel, size), 0)
    lane = lax.broadcasted_iota(jnp.int32, (panel, size), 1)
    identity = jnp.where(line == lane, 1.0, 0.0).astype(F32)
    done = []
    for start in range(0, size, panel):
        block = jnp.concatenate(
            [left[:panel, start : start + panel], identity[:, : size - panel]], axis=1
        )
        for group in range(0, panel, GROUP):
            spread = [
                jnp.broadcast_to(block[:, group + i : group + i + 1], (panel, size))
                for i in range(GROUP)
            ]
            for p in range(0, GROUP, 2):
                q = group + p
                one, two = spread[p], spread[p + 1]
                a, b, c = one[q : q + 1], two[q : q + 1], two[q + 1 : q + 2]
                scale = 1.0 / (a * c - b * b)
                factor_one = (one * c - two * b) * scale
                factor_two = (two * a - one * b) * scale
                for t in range(p + 2, GROUP):
                    spread[t] = (
                        spread[t]
                        - factor_one * spread[t][q : q + 1]
                        - factor_two * spread[t][q + 1 : q + 2]
                    )
                row_one, row_two = block[q : q + 1], block[q + 1 : q + 2]
                block = jnp.where(
                    line > q + 1,
                    block - factor_one * row_one - factor_two * row_two,
                    jnp.where(line == q + 1, row_two - (b / a) * row_one, block),
                )
        pivots = jnp.sum(jnp.where(line == lane, block, 0.0), axis=1, keepdims=True)
        small = block[:, panel : 2 * panel] * lax.rsqrt(pivots)
        rows = jnp.dot(
            small,
            jnp.concatenate([left[:panel], right[:panel]], axis=1),
            precision=HIGHEST,
            preferred_element_type=F32,
        )
        done.append(rows[:, size:])
        if start + panel < size:
            update = lax.dot_general(
                rows[:, start + panel : size],
                rows,
                (((0,), (0,)), ((), ())),
                precision=HIGHEST,
                preferred_element_type=F32,
            )
            left = left[panel:] - update[:, :size]
            right = right[panel:] - update[:, size:]
    return jnp.concatenate(done, axis=0) * by_lane


def apply_inverse(image, inverse):
    return lax.dot_general(
        image, inverse, (((1,), (1,)), ((), ())), precision=HIGHEST, preferred_element_type=F32
    )


def next_scaled(gram, spreads, total_rows):
    rows, width = spreads[0].shape

    def kernel(gram_ref, *refs):
        out_ref = refs[-1]
        inverse = inverse_factor(gram_ref[...] / total_rows)
        for i, ref in enumerate(refs[:-1]):
            current = apply_inverse(ref[...], inverse)
            out_ref[pl.ds(i * rows, rows)] = current.astype(out_ref.dtype)

    return pl.pallas_call(
        kernel,
        name="next_scaled",
        out_shape=jax.ShapeDtypeStruct((rows * len(spreads), width), jnp.bfloat16),
        in_specs=[VMEM] * (1 + len(spreads)),
        out_specs=VMEM,
        compiler_params=pltpu.CompilerParams(vmem_limit_bytes=8 * MIB),
    )(gram, *spreads)


def last_vectors(gram, images, col_place, total_rows):
    rows, width = images[0].shape
    number = len(images)

    def kernel(place_ref, gram_ref, *refs):
        out_ref = refs[-1]
        inverse = inverse_factor(gram_ref[...] / total_rows)
        for i in range(number):
            target = pl.multiple_of(lax.rem(place_ref[0] + i, number) * rows, rows)
            out_ref[pl.ds(target, rows)] = apply_inverse(refs[i][...], inverse)

    return pl.pallas_call(
        kernel,
        name="last_vectors",
        out_shape=jax.ShapeDtypeStruct((rows * number, width), F32),
        in_specs=[SMEM] + [VMEM] * (1 + number),
        out_specs=VMEM,
        compiler_params=pltpu.CompilerParams(vmem_limit_bytes=8 * MIB),
    )(col_place.reshape(1), gram, *images)


def sum_gram(gram, beside):
    one, two, three = (shift_cols(gram, d) for d in (1, 2, 3))
    gram = (gram + two) + (one + three)
    gram = gram + shift_rows(gram, (0, 0), (0, 0), 1)
    one, two, three = (shift_rows(gram, (d, 0), (d, 0)) for d in (1, 2, 3))
    gram = (gram + two) + (one + three)
    for sources in (
        (1, 0, 3, 2, 5, 4, 7, 6),
        (2, 3, 0, 1, 6, 7, 4, 5),
        (6, 7, 4, 5, 2, 3, 0, 1),
    ):
        if sources[0] == 6:
            gram, beside = lax.optimization_barrier((gram, beside))
        pairs = [
            (row_index(y, sources[z], core), row_index(y, z, core))
            for y in range(NY)
            for z in range(NZ)
            for core in range(NC)
        ]
        gram = gram + lax.ppermute(gram, "rows", pairs)
    return gram, beside


def shards(start, degrees, tiles, tile_rows, tile_cols, tile_counts):
    rows_here, width = start.shape
    edge = tiles.shape[1]
    slots = tiles.shape[0]
    row_tiles = rows_here // edge
    col_parts = lax.axis_size("cols")
    share = row_tiles // col_parts
    quarter = share * edge
    col_place = lax.axis_index("cols").astype(jnp.int32)
    row_place = lax.axis_index("rows").astype(jnp.int32)
    total_rows = rows_here * lax.axis_size("rows")
    core = row_place % NC
    here_z = row_place // NC % NZ
    here_y = row_place // (NC * NZ)

    degrees_part = lax.dynamic_slice_in_dim(degrees, col_place * quarter, quarter)
    spread = jnp.broadcast_to(lax.rsqrt(degrees_part.astype(F32))[:, None], (quarter, width))

    out_rows = (tile_rows - row_place * row_tiles - col_place * share) % row_tiles
    source = tile_cols // row_tiles
    place = place_of(
        (source // (NC * NZ) - here_y) % NY,
        (source // NC % NZ - here_z) % NZ,
        source % NC,
        core,
        jnp.where,
    )
    plan = plan_tiles(out_rows, place, (tile_cols % share, share), tile_counts[0], early_units())

    own_tags = [[(0, 0, 0)], [(0, 0, 1)]]
    section = lax.dynamic_slice_in_dim(start, col_place * quarter, quarter)
    column = join(*column_steps(Piece((section * spread).astype(jnp.bfloat16), own_tags)))
    tiles_held = None
    for rounds in range(ITERS):

        def early(pieces, fresh):
            codes, steps = plan if fresh is None else fresh[0]
            values = [p.value for p in pieces]
            if tiles_held is None:
                return multiply_tiles(tiles, codes, steps, tile_counts, 0, values)
            return *multiply_tiles(tiles_held, codes, steps, None, 0, values), tiles_held

        beside = (plan, spread) if rounds == 0 else None
        (totals, tiles_held), late, fresh = gather_column(column, beside, early)
        if rounds == 0:
            plan, spread = fresh
        own, one, two, three = multiply_tiles(
            tiles_held, *plan, None, 1, [p.value for p in late], totals, col_parts
        )
        one, two, three = (shift_cols(v, d) for d, v in ((1, one), (2, two), (3, three)))
        image = ((own + two) + (one + three)) * spread
        gram = lax.dot_general(
            image, image, (((0,), (0,)), ((), ())), precision=HIGHEST, preferred_element_type=F32
        )
        if rounds < ITERS - 1:
            steps_y = column_steps(Piece(image * spread, own_tags))
            gram, spreads = sum_gram(gram, [p.value for p in steps_y])
            tags = join(*(Piece(None, p.tags) for p in steps_y)).tags
            column = Piece(next_scaled(gram, spreads, total_rows), tags)
        else:
            images = [image] + [shift_cols(image, -d) for d in range(1, col_parts)]
            gram, images = sum_gram(gram, images)
    return last_vectors(gram, images, col_place, total_rows)


def solution(mesh):
    in_specs = (
        P("rows", None),
        P("rows"),
        P(("rows", "cols"), None, None),
        P(("rows", "cols")),
        P(("rows", "cols")),
        P(("rows", "cols")),
    )
    out_specs = P("rows", None)
    return jax.shard_map(shards, mesh=mesh, in_specs=in_specs, out_specs=out_specs, check_vma=False)
```

```python
import jax
import jax.numpy as jnp
import numpy as np
from jax import lax
from jax.experimental import pallas as pl
from jax.experimental.pallas import tpu as pltpu
from jax.sharding import PartitionSpec as P

ITERS = 2
NY, NZ, NC = 4, 8, 2
EDGE = 128
TILE_ROWS = 8
STEP = 40
CODE = 128
LOAD_STEP = 1
PANEL = 64
GROUP = 16
HIGHEST = lax.Precision.HIGHEST
F32 = jnp.float32
MIB = 1024 * 1024

VMEM = pl.BlockSpec(memory_space=pltpu.VMEM)
SMEM = pl.BlockSpec(memory_space=pltpu.SMEM)
ANY = pl.BlockSpec(memory_space=pl.ANY)
HBM = pl.BlockSpec(memory_space=pltpu.HBM)


def row_index(y, z, core):
    return ((y % NY) * NZ + z % NZ) * NC + core


def shift_rows(value, even, odd, flip=0):
    pairs = []
    for y in range(NY):
        for z in range(NZ):
            for core in range(NC):
                dy, dz = (even, odd)[core]
                pairs.append((row_index(y, z, core), row_index(y + dy, z + dz, core ^ flip)))
    return lax.ppermute(value, "rows", pairs)


def shift_cols(value, step):
    size = lax.axis_size("cols")
    return lax.ppermute(value, "cols", [(i, (i + step) % size) for i in range(size)])


class Piece:
    def __init__(self, value, tags):
        self.value, self.tags = value, tags

    def move(self, even, odd, flip=0):
        tags = [None, None]
        for core in range(NC):
            dy, dz = (even, odd)[core]
            tags[core ^ flip] = [((a - dy) % NY, (b - dz) % NZ, k) for a, b, k in self.tags[core]]
        value = None if self.value is None else shift_rows(self.value, even, odd, flip)
        return Piece(value, tags)

    def swap(self):
        return self.move((0, 0), (0, 0), 1)


def join(*pieces):
    tags = [sum((p.tags[core] for p in pieces), []) for core in range(NC)]
    if pieces[0].value is None:
        return Piece(None, tags)
    return Piece(jnp.concatenate([p.value for p in pieces], axis=0), tags)


def column_steps(own):
    return [own] + [own.move(d, d) for d in ((1, 0), (-1, 0), (2, 0))]


def gather_column(column, beside, early):
    rings = [column, column.swap()]
    pieces = list(rings)
    held = None
    for step in range(NZ // 2 - 1):
        if step == NZ // 2 - 2:
            first, pieces = pieces, []
        rings = [ring.move((0, 1), (0, -1)) for ring in rings]
        if beside and step == LOAD_STEP:
            held = beside()
            rings[0].value, held = lax.optimization_barrier((rings[0].value, held))
        if step < NZ // 2 - 2:
            pieces += rings + [ring.swap() for ring in rings]
    last = rings[0].move((0, 1), (0, -1))
    result = early(first, held)
    if column.value is not None:
        rings[1].value, result = lax.optimization_barrier((rings[1].value, result))
        other = rings[1].swap()
        last.value, other.value = lax.optimization_barrier((last.value, other.value))
    if column.value is None:
        other = rings[1].swap()
    late = [rings[0], rings[1], rings[0].swap(), other, last, last.swap()]
    return result, late, held


def place_of(dy, dz, k, core, where):
    mine = k == core
    line = where(dy == 0, 0, where(dy == NY - 1, 1, dy + 1))
    direct = (dz < NZ // 2) == (core == 1)
    hops = where(dz < NZ // 2, dz, NZ - dz)
    piece = 4 * hops - 2 + where(direct, where(mine, 0, 1), where(mine, 3, 2))
    ends = where(mine, 0, 1)
    piece = where(dz == 0, ends, where(dz == NZ // 2, ends + 2 * NZ - 2, piece))
    return piece * NY + line


def early_units():
    column = join(*column_steps(Piece(None, [[(0, 0, 0)], [(0, 0, 1)]])))
    first, late, _ = gather_column(column, None, lambda pieces, held: pieces)
    for core in range(NC):
        units = np.array(sum((p.tags[core] for p in first + late), []))
        found = place_of(units[:, 0], units[:, 1], units[:, 2], core, np.where)
        assert (found == np.arange(NY * NZ * NC)).all()
    return sum(len(p.tags[0]) for p in first)


def load_tiles(tiles, count):
    all_steps = range(tiles.shape[0] // STEP)

    def kernel(count_ref, tiles_ref, out_ref, sem):
        steps = (count_ref[0] + STEP - 1) // STEP

        def copy(step):
            place = pl.ds(step * STEP, STEP)
            return pltpu.make_async_copy(tiles_ref.at[place], out_ref.at[place], sem.at[step])

        for step in all_steps:

            @pl.when(step < steps)
            def _():
                copy(step).start()

        for step in all_steps:

            @pl.when(step < steps)
            def _():
                copy(step).wait()

    return pl.pallas_call(
        kernel,
        name="load_tiles",
        out_shape=jax.ShapeDtypeStruct(tiles.shape, tiles.dtype),
        in_specs=[SMEM, HBM],
        out_specs=VMEM,
        scratch_shapes=[pltpu.SemaphoreType.DMA((len(all_steps),))],
        compiler_params=pltpu.CompilerParams(vmem_limit_bytes=40 * MIB),
        cost_estimate=pl.CostEstimate(flops=0, bytes_accessed=2 * tiles.size, transcendentals=0),
    )(count, tiles)


def plan_tiles(rows, places, halves, count, early):
    slots = rows.shape[0]
    share = halves[1]
    units = NY * NZ * NC
    index = jnp.arange(slots, dtype=jnp.int32)
    late = (places >= early).astype(jnp.int32)
    lot = jnp.where(index < count, late, 2)
    before = (lot[None, :] == lot[:, None]) & (index[None, :] < index[:, None])
    rank = jnp.sum(before.astype(jnp.int32), axis=1)
    steps_early = (jnp.sum((lot == 0).astype(jnp.int32)) + STEP - 1) // STEP
    steps_late = (jnp.sum((lot == 1).astype(jnp.int32)) + STEP - 1) // STEP
    room = (slots + 2 * STEP - 1) // STEP * STEP
    target = jnp.where(lot == 2, room, rank + late * steps_early * STEP)
    code = (index * TILE_ROWS + rows) * CODE + (places - late * early) * share + halves[0]
    spot = jnp.arange(room, dtype=jnp.int32)
    empty = jnp.where(spot < steps_early * STEP, early * share, (units - early) * share)
    hit = target[None, :] == spot[:, None]
    found = jnp.sum(jnp.where(hit, code[None, :] + 1, 0), axis=1)
    codes = jnp.where(found > 0, found - 1, empty)
    slot_of = codes // (CODE * TILE_ROWS)
    row_of = codes // CODE % TILE_ROWS
    line_of = codes % CODE * EDGE
    return (slot_of, row_of, line_of), jnp.stack([jnp.zeros_like(steps_early), steps_early, steps_early + steps_late])


def multiply_tiles(tiles, codes, steps, lot, parts, before=None, out_parts=None):
    slots, edge = tiles.shape[0], tiles.shape[1]
    width = parts[0].shape[1]
    sizes = [p.shape[0] // edge for p in parts]
    offsets = np.cumsum([0] + sizes)
    blocks = int(offsets[-1])
    given = [] if before is None else [before]

    def kernel(slot_ref, row_ref, line_ref, steps_ref, tiles_ref, *refs):
        given_refs, refs = refs[: len(given)], refs[len(given) :]
        part_refs, refs = refs[: len(parts)], refs[len(parts) :]
        if out_parts is None:
            totals, block_buffer, part_sems = refs
        else:
            out_refs, (totals, block_buffer, part_sems) = refs[:out_parts], refs[out_parts:]
        copies = [
            pltpu.make_async_copy(
                part_refs[i],
                block_buffer.at[pl.ds(int(offsets[i]) * edge, sizes[i] * edge)],
                part_sems.at[i],
            )
            for i in range(len(parts))
        ]
        for copy in copies:
            copy.start()
        totals[...] = given_refs[0][...] if given else jnp.zeros_like(totals)
        block_buffer[pl.ds(blocks * edge, edge)] = jnp.zeros((edge, width), block_buffer.dtype)
        for copy in copies:
            copy.wait()

        def body(step, carry):
            terms = []
            for u in range(STEP):
                line = pl.multiple_of(line_ref[step * STEP + u], edge)
                terms.append(
                    jnp.dot(
                        tiles_ref[slot_ref[step * STEP + u]],
                        block_buffer[pl.ds(line, edge)],
                        preferred_element_type=F32,
                    )
                )
            for u in range(STEP):
                totals[row_ref[step * STEP + u]] += terms[u]
            return carry

        lax.fori_loop(steps_ref[lot], steps_ref[lot + 1], body, 0)
        if out_parts is not None:
            for i, ref in enumerate(out_refs):
                for half in range(2):
                    ref[pl.ds(half * edge, edge)] = totals[2 * i + half]

    whole = (TILE_ROWS, edge, width)
    scratch = [pltpu.VMEM(((blocks + 1) * edge, width), parts[0].dtype), pltpu.SemaphoreType.DMA((len(parts),))]
    if out_parts is None:
        out_shape, out_specs = jax.ShapeDtypeStruct(whole, F32), VMEM
    else:
        out_shape = [jax.ShapeDtypeStruct((2 * edge, width), F32)] * out_parts
        out_specs = [VMEM] * out_parts
        scratch = [pltpu.VMEM(whole, F32)] + scratch
    return pl.pallas_call(
        kernel,
        name="multiply_tiles_early" if out_parts is None else "multiply_tiles_late",
        out_shape=out_shape,
        in_specs=[SMEM] * 4 + [VMEM] + [VMEM] * len(given) + [ANY] * len(parts),
        out_specs=out_specs,
        scratch_shapes=scratch,
        compiler_params=pltpu.CompilerParams(vmem_limit_bytes=12 * MIB),
        cost_estimate=pl.CostEstimate(
            flops=2 * slots * edge * edge * width,
            bytes_accessed=slots * edge * edge + blocks * edge * width * 2,
            transcendentals=0,
        ),
    )(*codes, steps, tiles, *given, *parts)


def inverse_factor(gram):
    size = gram.shape[0]
    panel = PANEL
    line_all = lax.broadcasted_iota(jnp.int32, (size, size), 0)
    lane_all = lax.broadcasted_iota(jnp.int32, (size, size), 1)
    diagonal = jnp.where(line_all == lane_all, gram, 0.0)
    by_lane = lax.rsqrt(jnp.sum(diagonal, axis=0, keepdims=True))
    by_line = lax.rsqrt(jnp.sum(diagonal, axis=1, keepdims=True))
    left = gram * by_lane * by_line
    right = jnp.where(line_all == lane_all, 1.0, 0.0).astype(F32)
    line = lax.broadcasted_iota(jnp.int32, (panel, size), 0)
    lane = lax.broadcasted_iota(jnp.int32, (panel, size), 1)
    identity = jnp.where(line == lane, 1.0, 0.0).astype(F32)
    done = []
    for start in range(0, size, panel):
        block = jnp.concatenate(
            [left[:panel, start : start + panel], identity[:, : size - panel]], axis=1
        )
        for group in range(0, panel, GROUP):
            spread = [
                jnp.broadcast_to(block[:, group + i : group + i + 1], (panel, size))
                for i in range(GROUP)
            ]
            for p in range(0, GROUP, 2):
                q = group + p
                one, two = spread[p], spread[p + 1]
                a, b, c = one[q : q + 1], two[q : q + 1], two[q + 1 : q + 2]
                scale = 1.0 / (a * c - b * b)
                factor_one = (one * c - two * b) * scale
                factor_two = (two * a - one * b) * scale
                for t in range(p + 2, GROUP):
                    spread[t] = (
                        spread[t]
                        - factor_one * spread[t][q : q + 1]
                        - factor_two * spread[t][q + 1 : q + 2]
                    )
                row_one, row_two = block[q : q + 1], block[q + 1 : q + 2]
                block = jnp.where(
                    line > q + 1,
                    block - factor_one * row_one - factor_two * row_two,
                    jnp.where(line == q + 1, row_two - (b / a) * row_one, block),
                )
        pivots = jnp.sum(jnp.where(line == lane, block, 0.0), axis=1, keepdims=True)
        small = block[:, panel : 2 * panel] * lax.rsqrt(pivots)
        rows = jnp.dot(
            small,
            jnp.concatenate([left[:panel], right[:panel]], axis=1),
            precision=HIGHEST,
            preferred_element_type=F32,
        )
        done.append(rows[:, size:])
        if start + panel < size:
            update = lax.dot_general(
                rows[:, start + panel : size],
                rows,
                (((0,), (0,)), ((), ())),
                precision=HIGHEST,
                preferred_element_type=F32,
            )
            left = left[panel:] - update[:, :size]
            right = right[panel:] - update[:, size:]
    return jnp.concatenate(done, axis=0) * by_lane


def apply_inverse(image, inverse):
    return lax.dot_general(
        image, inverse, (((1,), (1,)), ((), ())), precision=HIGHEST, preferred_element_type=F32
    )


def next_scaled(gram, spreads, total_rows):
    rows, width = spreads[0].shape

    def kernel(gram_ref, *refs):
        out_ref = refs[-1]
        inverse = inverse_factor(gram_ref[...] / total_rows)
        for i, ref in enumerate(refs[:-1]):
            current = apply_inverse(ref[...], inverse)
            out_ref[pl.ds(i * rows, rows)] = current.astype(out_ref.dtype)

    return pl.pallas_call(
        kernel,
        name="next_scaled",
        out_shape=jax.ShapeDtypeStruct((rows * len(spreads), width), jnp.bfloat16),
        in_specs=[VMEM] * (1 + len(spreads)),
        out_specs=VMEM,
        compiler_params=pltpu.CompilerParams(vmem_limit_bytes=8 * MIB),
    )(gram, *spreads)


def last_vectors(gram, images, col_place, total_rows):
    rows, width = images[0].shape
    number = len(images)

    def kernel(place_ref, gram_ref, *refs):
        out_ref = refs[-1]
        inverse = inverse_factor(gram_ref[...] / total_rows)
        for i in range(number):
            target = pl.multiple_of(lax.rem(place_ref[0] + i, number) * rows, rows)
            out_ref[pl.ds(target, rows)] = apply_inverse(refs[i][...], inverse)

    return pl.pallas_call(
        kernel,
        name="last_vectors",
        out_shape=jax.ShapeDtypeStruct((rows * number, width), F32),
        in_specs=[SMEM] + [VMEM] * (1 + number),
        out_specs=VMEM,
        compiler_params=pltpu.CompilerParams(vmem_limit_bytes=8 * MIB),
    )(col_place.reshape(1), gram, *images)


def sum_gram(gram, beside):
    one, two, three = (shift_cols(gram, d) for d in (1, 2, 3))
    gram = (gram + two) + (one + three)
    gram = gram + shift_rows(gram, (0, 0), (0, 0), 1)
    one, two, three = (shift_rows(gram, (d, 0), (d, 0)) for d in (1, 2, 3))
    gram = (gram + two) + (one + three)
    for sources in (
        (1, 0, 3, 2, 5, 4, 7, 6),
        (2, 3, 0, 1, 6, 7, 4, 5),
        (6, 7, 4, 5, 2, 3, 0, 1),
    ):
        if sources[0] == 6:
            gram, beside = lax.optimization_barrier((gram, beside))
        pairs = [
            (row_index(y, sources[z], core), row_index(y, z, core))
            for y in range(NY)
            for z in range(NZ)
            for core in range(NC)
        ]
        gram = gram + lax.ppermute(gram, "rows", pairs)
    return gram, beside


def shards(start, degrees, tiles, tile_rows, tile_cols, tile_counts):
    rows_here, width = start.shape
    edge = tiles.shape[1]
    slots = tiles.shape[0]
    row_tiles = rows_here // edge
    col_parts = lax.axis_size("cols")
    share = row_tiles // col_parts
    quarter = share * edge
    col_place = lax.axis_index("cols").astype(jnp.int32)
    row_place = lax.axis_index("rows").astype(jnp.int32)
    total_rows = rows_here * lax.axis_size("rows")
    core = row_place % NC
    here_z = row_place // NC % NZ
    here_y = row_place // (NC * NZ)

    degrees_part = lax.dynamic_slice_in_dim(degrees, col_place * quarter, quarter)
    spread = jnp.broadcast_to(lax.rsqrt(degrees_part.astype(F32))[:, None], (quarter, width))

    out_rows = (tile_rows - row_place * row_tiles - col_place * share) % row_tiles
    source = tile_cols // row_tiles
    place = place_of(
        (source // (NC * NZ) - here_y) % NY,
        (source // NC % NZ - here_z) % NZ,
        source % NC,
        core,
        jnp.where,
    )
    plan = plan_tiles(out_rows, place, (tile_cols % share, share), tile_counts[0], early_units())

    def load():
        return load_tiles(tiles, tile_counts), plan, spread

    own_tags = [[(0, 0, 0)], [(0, 0, 1)]]
    section = lax.dynamic_slice_in_dim(start, col_place * quarter, quarter)
    column = join(*column_steps(Piece((section * spread).astype(jnp.bfloat16), own_tags)))
    held = None
    for rounds in range(ITERS):
        known = held

        def early(pieces, fresh):
            tiles_held, (codes, steps), _ = known or fresh
            return multiply_tiles(tiles_held, codes, steps, 0, [p.value for p in pieces])

        beside = load if rounds == 0 else None
        totals, late, fresh = gather_column(column, beside, early)
        held = known or fresh
        tiles_held, (codes, steps), spread = held
        own, one, two, three = multiply_tiles(
            tiles_held, codes, steps, 1, [p.value for p in late], totals, col_parts
        )
        one, two, three = (shift_cols(v, d) for d, v in ((1, one), (2, two), (3, three)))
        image = ((own + two) + (one + three)) * spread
        gram = lax.dot_general(
            image, image, (((0,), (0,)), ((), ())), precision=HIGHEST, preferred_element_type=F32
        )
        if rounds < ITERS - 1:
            steps_y = column_steps(Piece(image * spread, own_tags))
            gram, spreads = sum_gram(gram, [p.value for p in steps_y])
            tags = join(*(Piece(None, p.tags) for p in steps_y)).tags
            column = Piece(next_scaled(gram, spreads, total_rows), tags)
        else:
            images = [image] + [shift_cols(image, -d) for d in range(1, col_parts)]
            gram, images = sum_gram(gram, images)
    return last_vectors(gram, images, col_place, total_rows)


def solution(mesh):
    in_specs = (
        P("rows", None),
        P("rows"),
        P(("rows", "cols"), None, None),
        P(("rows", "cols")),
        P(("rows", "cols")),
        P(("rows", "cols")),
    )
    out_specs = P("rows", None)
    return jax.shard_map(shards, mesh=mesh, in_specs=in_specs, out_specs=out_specs, check_vma=False)
```
